128 devices in a mesh: section: 2 (over core), exp: 16 (over x, z), tp: 4 (over y).
Axes of the slice: x: 4, y: 4, z: 4, core: 2. Of those that a mesh axis runs over, the one named last changes fastest.
Arguments:
- activations: bfloat16 [4, 2048, 1024], P(None, ('exp', 'tp')), may hold values from -6 to 6
- cotangent: bfloat16 [4, 2048, 1024], P(None, ('exp', 'tp')), may hold values from -6 to 6
- segments: int32 [4, 2048], P(None, 'exp'), may hold values from 0 to 127, as said below
- routes: int32 [4, 2048, 8], P(None, ('exp', 'tp')), may hold values from 0 to 31, all different within a row; in each aligned block of 32 rows (0 to 31, 32 to 63, ..., all dimensions but the last counted through in order) at most 16 rows name the same one
- attention_gain: bfloat16 [2, 1024], P('section'), may hold values from 0.5 to 1.5
- query_weight: bfloat16 [2, 1024, 1024], P('section', None, 'tp'), may hold values from -0.1875 to 0.1875
- key_weight: bfloat16 [2, 1024, 512], P('section', None, 'tp'), may hold values from -0.1875 to 0.1875
- value_weight: bfloat16 [2, 1024, 512], P('section', None, 'tp'), may hold values from -0.1875 to 0.1875
- output_weight: bfloat16 [2, 1024, 1024], P('section', 'tp'), may hold values from -0.75 to 0.75
- mixture_gain: bfloat16 [2, 1024], P('section'), may hold values from 0.5 to 1.5
- router_weight: bfloat16 [2, 1024, 32], P('section'), may hold values from -0.09375 to 0.09375
- expert_gate_up: bfloat16 [2, 32, 1024, 1024], P('section', 'exp'), may hold values from -0.1875 to 0.1875
- expert_down: bfloat16 [2, 32, 512, 1024], P('section', 'exp'), may hold values from -0.75 to 0.75
Outputs:
- section_output: bfloat16 [2, 4, 2048, 1024], P('section', None, ('exp', 'tp'))
- section_input_grad: float32 [2, 4, 2048, 1024], P('section', None, ('exp', 'tp'))
- grad_attention_gain: float32 [2, 1024], P('section')
- grad_query: float32 [2, 1024, 1024], P('section', 'exp', 'tp')
- grad_key: float32 [2, 1024, 512], P('section', 'exp', 'tp')
- grad_value: float32 [2, 1024, 512], P('section', 'exp', 'tp')
- grad_output: float32 [2, 1024, 1024], P('section', 'tp', 'exp')
- grad_mixture_gain: float32 [2, 1024], P('section')
- grad_router: float32 [2, 1024, 32], P('section')
- grad_gate_up: float32 [2, 32, 1024, 1024], P('section', 'exp', None, 'tp')
- grad_down: float32 [2, 32, 512, 1024], P('section', 'exp', None, 'tp')
The draws below stay inside these ranges and needn't reach their ends.
Inputs may be any that keep to these rules, and one draw needn't show every extreme that they name: `segments`: segment numbers never fall within each group of 128 rows; in each group one sequence starts within the first 32 rows and ends within the last 32; in each micro-batch one group is a single sequence of 128 rows. `routes`: within each aligned block of 32 rows (the rows of one device in one micro-batch) no expert is named by more than 16 rows.
All inputs are finite; a program needn't handle non-finite values.
Results may differ from the reference program's by a relative error of at most 0.039.
Values may be sent and summed in bfloat16 or wider, within the bound.
A program may use at most 192 MiB of HBM per device.

```python
import math
import jax
import jax.numpy as jnp
import numpy as np
from jax import lax

D = 1024
H = 16
KV = 8
HD = 64
E = 32
F = 512
K = 8
ROWS_DEV = 32
MB = 4
CAP = 16
ROWS = 128
TOKENS = 2048
N_EXP = 16
N_TP = 4


def draw_segments(key, part):
    key = jax.random.fold_in(key, 11)
    keys_all = jax.random.split(key, 5)
    block_count = MB * N_EXP
    spacing = jax.random.randint(keys_all[0], (block_count, 1), 3, 40)
    cuts = jax.random.randint(keys_all[1], (block_count, ROWS), 0, 1 << 20) % spacing == 0
    opening = jax.random.randint(keys_all[2], (block_count, 1), 0, ROWS_DEV)
    closing = jax.random.randint(keys_all[3], (block_count, 1), ROWS - ROWS_DEV + 1, ROWS + 1)
    picked_block = jax.random.randint(keys_all[4], (MB, 1), 0, N_EXP)
    whole = (jnp.arange(N_EXP, dtype=jnp.int32)[None, :] == picked_block).reshape(block_count, 1)
    opening = jnp.where(whole, 0, opening)
    closing = jnp.where(whole, ROWS, closing)
    places = jnp.arange(ROWS, dtype=jnp.int32)[None, :]
    inside = (places > opening) & (places < closing)
    cuts = cuts & jnp.logical_not(inside) | (places == opening) | (places == closing)
    cuts = cuts & (places > 0)
    numbers = jnp.cumsum(cuts.astype(jnp.int32), axis=1)
    numbers = jnp.where(whole, ROWS - 1, numbers)
    return numbers.reshape(MB, TOKENS).astype(jnp.int32)


def shard_levels(rng, extent, pieces, low, high):
    loudness = 1.0
    for axis_at, shards_of in pieces:
        steps = jax.random.uniform(jax.random.fold_in(jax.random.fold_in(rng, 6), axis_at), (shards_of,), jnp.float32, low / len(pieces), high / len(pieces))
        loudness = loudness * jnp.repeat(jnp.exp(steps), extent[axis_at] // shards_of).reshape((-1,) + (1,) * (len(extent) - 1 - axis_at))
    return loudness


def assign_block(rng, own, number, rows, number_of, top, limit, lean):
    order = jax.random.permutation(rng, number_of)
    crowded, ordinary = portions_of(number_of, rows * top, limit, lean, True), portions_of(number_of, rows * top, limit, lean, False)
    places = jnp.arange(number_of)

    def named(tallies, offset_by):
        used = int((tallies > 0).sum())
        fixed = max(1, used // 4)
        passed = fixed + (places - fixed + offset_by * (used - fixed)) % max(1, number_of - fixed)
        return jnp.zeros((number_of,), jnp.int32).at[order[jnp.where(places < fixed, places, passed)]].set(jnp.asarray(tallies, jnp.int32))

    tallies = jnp.where(number % 4 == 0, named(crowded, number // 4), named(ordinary, number - number // 4 - 1))
    mixed = jax.random.permutation(jax.random.fold_in(own, 3), number_of)
    source_of, receiver = mixed[0:number_of // 2 * 2:2], mixed[1:number_of // 2 * 2:2]
    room = jnp.minimum(tallies[source_of] - 1, limit - tallies[receiver]) // 2
    room = jnp.where((source_of == order[0]) | (receiver == order[0]) | (tallies[receiver] == 0), 0, jnp.maximum(room, 0))
    passed = jax.random.randint(jax.random.fold_in(own, 4), (number_of // 2,), 0, 1 << 20) % (room + 1)
    tallies = tallies.at[source_of].add(-passed).at[receiver].add(passed)
    members = jnp.searchsorted(jnp.cumsum(tallies), jnp.arange(rows * top), side="right").astype(jnp.int32)
    grid = members.reshape(top, rows).T
    grid = grid[jax.random.permutation(jax.random.fold_in(own, 1), rows)]
    offset_by = jax.random.randint(jax.random.fold_in(own, 2), (rows, 1), 0, top)
    return jnp.take_along_axis(grid, (jnp.arange(top)[None, :] + offset_by) % top, axis=1)


def portions_of(amount, total, most, slope, full):
    loads = [(1 << 20) // math.isqrt(rank ** slope) + 1 for rank in range(1, amount + 1)]
    largest = most if full else min(most, max(-(-total // amount), total * loads[0] // sum(loads)))
    least = 1 if total - largest >= amount - 1 else 0
    counts, rest = [largest] + [least] * (amount - 1), total - largest - least * (amount - 1)
    while rest > 0:
        free = [i for i in range(1, amount) if counts[i] < largest] or [i for i in range(1, amount) if counts[i] < most]
        mass, remaining = sum([loads[i] for i in free]), rest
        for i in free:
            addition = min(most - counts[i], max(1, remaining * loads[i] // mass), rest)
            counts[i] = counts[i] + addition
            rest = rest - addition
    return np.array(counts)


def noise(own_key, shape, spread, bound, shards=(), kind=jnp.bfloat16):
    level = shard_levels(own_key, shape, shards, -0.22, 0.18) if shards else 1.0
    array = jax.random.normal(own_key, shape, jnp.float32) * spread * level
    return jnp.minimum(jnp.maximum(array, -bound), bound).astype(kind)


def setup_inputs(seed: int = 0) -> dict:
    key_of = jax.random.split(jax.random.key(seed), 14)
    activations = noise(key_of[0], (MB, TOKENS, D), 1.0, 6.0, ((1, 64),))
    cotangent = noise(key_of[1], (MB, TOKENS, D), 1.0, 6.0, ((1, 64),))
    segments = draw_segments(jax.random.fold_in(key_of[13], 71), 0)
    routes_keys = jax.random.split(jax.random.fold_in(key_of[3], 1), MB * TOKENS // ROWS_DEV)
    routes_turns = jax.random.permutation(jax.random.fold_in(key_of[3], 3), MB * TOKENS // ROWS_DEV)
    routes = jax.vmap(lambda own, number: assign_block(jax.random.fold_in(key_of[3], 2), own, number, ROWS_DEV, E, K, CAP, 1))(routes_keys, routes_turns).reshape((MB, TOKENS, K))
    attention_gain = jnp.clip(1.0 + 0.1 * jax.random.normal(key_of[4], (2, D), jnp.float32), 0.5, 1.5).astype(jnp.bfloat16)
    query_weight = noise(key_of[5], (2, D, H * HD), D ** -0.5, 0.1875, ((0, 2), (2, 4)))
    key_weight = noise(key_of[6], (2, D, KV * HD), D ** -0.5, 0.1875, ((0, 2), (2, 4)))
    value_weight = noise(key_of[7], (2, D, KV * HD), D ** -0.5, 0.1875, ((0, 2), (2, 4)))
    output_weight = noise(key_of[8], (2, H * HD, D), (H * HD // 16) ** -0.5, 0.75, ((0, 2), (1, 4)))
    mixture_gain = jnp.clip(1.0 + 0.1 * jax.random.normal(key_of[9], (2, D), jnp.float32), 0.5, 1.5).astype(jnp.bfloat16)
    router_weight = noise(key_of[10], (2, D, E), (4 * D) ** -0.5, 0.09375, ((0, 2),))
    expert_gate_up = noise(key_of[11], (2, E, D, 2 * F), D ** -0.5, 0.1875, ((0, 2), (1, 16)))
    expert_down = noise(key_of[12], (2, E, F, D), (F // 8) ** -0.5, 0.75, ((0, 2), (1, 16)))
    return dict(activations=activations, cotangent=cotangent, segments=segments, routes=routes, attention_gain=attention_gain, query_weight=query_weight, key_weight=key_weight, value_weight=value_weight, output_weight=output_weight, mixture_gain=mixture_gain, router_weight=router_weight, expert_gate_up=expert_gate_up, expert_down=expert_down)


EPSILON = 1e-06
ROPE_BASE = 10000.0
SCORE_SCALE = 0.125
MASKED = -1e+30
HIGHEST = lax.Precision.HIGHEST

@jax.custom_vjp
def low(v):
    return lax.optimization_barrier(v.astype(jnp.bfloat16)).astype(jnp.float32)

@jax.custom_vjp
def low_back(v):
    return v

def low_keep(v):
    return (low(v), None)

def low_pass(kept, grad):
    return (grad,)

def back_keep(v):
    return (v, None)

def back_low(kept, grad):
    return (low(grad),)
low.defvjp(low_keep, low_pass)
low_back.defvjp(back_keep, back_low)

def rotate_half(values):
    middle = values.shape[-1] // 2
    return jnp.concatenate([-values[..., middle:], values[..., :middle]], axis=-1)

def rotary(values, cosine_part, sine_part):
    return values * cosine_part + rotate_half(values) * sine_part

def rope_tables(seg_rows, head_size):
    length = seg_rows.shape[0]
    before = lax.optimization_barrier(jnp.sum((seg_rows[None, :] < seg_rows[:, None]).astype(jnp.int32), axis=1))
    places = (jnp.arange(length, dtype=jnp.int32) - before).astype(jnp.float32)
    powers = jnp.arange(0, head_size, 2, dtype=jnp.int32).astype(jnp.float32) / head_size
    angles = places[:, None] * (ROPE_BASE ** (-powers))[None, :]
    angles = jnp.concatenate([angles, angles], axis=1)
    indices = jnp.arange(length, dtype=jnp.int32)
    allowed = (seg_rows[:, None] == seg_rows[None, :]) & (indices[None, :] <= indices[:, None])
    return (jnp.cos(angles), jnp.sin(angles), allowed)

def routing_plan(route_rows, experts, capacity):
    row_count, pick_count = route_rows.shape
    labels = jnp.arange(experts, dtype=jnp.int32)
    onehot = (route_rows[:, :, None] == labels[None, None, :]).astype(jnp.int32)
    flattened = onehot.reshape(row_count * pick_count, experts)
    earlier = jnp.cumsum(flattened, axis=0) - flattened
    within = lax.optimization_barrier(jnp.sum(earlier * flattened, axis=1)).reshape(row_count, pick_count)
    target = (route_rows * capacity + within).astype(jnp.int32)
    slot_ids = jnp.arange(experts * capacity, dtype=jnp.int32)
    matched = target.reshape(-1)[:, None] == slot_ids[None, :]
    filled = jnp.any(matched, axis=0)
    pair_ids = jnp.arange(row_count * pick_count, dtype=jnp.int32)
    source = lax.optimization_barrier(jnp.sum(jnp.where(matched, pair_ids[:, None], 0), axis=0)).astype(jnp.int32)
    return (onehot, target, filled, source)

def rms_scale(values, gain):
    return values * lax.rsqrt(lax.optimization_barrier(jnp.mean(values * values, axis=-1, keepdims=True)) + EPSILON) * gain

def matmul(left_side, right_side):
    return jnp.dot(left_side, right_side, precision=HIGHEST)

def layer(layer_in, seg_mb, route_mb, attention_gain, query_weight, key_weight, value_weight, output_weight, mixture_gain, router_weight, expert_gate_up, expert_down):
    tokens = layer_in.shape[0]
    model_width = layer_in.shape[1]
    group_size = H // KV
    normed = low(rms_scale(layer_in, attention_gain))
    cosine_table, sine_table, allowed = jax.vmap(lambda block_ids: rope_tables(block_ids, HD))(seg_mb.reshape(N_EXP, ROWS))
    queries = low_back(matmul(normed, query_weight)).reshape(N_EXP, ROWS, KV, group_size, HD)
    queries = low(rotary(queries, cosine_table[:, :, None, None, :], sine_table[:, :, None, None, :]))
    key_heads = low_back(matmul(normed, key_weight)).reshape(N_EXP, ROWS, KV, HD)
    key_heads = low(rotary(key_heads, cosine_table[:, :, None, :], sine_table[:, :, None, :]))
    value_heads = low(low_back(matmul(normed, value_weight))).reshape(N_EXP, ROWS, KV, HD)
    scores = low_back(SCORE_SCALE * jnp.einsum('bqgjd,bkgd->bgjqk', queries, key_heads, precision=HIGHEST))
    scores = jnp.where(allowed[:, None, None, :, :], scores, MASKED)
    attention = jax.nn.softmax(scores, axis=-1)
    attended = jnp.einsum('bgjqk,bkgd->bqgjd', low(attention), value_heads, precision=HIGHEST).reshape(tokens, H * HD)
    attended = low(low_back(attended))
    after_attn = layer_in + low_back(matmul(attended, output_weight))
    normed_two = low(rms_scale(after_attn, mixture_gain))
    logits = matmul(normed_two, router_weight)
    block_count = N_EXP * N_TP
    onehot, target, filled, source = jax.vmap(lambda block_routes: routing_plan(block_routes, E, CAP))(route_mb.reshape(block_count, ROWS_DEV, K))
    chosen = lax.optimization_barrier(jnp.sum(onehot.reshape(tokens, K, E).astype(jnp.float32) * logits[:, None, :], axis=2))
    gate_weights = jax.nn.softmax(chosen, axis=1)
    by_block = normed_two.reshape(block_count, ROWS_DEV, model_width)
    gathered = jnp.take_along_axis(by_block, (source // K)[:, :, None], axis=1)
    outgoing = jnp.where(filled[:, :, None], gathered, 0.0)
    incoming = outgoing.reshape(block_count, E, CAP, model_width).transpose(1, 0, 2, 3).reshape(E, block_count * CAP, model_width)
    incoming = low_back(incoming)
    gate_up = low_back(jnp.einsum('esd,edf->esf', incoming, expert_gate_up, precision=HIGHEST))
    hidden = low(jax.nn.silu(gate_up[..., :F]) * gate_up[..., F:])
    produced = low(low_back(jnp.einsum('esf,efd->esd', hidden, expert_down, precision=HIGHEST)))
    returned = produced.reshape(E, block_count, CAP, model_width).transpose(1, 0, 2, 3).reshape(block_count, E * CAP, model_width)
    picked = jnp.take_along_axis(returned, target.reshape(block_count, ROWS_DEV * K)[:, :, None], axis=1).reshape(tokens, K, model_width)
    return after_attn + lax.optimization_barrier(jnp.sum(gate_weights[:, :, None] * picked, axis=1))

def reference(activations, cotangent, segments, routes, attention_gain, query_weight, key_weight, value_weight, output_weight, mixture_gain, router_weight, expert_gate_up, expert_down):
    params = tuple((member.astype(jnp.float32) for member in (attention_gain, query_weight, key_weight, value_weight, output_weight, mixture_gain, router_weight, expert_gate_up, expert_down)))

    def step(totals, inputs_mb):
        rows_mb, grad_mb, seg_mb, route_mb = inputs_mb

        def run(layer_in, probe_zero, weights):
            first_out = layer(layer_in, seg_mb, route_mb, *[member[0] for member in weights])
            sent_out = low(first_out)
            second_out = layer(low_back(sent_out) + probe_zero, seg_mb, route_mb, *[member[1] for member in weights])
            return (second_out, sent_out)
        start_rows = rows_mb.astype(jnp.float32)
        second_out, back_fn, sent_out = jax.vjp(run, start_rows, jnp.zeros_like(start_rows), params, has_aux=True)
        grad_start, grad_probe, grad_params = back_fn(grad_mb.astype(jnp.float32))
        return (jax.tree.map(jnp.add, totals, grad_params), (sent_out, second_out, grad_start, grad_probe))
    zeros_tree = jax.tree.map(jnp.zeros_like, params)
    totals, (sent_all, second_all, grad_first, grad_second) = lax.scan(step, zeros_tree, (activations, cotangent, segments, routes))
    section_output = jnp.stack([sent_all, second_all]).astype(jnp.bfloat16)
    section_input_grad = jnp.stack([grad_first, grad_second])
    return (section_output, section_input_grad, totals[0], totals[1], totals[2], totals[3], totals[4], totals[5], totals[6], totals[7], totals[8])
```

```python
import functools

import jax
import jax.numpy as jnp
from jax import lax
from jax.experimental import pallas as pl
from jax.experimental.pallas import tpu as pltpu
from jax.sharding import PartitionSpec as P

D = 1024
HD = 64
E = 32
F = 512
LANES = 128
EPSILON = 1e-06
ROPE_BASE = 10000.0
SCORE_SCALE = 0.125
MASKED = -1e30
MESH = pl.DeviceIdType.MESH
VMEM_LIMIT = 56 * 1024 * 1024
BF16 = jnp.bfloat16
F32 = jnp.float32


def dot(a, b):
    return jnp.dot(a, b, preferred_element_type=F32)


def dot_nt(a, b):
    return lax.dot_general(a, b, (((1,), (1,)), ((), ())), preferred_element_type=F32)


def dot_tn(a, b):
    return lax.dot_general(a, b, (((0,), (0,)), ((), ())), preferred_element_type=F32)


def in_vmem():
    return pl.BlockSpec(memory_space=pltpu.VMEM)


def in_any():
    return pl.BlockSpec(memory_space=pl.ANY)


def greet(peers):
    barrier = pltpu.get_barrier_semaphore()
    for peer in peers:
        pl.semaphore_signal(barrier, inc=1, device_id=peer, device_id_type=MESH)
    pl.semaphore_wait(barrier, len(peers))


def remote(src, dst, send_sem, recv_sem, peer):
    return pltpu.make_async_remote_copy(
        src_ref=src,
        dst_ref=dst,
        send_sem=send_sem,
        recv_sem=recv_sem,
        device_id=peer,
        device_id_type=MESH,
    )


def comm_params(number):
    return pltpu.CompilerParams(
        collective_id=number, has_side_effects=True, vmem_limit_bytes=VMEM_LIMIT
    )


def pair_kernel(count, *refs):
    ins, outs = refs[:count], refs[count : 2 * count]
    send_sem, recv_sem, own_sem = refs[2 * count :]
    me = lax.axis_index("section")
    peer = {"section": 1 - me}
    greet([peer])
    sends, owns = [], []
    for at in range(count):
        sends.append(
            remote(ins[at].at[0], outs[at].at[me], send_sem.at[at], recv_sem.at[at], peer)
        )
        owns.append(pltpu.make_async_copy(ins[at].at[0], outs[at].at[me], own_sem.at[at]))
        sends[-1].start()
        owns[-1].start()
    for at in range(count):
        owns[at].wait()
        sends[at].wait()


def pair_gather(arrays, number):
    count = len(arrays)
    return pl.pallas_call(
        functools.partial(pair_kernel, count),
        out_shape=[jax.ShapeDtypeStruct((2,) + a.shape[1:], a.dtype) for a in arrays],
        in_specs=[in_any()] * count,
        out_specs=[in_any()] * count,
        scratch_shapes=[pltpu.SemaphoreType.DMA((count,))] * 3,
        compiler_params=comm_params(number),
        name="pair_gather%d" % number,
    )(*arrays)


def tp_gather_kernel(x_ref, out_ref, send_sem, recv_sem):
    me = lax.axis_index("tp")
    peers = [{"tp": lax.rem(me + j, 4)} for j in (1, 2, 3)]
    greet(peers)
    mine = pl.ds(pl.multiple_of(me * 32, 32), 32)
    copies = [
        remote(x_ref, out_ref.at[:, mine], send_sem.at[j], recv_sem.at[j], peers[j])
        for j in range(3)
    ]
    for copy in copies:
        copy.start()
    out_ref[:, mine] = x_ref[...]
    for copy in copies:
        copy.wait()


def tp_gather(x):
    return pl.pallas_call(
        tp_gather_kernel,
        out_shape=jax.ShapeDtypeStruct((2, 128, D), BF16),
        in_specs=[in_vmem()],
        out_specs=in_vmem(),
        scratch_shapes=[pltpu.SemaphoreType.DMA((3,))] * 2,
        compiler_params=comm_params(2),
        name="tp_gather",
    )(x)


def tp_scatter_kernel(x_ref, out_ref, held, send_sem, recv_sem):
    me = lax.axis_index("tp")
    places = [lax.rem(me + j, 4) for j in (1, 2, 3)]
    greet([{"tp": place} for place in places])
    copies = []
    for j in range(3):
        theirs = pl.ds(pl.multiple_of(places[j] * 32, 32), 32)
        copies.append(
            remote(
                x_ref.at[:, theirs], held.at[j], send_sem.at[j], recv_sem.at[j], {"tp": places[j]}
            )
        )
        copies[-1].start()
    total = x_ref[:, pl.ds(pl.multiple_of(me * 32, 32), 32)].astype(F32)
    for j in range(3):
        copies[j].wait_recv()
        total = total + held[j].astype(F32)
    out_ref[...] = total
    for copy in copies:
        copy.wait_send()


def tp_scatter(x):
    return pl.pallas_call(
        tp_scatter_kernel,
        out_shape=jax.ShapeDtypeStruct((2, 32, D), F32),
        in_specs=[in_vmem()],
        out_specs=in_vmem(),
        scratch_shapes=[pltpu.VMEM((3, 2, 32, D), BF16)] + [pltpu.SemaphoreType.DMA((3,))] * 2,
        compiler_params=comm_params(3),
        name="tp_scatter",
    )(x)


def exp_places():
    me = lax.axis_index("exp")
    at_x, at_z = me // 4, lax.rem(me, 4)
    return me, at_x, at_z


def exp_gather_kernel(x_ref, out_ref, send_one, recv_one, send_two, recv_two):
    me, at_x, at_z = exp_places()

    def place(by_x, by_z):
        return lax.rem(at_x + by_x, 4) * 4 + lax.rem(at_z + by_z, 4)

    peers = [[{"exp": place(j, 0)} for j in (1, 2, 3)], [{"exp": place(0, j)} for j in (1, 2, 3)]]
    greet(peers[0] + peers[1])
    rows = [pl.ds(0, 32), pl.ds(32, 32)]
    first = [[], []]
    second = [[], []]
    for j in range(3):
        for half in range(2):
            copy = remote(
                x_ref.at[rows[half]],
                out_ref.at[me, rows[half]],
                send_one.at[half, j],
                recv_one.at[half, j],
                peers[half][j],
            )
            copy.start()
            first[half].append(copy)
    for j in range(3):
        for half in range(2):
            copy = remote(
                x_ref.at[rows[half]],
                out_ref.at[me, rows[half]],
                send_two.at[half, 0, j],
                recv_two.at[half, 0, j],
                peers[1 - half][j],
            )
            copy.start()
            second[half].append(copy)
    out_ref[me] = x_ref[...]
    for back in range(1, 4):
        for half in range(2):
            first[half][back - 1].wait_recv()
            origin = place(4 - back, 0) if half == 0 else place(0, 4 - back)
            for j in range(3):
                copy = remote(
                    out_ref.at[origin, rows[half]],
                    out_ref.at[origin, rows[half]],
                    send_two.at[half, back, j],
                    recv_two.at[half, back, j],
                    peers[1 - half][j],
                )
                copy.start()
                second[half].append(copy)
    for half in range(2):
        for copy in first[half]:
            copy.wait_send()
        for copy in second[half]:
            copy.wait()


def exp_gather(x):
    return pl.pallas_call(
        exp_gather_kernel,
        out_shape=jax.ShapeDtypeStruct((16, 64, D), BF16),
        in_specs=[in_vmem()],
        out_specs=in_vmem(),
        scratch_shapes=[
            pltpu.SemaphoreType.DMA((2, 3)),
            pltpu.SemaphoreType.DMA((2, 3)),
            pltpu.SemaphoreType.DMA((2, 4, 3)),
            pltpu.SemaphoreType.DMA((2, 4, 3)),
        ],
        compiler_params=comm_params(4),
        name="exp_gather",
    )(x)


def exp_scatter_kernel(
    x_ref, out_ref, held_one, ready, held_two, send_one, recv_one, send_two, recv_two
):
    me, at_x, at_z = exp_places()
    to_x = [lax.rem(at_x + j, 4) for j in (1, 2, 3)]
    to_z = [lax.rem(at_z + j, 4) for j in (1, 2, 3)]
    peers = [[{"exp": x * 4 + at_z} for x in to_x], [{"exp": at_x * 4 + z} for z in to_z]]
    greet(peers[0] + peers[1])
    rows = [pl.ds(0, 32), pl.ds(32, 32)]
    first = [[], []]
    second = [[], []]
    for j in range(3):
        for half in range(2):
            src = (
                x_ref.at[to_x[j], :, rows[0]] if half == 0 else x_ref.at[:, to_z[j], rows[1]]
            )
            copy = remote(
                src, held_one.at[half, j], send_one.at[half, j], recv_one.at[half, j], peers[half][j]
            )
            copy.start()
            first[half].append(copy)
    for half in range(2):
        for j in range(3):
            first[half][j].wait_recv()
        for j in range(3):
            to = to_z[j] if half == 0 else to_x[j]
            own = x_ref[at_x, to, rows[0]] if half == 0 else x_ref[to, at_z, rows[1]]
            total = own.astype(F32)
            for k in range(3):
                total = total + held_one[half, k, to].astype(F32)
            ready[half, j] = total.astype(BF16)
            copy = remote(
                ready.at[half, j],
                held_two.at[half, j],
                send_two.at[half, j],
                recv_two.at[half, j],
                peers[1 - half][j],
            )
            copy.start()
            second[half].append(copy)
    for half in range(2):
        total = x_ref[at_x, at_z, rows[half]].astype(F32)
        mine = at_z if half == 0 else at_x
        for k in range(3):
            total = total + held_one[half, k, mine].astype(F32)
        for k in range(3):
            second[half][k].wait_recv()
            total = total + held_two[half, k].astype(F32)
        out_ref[rows[half]] = total
    for half in range(2):
        for copy in first[half] + second[half]:
            copy.wait_send()


def exp_scatter(x, number):
    width = x.shape[-1]
    return pl.pallas_call(
        exp_scatter_kernel,
        out_shape=jax.ShapeDtypeStruct((64, width), F32),
        in_specs=[in_vmem()],
        out_specs=in_vmem(),
        scratch_shapes=[
            pltpu.VMEM((2, 3, 4, 32, width), BF16),
            pltpu.VMEM((2, 3, 32, width), BF16),
            pltpu.VMEM((2, 3, 32, width), BF16),
        ]
        + [pltpu.SemaphoreType.DMA((2, 3))] * 4,
        compiler_params=comm_params(number),
        name="exp_scatter%d" % number,
    )(x.reshape(4, 4, 64, width))


def half_swapped(values):
    width = values.shape[1]
    lane = lax.broadcasted_iota(jnp.int32, values.shape, 1)
    ahead = pltpu.roll(values, width - 32, 1)
    behind = pltpu.roll(values, 32, 1)
    return jnp.where(lax.rem(lane, 64) < 32, ahead, behind)


def three(table):
    return jnp.concatenate([table, table, table], axis=1)


def head(values, batch, first):
    return values[batch * 128 : batch * 128 + 128, first : first + HD]


def attention_forward_kernel(
    rows_ref, wqkv_ref, wo_ref, cos_ref, sin_ref, mask_ref, part_ref, qkv_ref, att_ref
):
    joined = dot(rows_ref[...], wqkv_ref[0])
    turned = joined[:, :384]
    turned = turned * three(cos_ref[...]) + half_swapped(turned) * three(sin_ref[...])
    qkv = jnp.concatenate([turned, joined[:, 384:]], axis=1).astype(BF16)
    qkv_ref[...] = qkv
    for batch in range(2):
        allowed = mask_ref[batch] > 0.5
        outs = []
        for h in range(4):
            q = head(qkv, batch, h * HD)
            k = head(qkv, batch, 256 + (h // 2) * HD)
            v = head(qkv, batch, 384 + (h // 2) * HD)
            scores = jnp.where(allowed, dot_nt(q, k) * SCORE_SCALE, MASKED)
            lifted = jnp.exp(scores - jnp.max(scores, axis=1, keepdims=True))
            share = lifted / jnp.sum(lifted, axis=1, keepdims=True)
            outs.append(dot(share.astype(BF16), v))
        attended = jnp.concatenate(outs, axis=1).astype(BF16)
        att_ref[batch * 128 : batch * 128 + 128] = attended
        part_ref[batch] = dot(attended, wo_ref[0]).astype(BF16)


def layer_block(shape, layer):
    return pl.BlockSpec((1,) + shape, lambda i: (layer,) + (0,) * len(shape))


def whole(*shape):
    return pl.BlockSpec(shape, lambda i: (0,) * len(shape))


def local_params():
    return pltpu.CompilerParams(vmem_limit_bytes=VMEM_LIMIT)


def attention_forward(rows, wqkv, wo, tables, layer):
    cosine, sine, mask = tables
    return pl.pallas_call(
        attention_forward_kernel,
        grid=(1,),
        out_shape=[
            jax.ShapeDtypeStruct((2, 128, D), BF16),
            jax.ShapeDtypeStruct((256, 512), BF16),
            jax.ShapeDtypeStruct((256, 256), BF16),
        ],
        in_specs=[
            whole(256, D),
            layer_block((D, 512), layer),
            layer_block((256, D), layer),
            whole(256, LANES),
            whole(256, LANES),
            whole(2, 128, 128),
        ],
        out_specs=[whole(2, 128, D), whole(256, 512), whole(256, 256)],
        compiler_params=local_params(),
        name="attention_forward",
    )(rows, wqkv, wo, cosine, sine, mask)


def attention_backward_kernel(
    rows_ref,
    ga_ref,
    qkv_ref,
    att_ref,
    wqkv_ref,
    wo_ref,
    cos_ref,
    sin_ref,
    mask_ref,
    dn_ref,
    dw_ref,
):
    ga = ga_ref[...]
    rows = rows_ref[...]
    dw_ref[:, 512:] = dot_tn(ga, att_ref[...]).astype(BF16)
    gatt = dot_nt(ga, wo_ref[0]).astype(BF16)
    qkv = qkv_ref[...]
    by_batch = []
    for batch in range(2):
        allowed = mask_ref[batch] > 0.5
        gqs, gks, gvs = [], [None, None], [None, None]
        for h in range(4):
            kv = h // 2
            q = head(qkv, batch, h * HD)
            k = head(qkv, batch, 256 + kv * HD)
            v = head(qkv, batch, 384 + kv * HD)
            go = head(gatt, batch, h * HD)
            scores = jnp.where(allowed, dot_nt(q, k) * SCORE_SCALE, MASKED)
            lifted = jnp.exp(scores - jnp.max(scores, axis=1, keepdims=True))
            share = lifted / jnp.sum(lifted, axis=1, keepdims=True)
            gp = dot_nt(go, v)
            gs = share * (gp - jnp.sum(share * gp, axis=1, keepdims=True))
            gs = gs.astype(BF16)
            gqs.append(dot(gs, k) * SCORE_SCALE)
            gk = dot_tn(gs, q) * SCORE_SCALE
            gv = dot_tn(share.astype(BF16), go)
            gks[kv] = gk if gks[kv] is None else gks[kv] + gk
            gvs[kv] = gv if gvs[kv] is None else gvs[kv] + gv
        by_batch.append(jnp.concatenate(gqs + gks + gvs, axis=1))
    joined = jnp.concatenate(by_batch, axis=0)
    turned = joined[:, :384]
    turned = turned * three(cos_ref[...]) - half_swapped(turned) * three(sin_ref[...])
    gqkv = jnp.concatenate([turned, joined[:, 384:]], axis=1).astype(BF16)
    dw_ref[:, :512] = dot_tn(rows, gqkv).astype(BF16)
    dn = dot_nt(gqkv, wqkv_ref[0]).astype(BF16)
    dn_ref[0] = dn[:128]
    dn_ref[1] = dn[128:]


def attention_backward(rows, ga, qkv, att, wqkv, wo, tables, layer):
    cosine, sine, mask = tables
    return pl.pallas_call(
        attention_backward_kernel,
        grid=(1,),
        out_shape=[
            jax.ShapeDtypeStruct((2, 128, D), BF16),
            jax.ShapeDtypeStruct((D, 768), BF16),
        ],
        in_specs=[
            whole(256, D),
            whole(256, D),
            whole(256, 512),
            whole(256, 256),
            layer_block((D, 512), layer),
            layer_block((256, D), layer),
            whole(256, LANES),
            whole(256, LANES),
            whole(2, 128, 128),
        ],
        out_specs=[whole(2, 128, D), whole(D, 768)],
        compiler_params=local_params(),
        name="attention_backward",
    )(rows, ga, qkv, att, wqkv, wo, cosine, sine, mask)


def masked_softmax(logits, mask):
    routed = mask > 0.5
    shown = jnp.where(routed, logits, MASKED)
    lifted = jnp.where(routed, jnp.exp(shown - jnp.max(shown, axis=1, keepdims=True)), 0.0)
    return lifted / jnp.sum(lifted, axis=1, keepdims=True)


def experts_forward_kernel(x_ref, wgu_ref, wd_ref, router_ref, mask_ref, sel_ref, y_ref, gu_ref):
    x = x_ref[...]
    gates = masked_softmax(dot(x, router_ref[0]), mask_ref[...])
    total = None
    for e in range(2):
        gate = jnp.sum(gates * sel_ref[e : e + 1], axis=1, keepdims=True)
        gu = dot(x, wgu_ref[0, e])
        gu_ref[e] = gu.astype(BF16)
        part, upper = gu[:, :F], gu[:, F:]
        hidden = part * jax.nn.sigmoid(part) * upper
        made = dot((hidden * gate).astype(BF16), wd_ref[0, e])
        total = made if total is None else total + made
    y_ref[...] = total.astype(BF16)


def experts_forward(x, wgu, wd, router, mask, sel, layer):
    count = x.shape[0]
    tile = 256
    return pl.pallas_call(
        experts_forward_kernel,
        grid=(count // tile,),
        out_shape=[
            jax.ShapeDtypeStruct((count, D), BF16),
            jax.ShapeDtypeStruct((2, count, 2 * F), BF16),
        ],
        in_specs=[
            pl.BlockSpec((tile, D), lambda i: (i, 0)),
            layer_block((2, D, 2 * F), layer),
            layer_block((2, F, D), layer),
            layer_block((D, LANES), layer),
            pl.BlockSpec((tile, LANES), lambda i: (i, 0)),
            whole(8, LANES),
        ],
        out_specs=[
            pl.BlockSpec((tile, D), lambda i: (i, 0)),
            pl.BlockSpec((2, tile, 2 * F), lambda i: (0, i, 0)),
        ],
        compiler_params=local_params(),
        name="experts_forward",
    )(x, wgu, wd, router, mask, sel)


def experts_backward_kernel(
    x_ref,
    g_ref,
    gu_ref,
    wgu_ref,
    wd_ref,
    router_ref,
    mask_ref,
    sel_ref,
    dx_ref,
    dgu_ref,
    dd_ref,
    dr_ref,
    gates,
    gl,
    gj,
    hs,
    dx_sum,
):
    e = pl.program_id(0)
    tile = 256
    tiles = x_ref.shape[0] // tile
    chosen = jnp.where(e == 0, sel_ref[0:1], sel_ref[1:2])

    @pl.when(e == 0)
    def _():
        @pl.loop(0, tiles)
        def _(i):
            r = pl.ds(pl.multiple_of(i * tile, tile), tile)
            gates[r] = masked_softmax(dot(x_ref[r], router_ref[0]), mask_ref[r])
            gl[r] = jnp.zeros((tile, LANES), F32)

    @pl.loop(0, tiles)
    def _(i):
        r = pl.ds(pl.multiple_of(i * tile, tile), tile)
        gate = jnp.sum(gates[r] * chosen, axis=1, keepdims=True)
        gh = dot_nt(g_ref[r], wd_ref[0, 0])
        part = gu_ref[0, r, :F].astype(F32)
        upper = gu_ref[0, r, F:].astype(F32)
        s = jax.nn.sigmoid(part)
        act = part * s
        hidden = act * upper
        gl[r] += (gate * jnp.sum(hidden * gh, axis=1, keepdims=True)) * chosen
        hs[r] = (hidden * gate).astype(BF16)
        gh = gh * gate
        gj[r, :F] = (gh * upper * (s + act * (1.0 - s))).astype(BF16)
        gj[r, F:] = (gh * act).astype(BF16)
        dx = dot_nt(gj[r], wgu_ref[0, 0])

        @pl.when(e == 0)
        def _():
            dx_sum[r] = dx

        @pl.when(e == 1)
        def _():
            dx_ref[r] = (dx_sum[r] + dx + dot_nt(gl[r].astype(BF16), router_ref[0])).astype(BF16)

    @pl.loop(0, D // 256)
    def _(i):
        c = pl.ds(pl.multiple_of(i * 256, 256), 256)
        dgu_ref[0, c] = dot_tn(x_ref[:, c], gj[...]).astype(BF16)

    @pl.loop(0, F // 256)
    def _(i):
        c = pl.ds(pl.multiple_of(i * 256, 256), 256)
        dd_ref[0, c] = dot_tn(hs[:, c], g_ref[...]).astype(BF16)

    @pl.when(e == 1)
    def _():
        dr_ref[...] = dot_tn(gl[...].astype(BF16), x_ref[...])[:E]


def experts_backward(x, g, gu, wgu, wd, router, mask, sel, layer):
    count = x.shape[0]
    return pl.pallas_call(
        experts_backward_kernel,
        grid=(2,),
        out_shape=[
            jax.ShapeDtypeStruct((count, D), BF16),
            jax.ShapeDtypeStruct((2, D, 2 * F), BF16),
            jax.ShapeDtypeStruct((2, F, D), BF16),
            jax.ShapeDtypeStruct((E, D), F32),
        ],
        in_specs=[
            whole(count, D),
            whole(count, D),
            pl.BlockSpec((1, count, 2 * F), lambda e: (e, 0, 0)),
            pl.BlockSpec((1, 1, D, 2 * F), lambda e: (layer, e, 0, 0)),
            pl.BlockSpec((1, 1, F, D), lambda e: (layer, e, 0, 0)),
            layer_block((D, LANES), layer),
            whole(count, LANES),
            whole(8, LANES),
        ],
        out_specs=[
            whole(count, D),
            pl.BlockSpec((1, D, 2 * F), lambda e: (e, 0, 0)),
            pl.BlockSpec((1, F, D), lambda e: (e, 0, 0)),
            whole(E, D),
        ],
        scratch_shapes=[
            pltpu.VMEM((count, LANES), F32),
            pltpu.VMEM((count, LANES), F32),
            pltpu.VMEM((count, 2 * F), BF16),
            pltpu.VMEM((count, F), BF16),
            pltpu.VMEM((count, D), F32),
        ],
        compiler_params=local_params(),
        name="experts_backward",
    )(x, g, gu, wgu, wd, router, mask, sel)


def inverse_rms(values):
    return lax.rsqrt(jnp.mean(values * values, axis=1, keepdims=True) + EPSILON)


def layer_forward(layer_in, layer, common, weights):
    tables, mask_own, mask_all, sel = common
    wqkv, wo, gains, router, wgu, wd = weights
    inverse_one = inverse_rms(layer_in)
    normed = (layer_in * inverse_one * gains[layer, 0:1]).astype(BF16)
    rows = tp_gather(normed.reshape(2, 32, D)).reshape(256, D)
    part, qkv, att = attention_forward(rows, wqkv, wo, tables, layer)
    after = layer_in + tp_scatter(part).reshape(64, D)
    inverse_two = inverse_rms(after)
    normed_two = (after * inverse_two * gains[layer, 1:2]).astype(BF16)
    x_all = exp_gather(normed_two).reshape(1024, D)
    made, gu = experts_forward(x_all, wgu, wd, router, mask_all, sel, layer)
    y = exp_scatter(made, 5)
    stored = (layer_in, inverse_one, rows, qkv, att, after, inverse_two, normed_two, x_all, gu, y)
    return after + y, stored


def layer_backward(grad, stored, layer, common, weights):
    tables, mask_own, mask_all, sel = common
    wqkv, wo, gains, router, wgu, wd = weights
    layer_in, inverse_one, rows, qkv, att, after, inverse_two, normed_two, x_all, gu, y = stored
    g_all = exp_gather(grad).reshape(1024, D)
    dx, dgu, dd, dr = experts_backward(x_all, g_all, gu, wgu, wd, router, mask_all, sel, layer)
    gates = masked_softmax(dot(normed_two, router[layer]), mask_own)
    gf = grad.astype(F32)
    gc = (gates * jnp.sum(gf * y, axis=1, keepdims=True)).astype(BF16)
    grad_n = exp_scatter(dx, 5) - dot_nt(gc, router[layer])
    dr = dr - dot_tn(gc, normed_two)[:E]
    scaled = grad_n * gains[layer, 1:2]
    grad_after = (
        gf
        + inverse_two * scaled
        - after * inverse_two**3 * jnp.mean(after * scaled, axis=1, keepdims=True)
    )
    d_mixture = jnp.sum(grad_n * after * inverse_two, axis=0, keepdims=True)
    ga = tp_gather(grad_after.astype(BF16).reshape(2, 32, D)).reshape(256, D)
    dn, dw = attention_backward(rows, ga, qkv, att, wqkv, wo, tables, layer)
    grad_n = tp_scatter(dn).reshape(64, D)
    scaled = grad_n * gains[layer, 0:1]
    grad_in = (
        grad_after
        + inverse_one * scaled
        - layer_in * inverse_one**3 * jnp.mean(layer_in * scaled, axis=1, keepdims=True)
    )
    d_attention = jnp.sum(grad_n * layer_in * inverse_one, axis=0, keepdims=True)
    small = jnp.concatenate([dr, d_attention, d_mixture, jnp.zeros((6, D), F32)], axis=0)
    return grad_in, (dgu, dd, dw, small)


def rope_tables(seg_rows):
    length = seg_rows.shape[0]
    before = jnp.sum((seg_rows[None, :] < seg_rows[:, None]).astype(jnp.int32), axis=1)
    places = (jnp.arange(length, dtype=jnp.int32) - before).astype(F32)
    powers = jnp.arange(0, HD, 2, dtype=jnp.int32).astype(F32) / HD
    angles = places[:, None] * (ROPE_BASE ** (-powers))[None, :]
    cosine, sine = jnp.cos(angles), jnp.sin(angles)
    indices = jnp.arange(length, dtype=jnp.int32)
    allowed = (seg_rows[:, None] == seg_rows[None, :]) & (indices[None, :] <= indices[:, None])
    return (
        jnp.concatenate([cosine] * 4, axis=1),
        jnp.concatenate([-sine, sine, -sine, sine], axis=1),
        allowed.astype(F32),
    )


def routed(routes):
    labels = jnp.arange(LANES, dtype=jnp.int32)
    return jnp.sum((routes[:, :, None] == labels[None, None, :]).astype(F32), axis=1)


def per_device(
    activations,
    cotangent,
    segments,
    routes,
    attention_gain,
    query_weight,
    key_weight,
    value_weight,
    output_weight,
    mixture_gain,
    router_weight,
    expert_gate_up,
    expert_down,
):
    section = lax.axis_index("section")
    expert = lax.axis_index("exp")

    def own_batches(array):
        return lax.dynamic_slice_in_dim(array, 2 * section, 2, 0)

    def to_owner(first, second):
        sent = jnp.where(section == 0, second, first)
        kept = jnp.where(section == 0, first, second)
        return kept, lax.ppermute(sent, "section", [(0, 1), (1, 0)])

    def by_layer(first, second):
        kept, got = to_owner(first, second)
        kept, got = kept.reshape(2, 32, D), got.reshape(2, 32, D)
        return jnp.where(
            section == 0,
            jnp.concatenate([kept, got], axis=0),
            jnp.concatenate([got, kept], axis=0),
        )[None]

    qkv_own = jnp.concatenate([query_weight, key_weight, value_weight], axis=2)
    gains_own = jnp.concatenate(
        [attention_gain, mixture_gain, jnp.zeros((6, D), BF16)], axis=0
    ).astype(F32)[None]
    router_own = jnp.pad(router_weight, ((0, 0), (0, 0), (0, LANES - E)))
    wqkv, wo, gains, router = pair_gather([qkv_own, output_weight, gains_own, router_own], 0)
    wgu, wd = pair_gather([expert_gate_up, expert_down], 1)
    weights = (wqkv, wo, gains, router, wgu, wd)

    cosine, sine, mask = jax.vmap(rope_tables)(own_batches(segments))
    tables = (cosine.reshape(256, LANES), sine.reshape(256, LANES), mask)
    routes_own = own_batches(routes).reshape(64, 8)
    routes_all = lax.all_gather(routes_own, "exp", axis=0, tiled=True)
    lanes = lax.broadcasted_iota(jnp.int32, (8, LANES), 1)
    sel = (lanes == 2 * expert + lax.broadcasted_iota(jnp.int32, (8, LANES), 0)).astype(F32)
    common = (tables, routed(routes_own), routed(routes_all), sel)

    start = own_batches(activations).reshape(64, D).astype(F32)
    result, kept_first = layer_forward(start, 0, common, weights)
    out_first = result.astype(BF16)
    result, kept_second = layer_forward(out_first.astype(F32), 1, common, weights)
    out_second = result.astype(BF16)
    grad = own_batches(cotangent).reshape(64, D)
    grad_second, pieces_second = layer_backward(grad, kept_second, 1, common, weights)
    grad_first, pieces_first = layer_backward(
        grad_second.astype(BF16), kept_first, 0, common, weights
    )

    def summed(first, second):
        kept, got = to_owner(first, second)
        return kept.astype(F32) + got.astype(F32)

    dgu, dd, dw, small = [summed(a, b) for a, b in zip(pieces_first, pieces_second)]
    dgu = lax.psum_scatter(dgu.astype(BF16), "tp", scatter_dimension=2, tiled=True)
    dd = lax.psum_scatter(dd.astype(BF16), "tp", scatter_dimension=2, tiled=True)
    dw = exp_scatter(dw.astype(BF16), 6)
    small = lax.psum(small, ("exp", "tp"))
    return (
        by_layer(out_first, out_second),
        by_layer(grad_first, grad_second),
        small[E : E + 1],
        dw[None, :, :256],
        dw[None, :, 256:384],
        dw[None, :, 384:512],
        dw[:, 512:].T[None],
        small[E + 1 : E + 2],
        small[:E].T[None],
        dgu.astype(F32)[None],
        dd.astype(F32)[None],
    )


def solution(mesh):
    placed = (
        P(None, ("exp", "tp"), None),
        P(None, ("exp", "tp"), None),
        P(None, "exp"),
        P(None, ("exp", "tp"), None),
        P("section", None),
        P("section", None, "tp"),
        P("section", None, "tp"),
        P("section", None, "tp"),
        P("section", "tp", None),
        P("section", None),
        P("section", None, None),
        P("section", "exp", None, None),
        P("section", "exp", None, None),
    )
    return jax.shard_map(
        per_device,
        mesh=mesh,
        in_specs=placed,
        out_specs=(
            P("section", None, ("exp", "tp"), None),
            P("section", None, ("exp", "tp"), None),
            P("section", None),
            P("section", "exp", "tp"),
            P("section", "exp", "tp"),
            P("section", "exp", "tp"),
            P("section", "tp", "exp"),
            P("section", None),
            P("section", None, None),
            P("section", "exp", None, "tp"),
            P("section", "exp", None, "tp"),
        ),
        check_vma=False,
    )
```

```python
import functools

import jax
import jax.numpy as jnp
from jax import lax
from jax.experimental import pallas as pl
from jax.experimental.pallas import tpu as pltpu
from jax.sharding import PartitionSpec as P

D = 1024
HD = 64
E = 32
F = 512
LANES = 128
EPSILON = 1e-06
ROPE_BASE = 10000.0
SCORE_SCALE = 0.125
MASKED = -1e30
MESH = pl.DeviceIdType.MESH
VMEM_LIMIT = 56 * 1024 * 1024
BF16 = jnp.bfloat16
F32 = jnp.float32


def dot(a, b):
    return jnp.dot(a, b, preferred_element_type=F32)


def dot_nt(a, b):
    return lax.dot_general(a, b, (((1,), (1,)), ((), ())), preferred_element_type=F32)


def dot_tn(a, b):
    return lax.dot_general(a, b, (((0,), (0,)), ((), ())), preferred_element_type=F32)


def in_vmem():
    return pl.BlockSpec(memory_space=pltpu.VMEM)


def in_any():
    return pl.BlockSpec(memory_space=pl.ANY)


def greet(peers):
    barrier = pltpu.get_barrier_semaphore()
    for peer in peers:
        pl.semaphore_signal(barrier, inc=1, device_id=peer, device_id_type=MESH)
    pl.semaphore_wait(barrier, len(peers))


def remote(src, dst, send_sem, recv_sem, peer):
    return pltpu.make_async_remote_copy(
        src_ref=src,
        dst_ref=dst,
        send_sem=send_sem,
        recv_sem=recv_sem,
        device_id=peer,
        device_id_type=MESH,
    )


def comm_params(number):
    return pltpu.CompilerParams(
        collective_id=number, has_side_effects=True, vmem_limit_bytes=VMEM_LIMIT
    )


class Part:
    def __init__(self, arrays, in_specs, out_shapes, out_specs, scratch, axes, body):
        self.arrays, self.in_specs = arrays, in_specs
        self.out_shapes, self.out_specs = out_shapes, out_specs
        self.scratch, self.axes, self.body = scratch, axes, body


def around(axis):
    if axis == "section":
        return [{"section": 1 - lax.axis_index("section")}]
    if axis == "tp":
        me = lax.axis_index("tp")
        return [{"tp": lax.rem(me + j, 4)} for j in (3, 1)]
    if axis == "tp_opposite":
        return [{"tp": lax.rem(lax.axis_index("tp") + 2, 4)}]
    me = lax.axis_index("exp")
    at_x, at_z = me // 4, lax.rem(me, 4)
    if axis == "x":
        return [{"exp": lax.rem(at_x + j, 4) * 4 + at_z} for j in (3, 1)]
    return [{"exp": at_x * 4 + lax.rem(at_z + j, 4)} for j in (3, 1)]


def fused_kernel(parts, *refs):
    refs = list(refs)

    def take(count):
        taken = refs[:count]
        del refs[:count]
        return taken

    ins = [take(len(part.arrays)) for part in parts]
    outs = [take(len(part.out_shapes)) for part in parts]
    scratch = [take(len(part.scratch)) for part in parts]
    axes = []
    for part in parts:
        axes += [axis for axis in part.axes if axis not in axes]
    greet([peer for axis in axes for peer in around(axis)])
    running = [part.body(i, o, s) for part, i, o, s in zip(parts, ins, outs, scratch)]
    while running:
        for one in list(running):
            if next(one, "end") == "end":
                running.remove(one)


def fuse(parts, number, name):
    outs = pl.pallas_call(
        functools.partial(fused_kernel, parts),
        out_shape=[o for part in parts for o in part.out_shapes],
        in_specs=[s for part in parts for s in part.in_specs],
        out_specs=[s for part in parts for s in part.out_specs],
        scratch_shapes=[s for part in parts for s in part.scratch],
        compiler_params=comm_params(number),
        name=name,
    )(*[a for part in parts for a in part.arrays])
    outs = list(outs)
    results = []
    for part in parts:
        count = len(part.out_shapes)
        results.append(outs[:count] if count > 1 else outs[0])
        outs = outs[count:]
    return results


def sems(*shape):
    return [pltpu.SemaphoreType.DMA(shape)] * 2


def pair_part(arrays):
    count = len(arrays)

    def body(ins, outs, scratch):
        held, (send, recv, read, write) = scratch[:count], scratch[count:]
        me = lax.axis_index("section")
        (peer,) = around("section")
        sends, reads, writes = [], [], []
        for at in range(count):
            sends.append(remote(ins[at].at[0], outs[at].at[me], send.at[at], recv.at[at], peer))
            reads.append(pltpu.make_async_copy(ins[at].at[0], held[at], read.at[at]))
            writes.append(pltpu.make_async_copy(held[at], outs[at].at[me], write.at[at]))
            sends[-1].start()
            reads[-1].start()
        yield
        for at in range(count):
            reads[at].wait()
            writes[at].start()
        yield
        yield
        yield
        for at in range(count):
            writes[at].wait()
            sends[at].wait()

    return Part(
        arrays,
        [in_any()] * count,
        [jax.ShapeDtypeStruct((2,) + a.shape[1:], a.dtype) for a in arrays],
        [in_any()] * count,
        [pltpu.VMEM(a.shape[1:], a.dtype) for a in arrays]
        + [pltpu.SemaphoreType.DMA((count,))] * 4,
        ["section"],
        body,
    )


class RingGather:
    def __init__(self, view, own, left, right, send, recv):
        self.view, self.own = view, own
        self.left, self.right, self.send, self.recv = left, right, send, recv
        self.copies = []

    def go(self, src, dst, at, peer):
        copy = remote(src, dst, self.send[at], self.recv[at], peer)
        copy.start()
        self.copies.append(copy)

    def start(self):
        own = self.view(0, None) if self.own is None else self.own
        self.go(own, self.view(0, None), 0, self.right)
        self.go(own, self.view(0, None), 1, self.left)

    def forward(self):
        self.copies[0].wait_recv()
        self.go(self.view(3, 0), self.view(3, 0), 2, self.right)
        self.copies[1].wait_recv()
        self.go(self.view(1, 1), self.view(1, 1), 3, self.left)

    def finish(self):
        self.copies[2].wait_recv()
        self.copies[3].wait_recv()

    def drain(self):
        for copy in self.copies:
            copy.wait_send()


class RingScatter:
    def __init__(self, view, temp, block, stage, left, right, send, recv):
        self.view, self.temp, self.block, self.stage = view, temp, block, stage
        self.left, self.right, self.send, self.recv = left, right, send, recv
        self.copies = []

    def go(self, src, dst, at, peer):
        copy = remote(src, dst, self.send[at], self.recv[at], peer)
        copy.start()
        self.copies.append(copy)

    def start(self):
        self.go(self.view(2, 0), self.temp(0), 0, self.right)
        self.go(self.view(2, 1), self.temp(1), 1, self.left)
        self.go(self.view(1, 1), self.block(0, 1), 2, self.right)
        self.go(self.view(3, 0), self.block(1, 0), 3, self.left)

    def middle(self):
        for side, nearer, peer in ((0, 1, self.right), (1, 3, self.left)):
            self.copies[side].wait_recv()
            term = self.view(nearer, side)[...].astype(F32) + self.temp(side)[...].astype(F32)
            self.stage(side)[...] = term.astype(BF16)
            self.go(self.stage(side), self.block(side, side), 4 + side, peer)

    def finish(self):
        for copy in self.copies[2:]:
            copy.wait_recv()

    def total(self, part):
        return (
            self.view(0, part)[...].astype(F32)
            + self.block(0, part)[...].astype(F32)
            + self.block(1, part)[...].astype(F32)
        )

    def drain(self):
        for copy in self.copies:
            copy.wait_send()


def tp_block(ref, k, part):
    place = lax.rem(lax.axis_index("tp") + k, 4)
    rows = pl.ds(pl.multiple_of(place * 32, 32), 32)
    return ref.at[:, rows] if part is None else ref.at[part, rows]


def tp_gather_part(x):
    def body(ins, outs, scratch):
        (x_ref,), (out_ref,), (send, recv) = ins, outs, scratch
        left, right = around("tp")
        ring = RingGather(
            functools.partial(tp_block, out_ref),
            x_ref,
            left,
            right,
            [send.at[i] for i in range(4)],
            [recv.at[i] for i in range(4)],
        )
        ring.start()
        tp_block(out_ref, 0, None)[...] = x_ref[...]
        yield
        ring.forward()
        yield
        ring.finish()
        ring.drain()

    return Part(
        [x],
        [in_vmem()],
        [jax.ShapeDtypeStruct((2, 128, D), BF16)],
        [in_vmem()],
        sems(4),
        ["tp"],
        body,
    )


def tp_scatter_part(x):
    def body(ins, outs, scratch):
        (x_ref,), (out_ref,), (temp, block, stage, send, recv) = ins, outs, scratch
        left, right = around("tp")
        ring = RingScatter(
            functools.partial(tp_block, x_ref),
            lambda side: temp.at[side],
            lambda side, part: block.at[side, part],
            lambda side: stage.at[side],
            left,
            right,
            [send.at[i] for i in range(6)],
            [recv.at[i] for i in range(6)],
        )
        ring.start()
        yield
        ring.middle()
        yield
        ring.finish()
        out_ref[0] = ring.total(0)
        out_ref[1] = ring.total(1)
        ring.drain()

    return Part(
        [x],
        [in_vmem()],
        [jax.ShapeDtypeStruct((2, 32, D), F32)],
        [in_vmem()],
        [
            pltpu.VMEM((2, 32, D), BF16),
            pltpu.VMEM((2, 2, 32, D), BF16),
            pltpu.VMEM((2, 32, D), BF16),
        ]
        + sems(6),
        ["tp"],
        body,
    )


def exp_block(ref, half, i, j, part):
    me = lax.axis_index("exp")
    at_x, at_z = me // 4, lax.rem(me, 4)
    i, j = (i, j) if half == 0 else (j, i)
    rows = pl.ds(32 * half, 32) if part is None else pl.ds(32 * half + 16 * part, 16)
    return ref.at[lax.rem(at_x + i, 4), lax.rem(at_z + j, 4), rows]


def exp_gather_steps(x_ref, out_ref, send, recv):
    sides = [around("x"), around("z")]
    first, second = [], []
    for half in range(2):

        def ring(view, own, at, axis, half=half):
            return RingGather(
                view,
                own,
                sides[axis][0],
                sides[axis][1],
                [send.at[half, at, n] for n in range(4)],
                [recv.at[half, at, n] for n in range(4)],
            )

        def along(k, part, half=half):
            return exp_block(out_ref, half, k, 0, part)

        own = x_ref.at[pl.ds(32 * half, 32)]
        first.append(ring(along, own, 4, half))
        second.append([])
        for i in range(4):

            def across(k, part, half=half, i=i):
                return exp_block(out_ref, half, i, k, part)

            second[half].append(ring(across, own if i == 0 else None, i, 1 - half))
    for half in range(2):
        first[half].start()
    for half in range(2):
        second[half][0].start()
        exp_block(out_ref, half, 0, 0, None)[...] = x_ref[pl.ds(32 * half, 32)]
    yield
    for half in range(2):
        first[half].forward()
        second[half][3].start()
        second[half][1].start()
    yield
    for half in range(2):
        second[half][0].forward()
    yield
    for half in range(2):
        first[half].finish()
        second[half][2].start()
    yield
    for i in (3, 1):
        for half in range(2):
            second[half][i].forward()
    yield
    for half in range(2):
        second[half][2].forward()
    yield
    for half in range(2):
        for ring in second[half]:
            ring.finish()
        for ring in second[half] + [first[half]]:
            ring.drain()


def exp_gather_part(x):
    def body(ins, outs, scratch):
        yield from exp_gather_steps(ins[0], outs[0], *scratch)

    return Part(
        [x],
        [in_vmem()],
        [jax.ShapeDtypeStruct((4, 4, 64, x.shape[1]), x.dtype)],
        [in_vmem()],
        sems(2, 5, 4),
        ["x", "z"],
        body,
    )


def exp_scatter_steps(x_ref, out_ref, temp, block, stage, ready, send, recv):
    sides = [around("x"), around("z")]
    first, second = [], []
    for half in range(2):

        def ring(view, at, axis, half=half):
            return RingScatter(
                view,
                lambda side: temp.at[half, at, side],
                lambda side, part: block.at[half, at, side, pl.ds(16 * part, 16)],
                lambda side: stage.at[half, at, side],
                sides[axis][0],
                sides[axis][1],
                [send.at[half, at, n] for n in range(6)],
                [recv.at[half, at, n] for n in range(6)],
            )

        first.append([])
        for j in range(4):

            def along(k, part, half=half, j=j):
                return exp_block(x_ref, half, k, j, part)

            first[half].append(ring(along, j, half))

        def across(k, part, half=half):
            return ready.at[half, k, pl.ds(16 * part, 16)]

        second.append(ring(across, 4, 1 - half))
    order = (2, 1, 3, 0)
    for j in order:
        for half in range(2):
            first[half][j].start()
    yield
    for j in order:
        for half in range(2):
            first[half][j].middle()
        yield
    for j in order:
        for half in range(2):
            first[half][j].finish()
            for part in range(2):
                ready[half, j, pl.ds(16 * part, 16)] = first[half][j].total(part).astype(BF16)
            if j == 3:
                second[half].start()
    yield
    for half in range(2):
        second[half].middle()
    yield
    for half in range(2):
        second[half].finish()
        for part in range(2):
            out_ref[pl.ds(32 * half + 16 * part, 16)] = second[half].total(part)
    for half in range(2):
        for ring in first[half] + [second[half]]:
            ring.drain()


def exp_scatter_scratch(width):
    return [
        pltpu.VMEM((2, 5, 2, 16, width), BF16),
        pltpu.VMEM((2, 5, 2, 32, width), BF16),
        pltpu.VMEM((2, 5, 2, 16, width), BF16),
        pltpu.VMEM((2, 4, 32, width), BF16),
    ] + sems(2, 5, 6)


def exp_scatter_part(x):
    width = x.shape[-1]

    def body(ins, outs, scratch):
        yield from exp_scatter_steps(ins[0], outs[0], *scratch)

    return Part(
        [x.reshape(4, 4, 64, width)],
        [in_vmem()],
        [jax.ShapeDtypeStruct((64, width), F32)],
        [in_vmem()],
        exp_scatter_scratch(width),
        ["x", "z"],
        body,
    )


def expert_part(grads, first_row):
    rows = pl.ds(first_row, 512)

    def body(ins, outs, scratch):
        (g_ref,), (out_ref,) = ins, outs
        own, got, temp, block, stage, send, recv, read, swap_send, swap_recv = scratch
        me = lax.axis_index("section")
        place = lax.axis_index("tp")
        left, right = around("tp")
        (peer,) = around("section")
        swap = remote(g_ref.at[1 - me, rows], got, swap_send.at[0], swap_recv.at[0], peer)
        swap.start()
        kept = pltpu.make_async_copy(g_ref.at[me, rows], own, read.at[0])
        kept.start()
        yield
        kept.wait()
        swap.wait_recv()

        @pl.loop(0, 8)
        def _(i):
            r = pl.ds(pl.multiple_of(i * 64, 64), 64)
            own[r] = (own[r].astype(F32) + got[r].astype(F32)).astype(BF16)

        def view(k, part):
            columns = pl.multiple_of(lax.rem(place + k, 4) * 256, 256)
            return own.at[pl.ds(256 * part, 256), pl.ds(columns, 256)]

        ring = RingScatter(
            view,
            lambda side: temp.at[side],
            lambda side, part: block.at[side, part],
            lambda side: stage.at[side],
            left,
            right,
            [send.at[i] for i in range(6)],
            [recv.at[i] for i in range(6)],
        )
        ring.start()
        yield
        yield
        yield
        ring.middle()
        yield
        yield
        yield
        ring.finish()
        out_ref[:256] = ring.total(0).astype(BF16)
        out_ref[256:] = ring.total(1).astype(BF16)
        ring.drain()
        swap.wait_send()

    return Part(
        [grads],
        [in_any()],
        [jax.ShapeDtypeStruct((512, 256), BF16)],
        [in_vmem()],
        [
            pltpu.VMEM((512, D), BF16),
            pltpu.VMEM((512, D), BF16),
            pltpu.VMEM((2, 256, 256), BF16),
            pltpu.VMEM((2, 2, 256, 256), BF16),
            pltpu.VMEM((2, 256, 256), BF16),
        ]
        + sems(6)
        + [pltpu.SemaphoreType.DMA((1,))] * 3,
        ["section", "tp"],
        body,
    )


WIDE = 896


def settle_part(first, second):
    def body(ins, outs, scratch):
        first_ref, second_ref = ins
        out_ref, small_ref = outs
        got, x_ref, total, piece, held = scratch[:5]
        scatter, rest = scratch[5:11], scratch[11:]
        swap_send, swap_recv, tp_send, tp_recv, gather_send, gather_recv = rest
        me = lax.axis_index("section")
        (peer,) = around("section")
        copies = [
            remote(ref, got, swap_send.at[0], swap_recv.at[0], peer)
            for ref in (second_ref, first_ref)
        ]
        for layer in range(2):

            @pl.when(me == layer)
            def _():
                copies[layer].start()

        yield
        copies[0].wait_recv()
        for at_x in range(4):
            for at_z in range(4):
                mine = jnp.where(me == 0, first_ref[at_x, at_z], second_ref[at_x, at_z])
                summed = mine.astype(F32) + got[at_x, at_z].astype(F32)
                x_ref[at_x, at_z] = summed.astype(BF16)
        yield from exp_scatter_steps(x_ref, total, *scatter)
        out_ref[...] = total[:, :768]
        piece[...] = total[:, 768:]
        partners = around("tp") + around("tp_opposite")
        sent = [
            remote(piece, held.at[at], tp_send.at[at], tp_recv.at[at], partner)
            for at, partner in enumerate(partners)
        ]
        for copy in sent:
            copy.start()
        yield
        for copy in sent:
            copy.wait()
        piece[...] = piece[...] + ((held[0] + held[1]) + held[2])
        yield from exp_gather_steps(piece, small_ref, gather_send, gather_recv)
        copies[0].wait_send()

    return Part(
        [first.reshape(4, 4, 64, WIDE), second.reshape(4, 4, 64, WIDE)],
        [in_vmem()] * 2,
        [
            jax.ShapeDtypeStruct((64, 768), F32),
            jax.ShapeDtypeStruct((4, 4, 64, LANES), F32),
        ],
        [in_vmem()] * 2,
        [
            pltpu.VMEM((4, 4, 64, WIDE), BF16),
            pltpu.VMEM((4, 4, 64, WIDE), BF16),
            pltpu.VMEM((64, WIDE), F32),
            pltpu.VMEM((64, LANES), F32),
            pltpu.VMEM((3, 64, LANES), F32),
        ]
        + exp_scatter_scratch(WIDE)
        + [pltpu.SemaphoreType.DMA((1,))] * 2
        + sems(3)
        + sems(2, 5, 4),
        ["section", "x", "z", "tp", "tp_opposite"],
        body,
    )


def half_swapped(values):
    width = values.shape[1]
    lane = lax.broadcasted_iota(jnp.int32, values.shape, 1)
    ahead = pltpu.roll(values, width - 32, 1)
    behind = pltpu.roll(values, 32, 1)
    return jnp.where(lax.rem(lane, 64) < 32, ahead, behind)


def three(table):
    return jnp.concatenate([table, table, table], axis=1)


def head(values, batch, first):
    return values[batch * 128 : batch * 128 + 128, first : first + HD]


def attention_forward_kernel(
    rows_ref, wqkv_ref, wo_ref, cos_ref, sin_ref, mask_ref, part_ref, qkv_ref, att_ref
):
    joined = dot(rows_ref[...], wqkv_ref[0])
    turned = joined[:, :384]
    turned = turned * three(cos_ref[...]) + half_swapped(turned) * three(sin_ref[...])
    qkv = jnp.concatenate([turned, joined[:, 384:]], axis=1).astype(BF16)
    qkv_ref[...] = qkv
    for batch in range(2):
        allowed = mask_ref[batch] > 0.5
        outs = []
        for h in range(4):
            q = head(qkv, batch, h * HD)
            k = head(qkv, batch, 256 + (h // 2) * HD)
            v = head(qkv, batch, 384 + (h // 2) * HD)
            scores = jnp.where(allowed, dot_nt(q, k) * SCORE_SCALE, MASKED)
            lifted = jnp.exp(scores - jnp.max(scores, axis=1, keepdims=True))
            share = lifted / jnp.sum(lifted, axis=1, keepdims=True)
            outs.append(dot(share.astype(BF16), v))
        attended = jnp.concatenate(outs, axis=1).astype(BF16)
        att_ref[batch * 128 : batch * 128 + 128] = attended
        part_ref[batch] = dot(attended, wo_ref[0]).astype(BF16)


def layer_block(shape, layer):
    return pl.BlockSpec((1,) + shape, lambda i: (layer,) + (0,) * len(shape))


def whole(*shape):
    return pl.BlockSpec(shape, lambda i: (0,) * len(shape))


def local_params():
    return pltpu.CompilerParams(vmem_limit_bytes=VMEM_LIMIT)


def attention_forward(rows, wqkv, wo, tables, layer):
    cosine, sine, mask = tables
    return pl.pallas_call(
        attention_forward_kernel,
        grid=(1,),
        out_shape=[
            jax.ShapeDtypeStruct((2, 128, D), BF16),
            jax.ShapeDtypeStruct((256, 512), BF16),
            jax.ShapeDtypeStruct((256, 256), BF16),
        ],
        in_specs=[
            whole(256, D),
            layer_block((D, 512), layer),
            layer_block((256, D), layer),
            whole(256, LANES),
            whole(256, LANES),
            whole(2, 128, 128),
        ],
        out_specs=[whole(2, 128, D), whole(256, 512), whole(256, 256)],
        compiler_params=local_params(),
        name="attention_forward",
    )(rows, wqkv, wo, cosine, sine, mask)


def attention_backward_kernel(
    rows_ref,
    ga_ref,
    qkv_ref,
    att_ref,
    wqkv_ref,
    wo_ref,
    cos_ref,
    sin_ref,
    mask_ref,
    dn_ref,
    dw_ref,
):
    ga = ga_ref[...]
    rows = rows_ref[...]
    dw_ref[:, 512:] = dot_tn(ga, att_ref[...]).astype(BF16)
    gatt = dot_nt(ga, wo_ref[0]).astype(BF16)
    qkv = qkv_ref[...]
    by_batch = []
    for batch in range(2):
        allowed = mask_ref[batch] > 0.5
        gqs, gks, gvs = [], [None, None], [None, None]
        for h in range(4):
            kv = h // 2
            q = head(qkv, batch, h * HD)
            k = head(qkv, batch, 256 + kv * HD)
            v = head(qkv, batch, 384 + kv * HD)
            go = head(gatt, batch, h * HD)
            scores = jnp.where(allowed, dot_nt(q, k) * SCORE_SCALE, MASKED)
            lifted = jnp.exp(scores - jnp.max(scores, axis=1, keepdims=True))
            share = lifted / jnp.sum(lifted, axis=1, keepdims=True)
            gp = dot_nt(go, v)
            gs = share * (gp - jnp.sum(share * gp, axis=1, keepdims=True))
            gs = gs.astype(BF16)
            gqs.append(dot(gs, k) * SCORE_SCALE)
            gk = dot_tn(gs, q) * SCORE_SCALE
            gv = dot_tn(share.astype(BF16), go)
            gks[kv] = gk if gks[kv] is None else gks[kv] + gk
            gvs[kv] = gv if gvs[kv] is None else gvs[kv] + gv
        by_batch.append(jnp.concatenate(gqs + gks + gvs, axis=1))
    joined = jnp.concatenate(by_batch, axis=0)
    turned = joined[:, :384]
    turned = turned * three(cos_ref[...]) - half_swapped(turned) * three(sin_ref[...])
    gqkv = jnp.concatenate([turned, joined[:, 384:]], axis=1).astype(BF16)
    dw_ref[:, :512] = dot_tn(rows, gqkv).astype(BF16)
    dn = dot_nt(gqkv, wqkv_ref[0]).astype(BF16)
    dn_ref[0] = dn[:128]
    dn_ref[1] = dn[128:]


def attention_backward(rows, ga, qkv, att, wqkv, wo, tables, layer):
    cosine, sine, mask = tables
    return pl.pallas_call(
        attention_backward_kernel,
        grid=(1,),
        out_shape=[
            jax.ShapeDtypeStruct((2, 128, D), BF16),
            jax.ShapeDtypeStruct((D, 768), BF16),
        ],
        in_specs=[
            whole(256, D),
            whole(256, D),
            whole(256, 512),
            whole(256, 256),
            layer_block((D, 512), layer),
            layer_block((256, D), layer),
            whole(256, LANES),
            whole(256, LANES),
            whole(2, 128, 128),
        ],
        out_specs=[whole(2, 128, D), whole(D, 768)],
        compiler_params=local_params(),
        name="attention_backward",
    )(rows, ga, qkv, att, wqkv, wo, cosine, sine, mask)


def masked_softmax(logits, mask):
    routed = mask > 0.5
    shown = jnp.where(routed, logits, MASKED)
    lifted = jnp.where(routed, jnp.exp(shown - jnp.max(shown, axis=1, keepdims=True)), 0.0)
    return lifted / jnp.sum(lifted, axis=1, keepdims=True)


def experts_forward_kernel(x_ref, wgu_ref, wd_ref, router_ref, mask_ref, sel_ref, y_ref, gu_ref):
    x = x_ref[...]
    gates = masked_softmax(dot(x, router_ref[0]), mask_ref[...])
    total = None
    for e in range(2):
        gate = jnp.sum(gates * sel_ref[e : e + 1], axis=1, keepdims=True)
        gu = dot(x, wgu_ref[0, e])
        gu_ref[e] = gu.astype(BF16)
        part, upper = gu[:, :F], gu[:, F:]
        hidden = part * jax.nn.sigmoid(part) * upper
        made = dot((hidden * gate).astype(BF16), wd_ref[0, e])
        total = made if total is None else total + made
    y_ref[...] = total.astype(BF16)


def experts_forward(x, wgu, wd, router, mask, sel, layer):
    count = x.shape[0]
    tile = 256
    return pl.pallas_call(
        experts_forward_kernel,
        grid=(count // tile,),
        out_shape=[
            jax.ShapeDtypeStruct((count, D), BF16),
            jax.ShapeDtypeStruct((2, count, 2 * F), BF16),
        ],
        in_specs=[
            pl.BlockSpec((tile, D), lambda i: (i, 0)),
            layer_block((2, D, 2 * F), layer),
            layer_block((2, F, D), layer),
            layer_block((D, LANES), layer),
            pl.BlockSpec((tile, LANES), lambda i: (i, 0)),
            whole(8, LANES),
        ],
        out_specs=[
            pl.BlockSpec((tile, D), lambda i: (i, 0)),
            pl.BlockSpec((2, tile, 2 * F), lambda i: (0, i, 0)),
        ],
        compiler_params=local_params(),
        name="experts_forward",
    )(x, wgu, wd, router, mask, sel)


def experts_backward_kernel(
    x_ref,
    g_ref,
    gu_ref,
    wgu_ref,
    wd_ref,
    router_ref,
    mask_ref,
    sel_ref,
    dx_ref,
    dgu_ref,
    dd_ref,
    dr_ref,
    gates,
    gl,
    gj,
    hs,
    dx_sum,
):
    e = pl.program_id(0)
    tile = 256
    tiles = x_ref.shape[0] // tile
    chosen = jnp.where(e == 0, sel_ref[0:1], sel_ref[1:2])

    @pl.when(e == 0)
    def _():
        @pl.loop(0, tiles)
        def _(i):
            r = pl.ds(pl.multiple_of(i * tile, tile), tile)
            gates[r] = masked_softmax(dot(x_ref[r], router_ref[0]), mask_ref[r])
            gl[r] = jnp.zeros((tile, LANES), F32)

    @pl.loop(0, tiles)
    def _(i):
        r = pl.ds(pl.multiple_of(i * tile, tile), tile)
        gate = jnp.sum(gates[r] * chosen, axis=1, keepdims=True)
        gh = dot_nt(g_ref[r], wd_ref[0, 0])
        part = gu_ref[0, r, :F].astype(F32)
        upper = gu_ref[0, r, F:].astype(F32)
        s = jax.nn.sigmoid(part)
        act = part * s
        hidden = act * upper
        gl[r] += (gate * jnp.sum(hidden * gh, axis=1, keepdims=True)) * chosen
        hs[r] = (hidden * gate).astype(BF16)
        gh = gh * gate
        gj[r, :F] = (gh * upper * (s + act * (1.0 - s))).astype(BF16)
        gj[r, F:] = (gh * act).astype(BF16)
        dx = dot_nt(gj[r], wgu_ref[0, 0])

        @pl.when(e == 0)
        def _():
            dx_sum[r] = dx

        @pl.when(e == 1)
        def _():
            dx_ref[r] = (dx_sum[r] + dx + dot_nt(gl[r].astype(BF16), router_ref[0])).astype(BF16)

    @pl.loop(0, D // 256)
    def _(i):
        c = pl.ds(pl.multiple_of(i * 256, 256), 256)
        dgu_ref[0, c] = dot_tn(x_ref[:, c], gj[...]).astype(BF16)

    @pl.loop(0, F // 256)
    def _(i):
        c = pl.ds(pl.multiple_of(i * 256, 256), 256)
        dd_ref[0, c] = dot_tn(hs[:, c], g_ref[...]).astype(BF16)

    @pl.when(e == 1)
    def _():
        dr_ref[...] = dot_tn(x_ref[...], gl[...].astype(BF16))


def experts_backward(x, g, gu, wgu, wd, router, mask, sel, layer):
    count = x.shape[0]
    return pl.pallas_call(
        experts_backward_kernel,
        grid=(2,),
        out_shape=[
            jax.ShapeDtypeStruct((count, D), BF16),
            jax.ShapeDtypeStruct((2, D, 2 * F), BF16),
            jax.ShapeDtypeStruct((2, F, D), BF16),
            jax.ShapeDtypeStruct((D, LANES), F32),
        ],
        in_specs=[
            whole(count, D),
            whole(count, D),
            pl.BlockSpec((1, count, 2 * F), lambda e: (e, 0, 0)),
            pl.BlockSpec((1, 1, D, 2 * F), lambda e: (layer, e, 0, 0)),
            pl.BlockSpec((1, 1, F, D), lambda e: (layer, e, 0, 0)),
            layer_block((D, LANES), layer),
            whole(count, LANES),
            whole(8, LANES),
        ],
        out_specs=[
            whole(count, D),
            pl.BlockSpec((1, D, 2 * F), lambda e: (e, 0, 0)),
            pl.BlockSpec((1, F, D), lambda e: (e, 0, 0)),
            whole(D, LANES),
        ],
        scratch_shapes=[
            pltpu.VMEM((count, LANES), F32),
            pltpu.VMEM((count, LANES), F32),
            pltpu.VMEM((count, 2 * F), BF16),
            pltpu.VMEM((count, F), BF16),
            pltpu.VMEM((count, D), F32),
        ],
        compiler_params=local_params(),
        name="experts_backward",
    )(x, g, gu, wgu, wd, router, mask, sel)


def inverse_rms(values):
    return lax.rsqrt(jnp.mean(values * values, axis=1, keepdims=True) + EPSILON)


def layer_forward(layer_in, layer, common, weights):
    tables, mask_own, mask_all, sel = common
    wqkv, wo, gains, router, wgu, wd = weights
    unpaired = wgu.shape[0] == 1
    inverse_one = inverse_rms(layer_in)
    normed = (layer_in * inverse_one * gains[layer, 0:1]).astype(BF16)
    rows = fuse([tp_gather_part(normed.reshape(2, 32, D))], 2, "tp_gather")[0].reshape(256, D)
    part, qkv, att = attention_forward(rows, wqkv, wo, tables, layer)
    after = layer_in + fuse([tp_scatter_part(part)], 3, "tp_scatter")[0].reshape(64, D)
    inverse_two = inverse_rms(after)
    normed_two = (after * inverse_two * gains[layer, 1:2]).astype(BF16)
    if unpaired:
        x_all, (wgu, wd) = fuse([exp_gather_part(normed_two), pair_part([wgu, wd])], 1, "gather_pair")
    else:
        (x_all,) = fuse([exp_gather_part(normed_two)], 4, "exp_gather")
    x_all = x_all.reshape(1024, D)
    made, gu = experts_forward(x_all, wgu, wd, router, mask_all, sel, layer)
    (y,) = fuse([exp_scatter_part(made)], 5, "exp_scatter")
    stored = (layer_in, inverse_one, rows, qkv, att, after, inverse_two, normed_two, x_all, gu, y)
    return after + y, stored, (wgu, wd)


def layer_backward(grad, stored, layer, common, weights, pending):
    tables, mask_own, mask_all, sel = common
    wqkv, wo, gains, router, wgu, wd = weights
    layer_in, inverse_one, rows, qkv, att, after, inverse_two, normed_two, x_all, gu, y = stored
    done = []
    if layer == 1:
        (g_all,) = fuse([exp_gather_part(grad)], 4, "exp_gather")
    else:
        g_all, more = fuse([exp_gather_part(grad), expert_part(*pending[0])], 7, "gather_expert")
        done.append(more)
    g_all = g_all.reshape(1024, D)
    dx, dgu, dd, dr = experts_backward(x_all, g_all, gu, wgu, wd, router, mask_all, sel, layer)
    pending = [(dgu, 0), (dgu, 512), (dd, 0)]
    gates = masked_softmax(dot(normed_two, router[layer]), mask_own)
    gf = grad.astype(F32)
    gc = (gates * jnp.sum(gf * y, axis=1, keepdims=True)).astype(BF16)
    count = 2 if layer == 1 else 1
    results = fuse(
        [exp_scatter_part(dx)] + [expert_part(*piece) for piece in pending[:count]],
        8 + layer,
        "scatter_expert",
    )
    done += results[1:]
    pending = pending[count:]
    grad_n = results[0] - dot_nt(gc, router[layer])
    dr = dr - dot_tn(normed_two, gc)
    scaled = grad_n * gains[layer, 1:2]
    grad_after = (
        gf
        + inverse_two * scaled
        - after * inverse_two**3 * jnp.mean(after * scaled, axis=1, keepdims=True)
    )
    d_mixture = jnp.sum(grad_n * after * inverse_two, axis=0)
    ga = grad_after.astype(BF16).reshape(2, 32, D)
    ga = fuse([tp_gather_part(ga)], 2, "tp_gather")[0].reshape(256, D)
    dn, dw = attention_backward(rows, ga, qkv, att, wqkv, wo, tables, layer)
    grad_n = fuse([tp_scatter_part(dn)], 3, "tp_scatter")[0].reshape(64, D)
    scaled = grad_n * gains[layer, 0:1]
    grad_in = (
        grad_after
        + inverse_one * scaled
        - layer_in * inverse_one**3 * jnp.mean(layer_in * scaled, axis=1, keepdims=True)
    )
    d_attention = jnp.sum(grad_n * layer_in * inverse_one, axis=0)
    lane = jnp.arange(LANES)[None, :]
    small = jnp.where(lane == E, d_attention[:, None], jnp.where(lane == E + 1, d_mixture[:, None], dr))
    wide = jnp.concatenate([dw, small.astype(BF16)], axis=1)
    return grad_in, wide, done, pending


def rope_tables(seg_rows):
    length = seg_rows.shape[0]
    before = jnp.sum((seg_rows[None, :] < seg_rows[:, None]).astype(jnp.int32), axis=1)
    places = (jnp.arange(length, dtype=jnp.int32) - before).astype(F32)
    powers = jnp.arange(0, HD, 2, dtype=jnp.int32).astype(F32) / HD
    angles = places[:, None] * (ROPE_BASE ** (-powers))[None, :]
    cosine, sine = jnp.cos(angles), jnp.sin(angles)
    indices = jnp.arange(length, dtype=jnp.int32)
    allowed = (seg_rows[:, None] == seg_rows[None, :]) & (indices[None, :] <= indices[:, None])
    return (
        jnp.concatenate([cosine] * 4, axis=1),
        jnp.concatenate([-sine, sine, -sine, sine], axis=1),
        allowed.astype(F32),
    )


def routed(routes):
    labels = jnp.arange(LANES, dtype=jnp.int32)
    return jnp.sum((routes[:, :, None] == labels[None, None, :]).astype(F32), axis=1)


def per_device(
    activations,
    cotangent,
    segments,
    routes,
    attention_gain,
    query_weight,
    key_weight,
    value_weight,
    output_weight,
    mixture_gain,
    router_weight,
    expert_gate_up,
    expert_down,
):
    section = lax.axis_index("section")
    expert = lax.axis_index("exp")

    def own_batches(array):
        return lax.dynamic_slice_in_dim(array, 2 * section, 2, 0)

    def to_owner(first, second):
        sent = jnp.where(section == 0, second, first)
        kept = jnp.where(section == 0, first, second)
        return kept, lax.ppermute(sent, "section", [(0, 1), (1, 0)])

    def by_layer(first, second):
        kept, got = to_owner(first, second)
        kept, got = kept.reshape(2, 32, D), got.reshape(2, 32, D)
        return jnp.where(
            section == 0,
            jnp.concatenate([kept, got], axis=0),
            jnp.concatenate([got, kept], axis=0),
        )[None]

    qkv_own = jnp.concatenate([query_weight, key_weight, value_weight], axis=2)
    gains_own = jnp.concatenate(
        [attention_gain, mixture_gain, jnp.zeros((6, D), BF16)], axis=0
    ).astype(F32)[None]
    router_own = jnp.pad(router_weight, ((0, 0), (0, 0), (0, LANES - E)))
    (paired,) = fuse([pair_part([qkv_own, output_weight, gains_own, router_own])], 0, "pair")
    weights = tuple(paired) + (expert_gate_up, expert_down)

    cosine, sine, mask = jax.vmap(rope_tables)(own_batches(segments))
    tables = (cosine.reshape(256, LANES), sine.reshape(256, LANES), mask)
    routes_own = own_batches(routes).reshape(64, 8)
    routes_all = lax.all_gather(routes_own, "exp", axis=0, tiled=True)
    lanes = lax.broadcasted_iota(jnp.int32, (8, LANES), 1)
    sel = (lanes == 2 * expert + lax.broadcasted_iota(jnp.int32, (8, LANES), 0)).astype(F32)
    common = (tables, routed(routes_own), routed(routes_all), sel)

    start = own_batches(activations).reshape(64, D).astype(F32)
    result, kept_first, experts = layer_forward(start, 0, common, weights)
    weights = tuple(paired) + tuple(experts)
    out_first = result.astype(BF16)
    result, kept_second, _ = layer_forward(out_first.astype(F32), 1, common, weights)
    out_second = result.astype(BF16)
    grad = own_batches(cotangent).reshape(64, D)
    grad_second, wide_second, done_second, pending = layer_backward(
        grad, kept_second, 1, common, weights, []
    )
    grad_first, wide_first, done_first, pending = layer_backward(
        grad_second.astype(BF16), kept_first, 0, common, weights, pending
    )
    done_second.append(done_first.pop(0))
    (dw, small), *rest = fuse(
        [settle_part(wide_first, wide_second)] + [expert_part(*piece) for piece in pending],
        6,
        "settle",
    )
    done_first += rest
    small = small.reshape(D, LANES)
    experts = []
    for first, second in zip(done_first, done_second):
        kept, got = to_owner(first, second)
        kept, got = kept.astype(F32), got.astype(F32)
        experts.append(
            jnp.where(section == 0, jnp.stack([kept, got]), jnp.stack([got, kept]))[None]
        )
    return (
        by_layer(out_first, out_second),
        by_layer(grad_first, grad_second),
        small[:, E][None],
        dw[None, :, :256],
        dw[None, :, 256:384],
        dw[None, :, 384:512],
        dw[:, 512:].T[None],
        small[:, E + 1][None],
        small[None, :, :E],
        jnp.concatenate(experts[:2], axis=2),
        experts[2],
    )


def solution(mesh):
    placed = (
        P(None, ("exp", "tp"), None),
        P(None, ("exp", "tp"), None),
        P(None, "exp"),
        P(None, ("exp", "tp"), None),
        P("section", None),
        P("section", None, "tp"),
        P("section", None, "tp"),
        P("section", None, "tp"),
        P("section", "tp", None),
        P("section", None),
        P("section", None, None),
        P("section", "exp", None, None),
        P("section", "exp", None, None),
    )
    return jax.shard_map(
        per_device,
        mesh=mesh,
        in_specs=placed,
        out_specs=(
            P("section", None, ("exp", "tp"), None),
            P("section", None, ("exp", "tp"), None),
            P("section", None),
            P("section", "exp", "tp"),
            P("section", "exp", "tp"),
            P("section", "exp", "tp"),
            P("section", "tp", "exp"),
            P("section", None),
            P("section", None, None),
            P("section", "exp", None, "tp"),
            P("section", "exp", None, "tp"),
        ),
        check_vma=False,
    )
```

```python
import functools

import jax
import jax.numpy as jnp
from jax import lax
from jax.experimental import pallas as pl
from jax.experimental.pallas import tpu as pltpu
from jax.sharding import PartitionSpec as P

D = 1024
HD = 64
E = 32
F = 512
LANES = 128
EPSILON = 1e-06
ROPE_BASE = 10000.0
SCORE_SCALE = 0.125
MASKED = -1e30
MESH = pl.DeviceIdType.MESH
VMEM_LIMIT = 56 * 1024 * 1024
BF16 = jnp.bfloat16
F32 = jnp.float32


def dot(a, b):
    return jnp.dot(a, b, preferred_element_type=F32)


def dot_nt(a, b):
    return lax.dot_general(a, b, (((1,), (1,)), ((), ())), preferred_element_type=F32)


def dot_tn(a, b):
    return lax.dot_general(a, b, (((0,), (0,)), ((), ())), preferred_element_type=F32)


def in_vmem():
    return pl.BlockSpec(memory_space=pltpu.VMEM)


def in_any():
    return pl.BlockSpec(memory_space=pl.ANY)


def greet(peers):
    barrier = pltpu.get_barrier_semaphore()
    for peer in peers:
        pl.semaphore_signal(barrier, inc=1, device_id=peer, device_id_type=MESH)
    pl.semaphore_wait(barrier, len(peers))


def remote(src, dst, send_sem, recv_sem, peer):
    return pltpu.make_async_remote_copy(
        src_ref=src,
        dst_ref=dst,
        send_sem=send_sem,
        recv_sem=recv_sem,
        device_id=peer,
        device_id_type=MESH,
    )


def comm_params(number):
    return pltpu.CompilerParams(
        collective_id=number, has_side_effects=True, vmem_limit_bytes=VMEM_LIMIT
    )


class Part:
    def __init__(self, arrays, in_specs, out_shapes, out_specs, scratch, axes, body):
        self.arrays, self.in_specs = arrays, in_specs
        self.out_shapes, self.out_specs = out_shapes, out_specs
        self.scratch, self.axes, self.body = scratch, axes, body


def around(axis):
    if axis == "section":
        return [{"section": 1 - lax.axis_index("section")}]
    if axis == "tp":
        me = lax.axis_index("tp")
        return [{"tp": lax.rem(me + j, 4)} for j in (3, 1)]
    if axis == "tp_opposite":
        return [{"tp": lax.rem(lax.axis_index("tp") + 2, 4)}]
    me = lax.axis_index("exp")
    at_x, at_z = me // 4, lax.rem(me, 4)
    if axis == "x":
        return [{"exp": lax.rem(at_x + j, 4) * 4 + at_z} for j in (3, 1)]
    return [{"exp": at_x * 4 + lax.rem(at_z + j, 4)} for j in (3, 1)]


def fused_kernel(parts, *refs):
    refs = list(refs)

    def take(count):
        taken = refs[:count]
        del refs[:count]
        return taken

    ins = [take(len(part.arrays)) for part in parts]
    outs = [take(len(part.out_shapes)) for part in parts]
    scratch = [take(len(part.scratch)) for part in parts]
    axes = []
    for part in parts:
        axes += [axis for axis in part.axes if axis not in axes]
    greet([peer for axis in axes for peer in around(axis)])
    running = [part.body(i, o, s) for part, i, o, s in zip(parts, ins, outs, scratch)]
    while running:
        for one in list(running):
            if next(one, "end") == "end":
                running.remove(one)


def fuse(parts, number, name):
    outs = pl.pallas_call(
        functools.partial(fused_kernel, parts),
        out_shape=[o for part in parts for o in part.out_shapes],
        in_specs=[s for part in parts for s in part.in_specs],
        out_specs=[s for part in parts for s in part.out_specs],
        scratch_shapes=[s for part in parts for s in part.scratch],
        compiler_params=comm_params(number),
        name=name,
    )(*[a for part in parts for a in part.arrays])
    outs = list(outs)
    results = []
    for part in parts:
        count = len(part.out_shapes)
        results.append(outs[:count] if count > 1 else outs[0])
        outs = outs[count:]
    return results


def sems(*shape):
    return [pltpu.SemaphoreType.DMA(shape)] * 2


def pair_part(arrays):
    count = len(arrays)

    def body(ins, outs, scratch):
        held, (send, recv, read, write) = scratch[:count], scratch[count:]
        me = lax.axis_index("section")
        (peer,) = around("section")
        sends, reads, writes = [], [], []
        for at in range(count):
            sends.append(remote(ins[at].at[0], outs[at].at[me], send.at[at], recv.at[at], peer))
            reads.append(pltpu.make_async_copy(ins[at].at[0], held[at], read.at[at]))
            writes.append(pltpu.make_async_copy(held[at], outs[at].at[me], write.at[at]))
            sends[-1].start()
            reads[-1].start()
        yield
        for at in range(count):
            reads[at].wait()
            writes[at].start()
        yield
        yield
        yield
        for at in range(count):
            writes[at].wait()
            sends[at].wait()

    return Part(
        arrays,
        [in_any()] * count,
        [jax.ShapeDtypeStruct((2,) + a.shape[1:], a.dtype) for a in arrays],
        [in_any()] * count,
        [pltpu.VMEM(a.shape[1:], a.dtype) for a in arrays]
        + [pltpu.SemaphoreType.DMA((count,))] * 4,
        ["section"],
        body,
    )


class RingGather:
    def __init__(self, view, own, left, right, send, recv):
        self.view, self.own = view, own
        self.left, self.right, self.send, self.recv = left, right, send, recv
        self.copies = []

    def go(self, src, dst, at, peer):
        copy = remote(src, dst, self.send[at], self.recv[at], peer)
        copy.start()
        self.copies.append(copy)

    def start(self):
        own = self.view(0, None) if self.own is None else self.own
        self.go(own, self.view(0, None), 0, self.right)
        self.go(own, self.view(0, None), 1, self.left)

    def forward(self):
        self.copies[0].wait_recv()
        self.go(self.view(3, 0), self.view(3, 0), 2, self.right)
        self.copies[1].wait_recv()
        self.go(self.view(1, 1), self.view(1, 1), 3, self.left)

    def finish(self):
        self.copies[2].wait_recv()
        self.copies[3].wait_recv()

    def drain(self):
        for copy in self.copies:
            copy.wait_send()


class RingScatter:
    def __init__(self, view, temp, block, stage, left, right, send, recv):
        self.view, self.temp, self.block, self.stage = view, temp, block, stage
        self.left, self.right, self.send, self.recv = left, right, send, recv
        self.copies = []

    def go(self, src, dst, at, peer):
        copy = remote(src, dst, self.send[at], self.recv[at], peer)
        copy.start()
        self.copies.append(copy)

    def start(self):
        self.go(self.view(2, 0), self.temp(0), 0, self.right)
        self.go(self.view(2, 1), self.temp(1), 1, self.left)
        self.go(self.view(1, 1), self.block(0, 1), 2, self.right)
        self.go(self.view(3, 0), self.block(1, 0), 3, self.left)

    def middle(self):
        for side, nearer, peer in ((0, 1, self.right), (1, 3, self.left)):
            self.copies[side].wait_recv()
            term = self.view(nearer, side)[...].astype(F32) + self.temp(side)[...].astype(F32)
            self.stage(side)[...] = term.astype(BF16)
            self.go(self.stage(side), self.block(side, side), 4 + side, peer)

    def finish(self):
        for copy in self.copies[2:]:
            copy.wait_recv()

    def total(self, part):
        return (
            self.view(0, part)[...].astype(F32)
            + self.block(0, part)[...].astype(F32)
            + self.block(1, part)[...].astype(F32)
        )

    def drain(self):
        for copy in self.copies:
            copy.wait_send()


def tp_block(ref, k, part):
    place = lax.rem(lax.axis_index("tp") + k, 4)
    rows = pl.ds(pl.multiple_of(place * 32, 32), 32)
    return ref.at[:, rows] if part is None else ref.at[part, rows]


def tp_gather_part(x):
    def body(ins, outs, scratch):
        (x_ref,), (out_ref,), (send, recv) = ins, outs, scratch
        left, right = around("tp")
        ring = RingGather(
            functools.partial(tp_block, out_ref),
            x_ref,
            left,
            right,
            [send.at[i] for i in range(4)],
            [recv.at[i] for i in range(4)],
        )
        ring.start()
        tp_block(out_ref, 0, None)[...] = x_ref[...]
        yield
        ring.forward()
        yield
        ring.finish()
        ring.drain()

    return Part(
        [x],
        [in_vmem()],
        [jax.ShapeDtypeStruct((2, 128, D), BF16)],
        [in_vmem()],
        sems(4),
        ["tp"],
        body,
    )


def tp_scatter_part(x):
    def body(ins, outs, scratch):
        (x_ref,), (out_ref,), (temp, block, stage, send, recv) = ins, outs, scratch
        left, right = around("tp")
        ring = RingScatter(
            functools.partial(tp_block, x_ref),
            lambda side: temp.at[side],
            lambda side, part: block.at[side, part],
            lambda side: stage.at[side],
            left,
            right,
            [send.at[i] for i in range(6)],
            [recv.at[i] for i in range(6)],
        )
        ring.start()
        yield
        ring.middle()
        yield
        ring.finish()
        out_ref[0] = ring.total(0)
        out_ref[1] = ring.total(1)
        ring.drain()

    return Part(
        [x],
        [in_vmem()],
        [jax.ShapeDtypeStruct((2, 32, D), F32)],
        [in_vmem()],
        [
            pltpu.VMEM((2, 32, D), BF16),
            pltpu.VMEM((2, 2, 32, D), BF16),
            pltpu.VMEM((2, 32, D), BF16),
        ]
        + sems(6),
        ["tp"],
        body,
    )


def exp_block(ref, half, i, j, part):
    me = lax.axis_index("exp")
    at_x, at_z = me // 4, lax.rem(me, 4)
    i, j = (i, j) if half == 0 else (j, i)
    rows = pl.ds(32 * half, 32) if part is None else pl.ds(32 * half + 16 * part, 16)
    return ref.at[lax.rem(at_x + i, 4), lax.rem(at_z + j, 4), rows]


def exp_gather_steps(x_ref, out_ref, send, recv):
    sides = [around("x"), around("z")]
    first, second = [], []
    for half in range(2):

        def ring(view, own, at, axis, half=half):
            return RingGather(
                view,
                own,
                sides[axis][0],
                sides[axis][1],
                [send.at[half, at, n] for n in range(4)],
                [recv.at[half, at, n] for n in range(4)],
            )

        def along(k, part, half=half):
            return exp_block(out_ref, half, k, 0, part)

        own = x_ref.at[pl.ds(32 * half, 32)]
        first.append(ring(along, own, 4, half))
        second.append([])
        for i in range(4):

            def across(k, part, half=half, i=i):
                return exp_block(out_ref, half, i, k, part)

            second[half].append(ring(across, own if i == 0 else None, i, 1 - half))
    for half in range(2):
        first[half].start()
    for half in range(2):
        second[half][0].start()
        exp_block(out_ref, half, 0, 0, None)[...] = x_ref[pl.ds(32 * half, 32)]
    yield
    for half in range(2):
        first[half].forward()
        second[half][3].start()
        second[half][1].start()
    yield
    for half in range(2):
        second[half][0].forward()
    yield
    for half in range(2):
        first[half].finish()
        second[half][2].start()
    yield
    for i in (3, 1):
        for half in range(2):
            second[half][i].forward()
    yield
    for half in range(2):
        second[half][2].forward()
    yield
    for half in range(2):
        for ring in second[half]:
            ring.finish()
        for ring in second[half] + [first[half]]:
            ring.drain()


def exp_gather_part(x):
    def body(ins, outs, scratch):
        yield from exp_gather_steps(ins[0], outs[0], *scratch)

    return Part(
        [x],
        [in_vmem()],
        [jax.ShapeDtypeStruct((4, 4, 64, x.shape[1]), x.dtype)],
        [in_vmem()],
        sems(2, 5, 4),
        ["x", "z"],
        body,
    )


def exp_scatter_steps(x_ref, out_ref, temp, block, stage, ready, send, recv):
    sides = [around("x"), around("z")]
    first, second = [], []
    for half in range(2):

        def ring(view, at, axis, half=half):
            return RingScatter(
                view,
                lambda side: temp.at[half, at, side],
                lambda side, part: block.at[half, at, side, pl.ds(16 * part, 16)],
                lambda side: stage.at[half, at, side],
                sides[axis][0],
                sides[axis][1],
                [send.at[half, at, n] for n in range(6)],
                [recv.at[half, at, n] for n in range(6)],
            )

        first.append([])
        for j in range(4):

            def along(k, part, half=half, j=j):
                return exp_block(x_ref, half, k, j, part)

            first[half].append(ring(along, j, half))

        def across(k, part, half=half):
            return ready.at[half, k, pl.ds(16 * part, 16)]

        second.append(ring(across, 4, 1 - half))
    order = (2, 1, 3, 0)
    for j in order:
        for half in range(2):
            first[half][j].start()
    yield
    for j in order:
        for half in range(2):
            first[half][j].middle()
        yield
    for j in order:
        for half in range(2):
            first[half][j].finish()
            for part in range(2):
                ready[half, j, pl.ds(16 * part, 16)] = first[half][j].total(part).astype(BF16)
            if j == 3:
                second[half].start()
    yield
    for half in range(2):
        second[half].middle()
    yield
    for half in range(2):
        second[half].finish()
        for part in range(2):
            out_ref[pl.ds(32 * half + 16 * part, 16)] = second[half].total(part)
    for half in range(2):
        for ring in first[half] + [second[half]]:
            ring.drain()


def exp_scatter_scratch(width):
    return [
        pltpu.VMEM((2, 5, 2, 16, width), BF16),
        pltpu.VMEM((2, 5, 2, 32, width), BF16),
        pltpu.VMEM((2, 5, 2, 16, width), BF16),
        pltpu.VMEM((2, 4, 32, width), BF16),
    ] + sems(2, 5, 6)


def exp_scatter_part(x):
    width = x.shape[-1]

    def body(ins, outs, scratch):
        yield from exp_scatter_steps(ins[0], outs[0], *scratch)

    return Part(
        [x.reshape(4, 4, 64, width)],
        [in_vmem()],
        [jax.ShapeDtypeStruct((64, width), F32)],
        [in_vmem()],
        exp_scatter_scratch(width),
        ["x", "z"],
        body,
    )


def expert_part(grads, first_row):
    rows = pl.ds(first_row, 512)

    def body(ins, outs, scratch):
        (g_ref,), (out_ref,) = ins, outs
        own, got, temp, block, stage, send, recv, read, swap_send, swap_recv = scratch
        me = lax.axis_index("section")
        place = lax.axis_index("tp")
        left, right = around("tp")
        (peer,) = around("section")
        swap = remote(g_ref.at[1 - me, rows], got, swap_send.at[0], swap_recv.at[0], peer)
        swap.start()
        kept = pltpu.make_async_copy(g_ref.at[me, rows], own, read.at[0])
        kept.start()
        yield
        kept.wait()
        swap.wait_recv()

        @pl.loop(0, 8)
        def _(i):
            r = pl.ds(pl.multiple_of(i * 64, 64), 64)
            own[r] = (own[r].astype(F32) + got[r].astype(F32)).astype(BF16)

        def view(k, part):
            columns = pl.multiple_of(lax.rem(place + k, 4) * 256, 256)
            return own.at[pl.ds(256 * part, 256), pl.ds(columns, 256)]

        ring = RingScatter(
            view,
            lambda side: temp.at[side],
            lambda side, part: block.at[side, part],
            lambda side: stage.at[side],
            left,
            right,
            [send.at[i] for i in range(6)],
            [recv.at[i] for i in range(6)],
        )
        ring.start()
        yield
        yield
        yield
        ring.middle()
        yield
        yield
        yield
        ring.finish()
        out_ref[:256] = ring.total(0).astype(BF16)
        out_ref[256:] = ring.total(1).astype(BF16)
        ring.drain()
        swap.wait_send()

    return Part(
        [grads],
        [in_any()],
        [jax.ShapeDtypeStruct((512, 256), BF16)],
        [in_vmem()],
        [
            pltpu.VMEM((512, D), BF16),
            pltpu.VMEM((512, D), BF16),
            pltpu.VMEM((2, 256, 256), BF16),
            pltpu.VMEM((2, 2, 256, 256), BF16),
            pltpu.VMEM((2, 256, 256), BF16),
        ]
        + sems(6)
        + [pltpu.SemaphoreType.DMA((1,))] * 3,
        ["section", "tp"],
        body,
    )


WIDE = 896


def settle_part(first, second):
    def body(ins, outs, scratch):
        first_ref, second_ref = ins
        out_ref, small_ref = outs
        got, x_ref, total, piece, held = scratch[:5]
        scatter, rest = scratch[5:11], scratch[11:]
        swap_send, swap_recv, tp_send, tp_recv, gather_send, gather_recv = rest
        me = lax.axis_index("section")
        (peer,) = around("section")
        copies = [
            remote(ref, got, swap_send.at[0], swap_recv.at[0], peer)
            for ref in (second_ref, first_ref)
        ]
        for layer in range(2):

            @pl.when(me == layer)
            def _():
                copies[layer].start()

        yield
        copies[0].wait_recv()
        for at_x in range(4):
            for at_z in range(4):
                mine = jnp.where(me == 0, first_ref[at_x, at_z], second_ref[at_x, at_z])
                summed = mine.astype(F32) + got[at_x, at_z].astype(F32)
                x_ref[at_x, at_z] = summed.astype(BF16)
        yield from exp_scatter_steps(x_ref, total, *scatter)
        out_ref[...] = total[:, :768]
        piece[...] = total[:, 768:]
        partners = around("tp") + around("tp_opposite")
        sent = [
            remote(piece, held.at[at], tp_send.at[at], tp_recv.at[at], partner)
            for at, partner in enumerate(partners)
        ]
        for copy in sent:
            copy.start()
        yield
        for copy in sent:
            copy.wait()
        piece[...] = piece[...] + ((held[0] + held[1]) + held[2])
        yield from exp_gather_steps(piece, small_ref, gather_send, gather_recv)
        copies[0].wait_send()

    return Part(
        [first.reshape(4, 4, 64, WIDE), second.reshape(4, 4, 64, WIDE)],
        [in_vmem()] * 2,
        [
            jax.ShapeDtypeStruct((64, 768), F32),
            jax.ShapeDtypeStruct((4, 4, 64, LANES), F32),
        ],
        [in_vmem()] * 2,
        [
            pltpu.VMEM((4, 4, 64, WIDE), BF16),
            pltpu.VMEM((4, 4, 64, WIDE), BF16),
            pltpu.VMEM((64, WIDE), F32),
            pltpu.VMEM((64, LANES), F32),
            pltpu.VMEM((3, 64, LANES), F32),
        ]
        + exp_scatter_scratch(WIDE)
        + [pltpu.SemaphoreType.DMA((1,))] * 2
        + sems(3)
        + sems(2, 5, 4),
        ["section", "x", "z", "tp", "tp_opposite"],
        body,
    )


def half_swapped(values):
    width = values.shape[1]
    lane = lax.broadcasted_iota(jnp.int32, values.shape, 1)
    ahead = pltpu.roll(values, width - 32, 1)
    behind = pltpu.roll(values, 32, 1)
    return jnp.where(lax.rem(lane, 64) < 32, ahead, behind)


def three(table):
    return jnp.concatenate([table, table, table], axis=1)


def head(values, batch, first):
    return values[batch * 128 : batch * 128 + 128, first : first + HD]


def layer_block(shape, layer):
    return pl.BlockSpec((1,) + shape, lambda i: (layer,) + (0,) * len(shape))


def whole(*shape):
    return pl.BlockSpec(shape, lambda i: (0,) * len(shape))


def local_params():
    return pltpu.CompilerParams(vmem_limit_bytes=VMEM_LIMIT)


def attention_backward_kernel(
    rows_ref,
    ga_ref,
    qkv_ref,
    att_ref,
    wqkv_ref,
    wo_ref,
    cos_ref,
    sin_ref,
    mask_ref,
    dn_ref,
    dw_ref,
):
    ga = ga_ref[...]
    rows = rows_ref[...]
    dw_ref[:, 512:] = dot_tn(ga, att_ref[...]).astype(BF16)
    gatt = dot_nt(ga, wo_ref[0]).astype(BF16)
    qkv = qkv_ref[...]
    by_batch = []
    for batch in range(2):
        allowed = mask_ref[batch] > 0.5
        gqs, gks, gvs = [], [None, None], [None, None]
        for h in range(4):
            kv = h // 2
            q = head(qkv, batch, h * HD)
            k = head(qkv, batch, 256 + kv * HD)
            v = head(qkv, batch, 384 + kv * HD)
            go = head(gatt, batch, h * HD)
            scores = jnp.where(allowed, dot_nt(q, k) * SCORE_SCALE, MASKED)
            lifted = jnp.exp(scores - jnp.max(scores, axis=1, keepdims=True))
            share = lifted / jnp.sum(lifted, axis=1, keepdims=True)
            gp = dot_nt(go, v)
            gs = share * (gp - jnp.sum(share * gp, axis=1, keepdims=True))
            gs = gs.astype(BF16)
            gqs.append(dot(gs, k) * SCORE_SCALE)
            gk = dot_tn(gs, q) * SCORE_SCALE
            gv = dot_tn(share.astype(BF16), go)
            gks[kv] = gk if gks[kv] is None else gks[kv] + gk
            gvs[kv] = gv if gvs[kv] is None else gvs[kv] + gv
        by_batch.append(jnp.concatenate(gqs + gks + gvs, axis=1))
    joined = jnp.concatenate(by_batch, axis=0)
    turned = joined[:, :384]
    turned = turned * three(cos_ref[...]) - half_swapped(turned) * three(sin_ref[...])
    gqkv = jnp.concatenate([turned, joined[:, 384:]], axis=1).astype(BF16)
    dw_ref[:, :512] = dot_tn(rows, gqkv).astype(BF16)
    dn = dot_nt(gqkv, wqkv_ref[0]).astype(BF16)
    dn_ref[0] = dn[:128]
    dn_ref[1] = dn[128:]


def attention_backward(rows, ga, qkv, att, wqkv, wo, tables, layer):
    cosine, sine, mask = tables
    return pl.pallas_call(
        attention_backward_kernel,
        grid=(1,),
        out_shape=[
            jax.ShapeDtypeStruct((2, 128, D), BF16),
            jax.ShapeDtypeStruct((D, 768), BF16),
        ],
        in_specs=[
            whole(256, D),
            whole(256, D),
            whole(256, 512),
            whole(256, 256),
            layer_block((D, 512), layer),
            layer_block((256, D), layer),
            whole(256, LANES),
            whole(256, LANES),
            whole(2, 128, 128),
        ],
        out_specs=[whole(2, 128, D), whole(D, 768)],
        compiler_params=local_params(),
        name="attention_backward",
    )(rows, ga, qkv, att, wqkv, wo, cosine, sine, mask)


def masked_softmax(logits, mask):
    routed = mask > 0.5
    shown = jnp.where(routed, logits, MASKED)
    lifted = jnp.where(routed, jnp.exp(shown - jnp.max(shown, axis=1, keepdims=True)), 0.0)
    return lifted / jnp.sum(lifted, axis=1, keepdims=True)


def experts_backward_kernel(
    x_ref,
    g_ref,
    gu_ref,
    wgu_ref,
    wd_ref,
    router_ref,
    mask_ref,
    sel_ref,
    dx_ref,
    dgu_ref,
    dd_ref,
    dr_ref,
    gates,
    gl,
    gj,
    hs,
    dx_sum,
):
    e = pl.program_id(0)
    tile = 256
    tiles = x_ref.shape[0] // tile
    chosen = jnp.where(e == 0, sel_ref[0:1], sel_ref[1:2])

    @pl.when(e == 0)
    def _():
        @pl.loop(0, tiles)
        def _(i):
            r = pl.ds(pl.multiple_of(i * tile, tile), tile)
            gates[r] = masked_softmax(dot(x_ref[r], router_ref[0]), mask_ref[r])
            gl[r] = jnp.zeros((tile, LANES), F32)

    @pl.loop(0, tiles)
    def _(i):
        r = pl.ds(pl.multiple_of(i * tile, tile), tile)
        gate = jnp.sum(gates[r] * chosen, axis=1, keepdims=True)
        gh = dot_nt(g_ref[r], wd_ref[0, 0])
        part = gu_ref[0, r, :F].astype(F32)
        upper = gu_ref[0, r, F:].astype(F32)
        s = jax.nn.sigmoid(part)
        act = part * s
        hidden = act * upper
        gl[r] += (gate * jnp.sum(hidden * gh, axis=1, keepdims=True)) * chosen
        hs[r] = (hidden * gate).astype(BF16)
        gh = gh * gate
        gj[r, :F] = (gh * upper * (s + act * (1.0 - s))).astype(BF16)
        gj[r, F:] = (gh * act).astype(BF16)
        dx = dot_nt(gj[r], wgu_ref[0, 0])

        @pl.when(e == 0)
        def _():
            dx_sum[r] = dx

        @pl.when(e == 1)
        def _():
            dx_ref[r] = (dx_sum[r] + dx + dot_nt(gl[r].astype(BF16), router_ref[0])).astype(BF16)

    @pl.loop(0, D // 256)
    def _(i):
        c = pl.ds(pl.multiple_of(i * 256, 256), 256)
        dgu_ref[0, c] = dot_tn(x_ref[:, c], gj[...]).astype(BF16)

    @pl.loop(0, F // 256)
    def _(i):
        c = pl.ds(pl.multiple_of(i * 256, 256), 256)
        dd_ref[0, c] = dot_tn(hs[:, c], g_ref[...]).astype(BF16)

    @pl.when(e == 1)
    def _():
        dr_ref[...] = dot_tn(x_ref[...], gl[...].astype(BF16))


def experts_backward(x, g, gu, wgu, wd, router, mask, sel, layer):
    count = x.shape[0]
    return pl.pallas_call(
        experts_backward_kernel,
        grid=(2,),
        out_shape=[
            jax.ShapeDtypeStruct((count, D), BF16),
            jax.ShapeDtypeStruct((2, D, 2 * F), BF16),
            jax.ShapeDtypeStruct((2, F, D), BF16),
            jax.ShapeDtypeStruct((D, LANES), F32),
        ],
        in_specs=[
            whole(count, D),
            whole(count, D),
            pl.BlockSpec((1, count, 2 * F), lambda e: (e, 0, 0)),
            pl.BlockSpec((1, 1, D, 2 * F), lambda e: (layer, e, 0, 0)),
            pl.BlockSpec((1, 1, F, D), lambda e: (layer, e, 0, 0)),
            layer_block((D, LANES), layer),
            whole(count, LANES),
            whole(8, LANES),
        ],
        out_specs=[
            whole(count, D),
            pl.BlockSpec((1, D, 2 * F), lambda e: (e, 0, 0)),
            pl.BlockSpec((1, F, D), lambda e: (e, 0, 0)),
            whole(D, LANES),
        ],
        scratch_shapes=[
            pltpu.VMEM((count, LANES), F32),
            pltpu.VMEM((count, LANES), F32),
            pltpu.VMEM((count, 2 * F), BF16),
            pltpu.VMEM((count, F), BF16),
            pltpu.VMEM((count, D), F32),
        ],
        compiler_params=local_params(),
        name="experts_backward",
    )(x, g, gu, wgu, wd, router, mask, sel)


def inverse_rms(values):
    return lax.rsqrt(jnp.mean(values * values, axis=1, keepdims=True) + EPSILON)


class Names:
    pass


def take_turns(running):
    running = list(running)
    while running:
        for one in list(running):
            if next(one, "end") == "end":
                running.remove(one)


def one_kernel(name, number, axes, ins, outs, scratch, chains):
    names = list(ins) + list(outs) + list(scratch)

    def kernel(*refs):
        at = Names()
        for key, ref in zip(names, refs):
            setattr(at, key, ref)
        greet([peer for axis in axes for peer in around(axis)])
        take_turns(chains(at))

    results = pl.pallas_call(
        kernel,
        out_shape=[jax.ShapeDtypeStruct(o[0], o[1]) for o in outs.values()],
        in_specs=[i[1] for i in ins.values()],
        out_specs=[o[2] for o in outs.values()],
        scratch_shapes=list(scratch.values()),
        compiler_params=comm_params(number),
        name=name,
    )(*[i[0] for i in ins.values()])
    made = Names()
    for key, result in zip(outs, results):
        setattr(made, key, result)
    return made


def chain_tp_block(ref, c, k, part):
    place = lax.rem(lax.axis_index("tp") + k, 4)
    if part is None:
        return ref.at[c, pl.ds(pl.multiple_of(place * 32, 32), 32)]
    return ref.at[c, pl.ds(pl.multiple_of(place * 32 + 16 * part, 16), 16)]


def chain_tp_gather(own, ref, c, send, recv):
    left, right = around("tp")
    ring = RingGather(
        lambda k, part: chain_tp_block(ref, c, k, part),
        own,
        left,
        right,
        [send.at[c, i] for i in range(4)],
        [recv.at[c, i] for i in range(4)],
    )
    ring.start()
    chain_tp_block(ref, c, 0, None)[...] = own[...]
    yield
    ring.forward()
    yield
    ring.finish()
    ring.drain()


def chain_tp_scatter(ref, c, temp, block, stage, send, recv, out):
    left, right = around("tp")
    ring = RingScatter(
        lambda k, part: chain_tp_block(ref, c, k, part),
        lambda side: temp.at[c, side],
        lambda side, part: block.at[c, side, part],
        lambda side: stage.at[c, side],
        left,
        right,
        [send.at[c, i] for i in range(6)],
        [recv.at[c, i] for i in range(6)],
    )
    ring.start()
    yield
    ring.middle()
    yield
    ring.finish()
    for part in range(2):
        out[c, pl.ds(16 * part, 16)] = ring.total(part)
    ring.drain()


TP_SCRATCH = dict(
    tp_temp=pltpu.VMEM((2, 2, 16, D), BF16),
    tp_block=pltpu.VMEM((2, 2, 2, 16, D), BF16),
    tp_stage=pltpu.VMEM((2, 2, 16, D), BF16),
    tp_sum=pltpu.VMEM((2, 32, D), F32),
    tp_send=pltpu.SemaphoreType.DMA((2, 6)),
    tp_recv=pltpu.SemaphoreType.DMA((2, 6)),
    tg_send=pltpu.SemaphoreType.DMA((2, 4)),
    tg_recv=pltpu.SemaphoreType.DMA((2, 4)),
)


def chain_block(ref, c, half, i, j, part, width):
    me = lax.axis_index("exp")
    at_x, at_z = me // 4, lax.rem(me, 4)
    i, j = (i, j) if half == 0 else (j, i)
    rows = pl.ds(0, 32) if part is None else pl.ds(16 * part, 16)
    columns = pl.ds(width * half, width)
    return ref.at[c, lax.rem(at_x + i, 4), lax.rem(at_z + j, 4), rows, columns]


def chain_exp_gather(own, ref, c, send, recv, width=512):
    sides = [around("x"), around("z")]
    first, second = [], []
    for half in range(2):

        def ring(view, src, at, axis, half=half):
            return RingGather(
                view,
                src,
                sides[axis][0],
                sides[axis][1],
                [send.at[c, half, at, n] for n in range(4)],
                [recv.at[c, half, at, n] for n in range(4)],
            )

        def along(k, part, half=half):
            return chain_block(ref, c, half, k, 0, part, width)

        src = own.at[:, pl.ds(width * half, width)]
        first.append(ring(along, src, 4, half))
        second.append([])
        for i in range(4):

            def across(k, part, half=half, i=i):
                return chain_block(ref, c, half, i, k, part, width)

            second[half].append(ring(across, src if i == 0 else None, i, 1 - half))
    for half in range(2):
        first[half].start()
    for half in range(2):
        second[half][0].start()
        chain_block(ref, c, half, 0, 0, None, width)[...] = own[:, pl.ds(width * half, width)]
    yield
    for half in range(2):
        first[half].forward()
        second[half][3].start()
        second[half][1].start()
    yield
    for half in range(2):
        second[half][0].forward()
    for half in range(2):
        first[half].finish()
        second[half][2].start()
    yield
    for i in (3, 1):
        for half in range(2):
            second[half][i].forward()
    yield
    for half in range(2):
        second[half][2].forward()
    yield
    for half in range(2):
        for ring in second[half]:
            ring.finish()
        for ring in second[half] + [first[half]]:
            ring.drain()


def chain_exp_scatter(ref, c, temp, block, stage, ready, send, recv, out):
    sides = [around("x"), around("z")]
    first, second = [], []
    for half in range(2):

        def ring(view, at, axis, half=half):
            return RingScatter(
                view,
                lambda side: temp.at[c, half, at, side],
                lambda side, part: block.at[c, half, at, side, pl.ds(16 * part, 16)],
                lambda side: stage.at[c, half, at, side],
                sides[axis][0],
                sides[axis][1],
                [send.at[c, half, at, n] for n in range(6)],
                [recv.at[c, half, at, n] for n in range(6)],
            )

        first.append([])
        for j in range(4):

            def along(k, part, half=half, j=j):
                return chain_block(ref, c, half, k, j, part, 512)

            first[half].append(ring(along, j, half))

        def across(k, part, half=half):
            return ready.at[c, half, k, pl.ds(16 * part, 16)]

        second.append(ring(across, 4, 1 - half))
    order = (2, 1, 3, 0)
    for j in order:
        for half in range(2):
            first[half][j].start()
    yield
    for j in order:
        for half in range(2):
            first[half][j].middle()
    yield
    for j in order:
        for half in range(2):
            first[half][j].finish()
            for part in range(2):
                ready[c, half, j, pl.ds(16 * part, 16)] = first[half][j].total(part).astype(BF16)
            if j == 3:
                second[half].start()
    yield
    for half in range(2):
        second[half].middle()
    yield
    for half in range(2):
        second[half].finish()
        for part in range(2):
            out[c, pl.ds(16 * part, 16), pl.ds(512 * half, 512)] = second[half].total(part)
    for half in range(2):
        for ring in first[half] + [second[half]]:
            ring.drain()


EXP_SCRATCH = dict(
    es_temp=pltpu.VMEM((2, 2, 5, 2, 16, 512), BF16),
    es_block=pltpu.VMEM((2, 2, 5, 2, 32, 512), BF16),
    es_stage=pltpu.VMEM((2, 2, 5, 2, 16, 512), BF16),
    es_ready=pltpu.VMEM((2, 2, 4, 32, 512), BF16),
    es_made=pltpu.VMEM((2, 4, 4, 32, D), BF16),
    es_send=pltpu.SemaphoreType.DMA((2, 2, 5, 6)),
    es_recv=pltpu.SemaphoreType.DMA((2, 2, 5, 6)),
    eg_send=pltpu.SemaphoreType.DMA((2, 2, 5, 4)),
    eg_recv=pltpu.SemaphoreType.DMA((2, 2, 5, 4)),
)


def rope(values, cosine, sine):
    return values * three(cosine) + half_swapped(values) * three(sine)


def unrope(values, cosine, sine):
    return values * three(cosine) - half_swapped(values) * three(sine)


def shares(q, k, allowed):
    scores = jnp.where(allowed, dot_nt(q, k) * SCORE_SCALE, MASKED)
    lifted = jnp.exp(scores - jnp.max(scores, axis=1, keepdims=True))
    return lifted / jnp.sum(lifted, axis=1, keepdims=True)


def forward_chain(at, c, layer, loads):
    x = at.xin[c].astype(F32)
    at.normed[c] = (x * inverse_rms(x) * at.gains[layer, 0:1]).astype(BF16)
    yield from chain_tp_gather(at.normed.at[c], at.rows, c, at.tg_send, at.tg_recv)
    if c == 0:
        loads["wqkv"].wait()
        loads["wo"].wait()
    joined = dot(at.rows[c], at.v_wqkv[...])
    spot = slice(c * 128, c * 128 + 128)
    turned = rope(joined[:, :384], at.cosine[spot], at.sine[spot])
    qkv = jnp.concatenate([turned, joined[:, 384:]], axis=1).astype(BF16)
    at.qkv[c] = qkv
    allowed = at.mask[c] > 0.5
    outs = []
    for h in range(4):
        kv = h // 2
        share = shares(head(qkv, 0, h * HD), head(qkv, 0, 256 + kv * HD), allowed)
        outs.append(dot(share.astype(BF16), head(qkv, 0, 384 + kv * HD)))
    attended = jnp.concatenate(outs, axis=1).astype(BF16)
    at.att[c] = attended
    at.part[c] = dot(attended, at.v_wo[...]).astype(BF16)
    yield from chain_tp_scatter(
        at.part, c, at.tp_temp, at.tp_block, at.tp_stage, at.tp_send, at.tp_recv, at.tp_sum
    )
    after = x + at.tp_sum[c]
    at.after[c] = after
    at.normed_two[c] = (after * inverse_rms(after) * at.gains[layer, 1:2]).astype(BF16)
    yield from chain_exp_gather(at.normed_two.at[c], at.v_x, c, at.eg_send, at.eg_recv)
    at.saves[c].start()
    if c == 0:
        for key in ("router", "wgu", "wd"):
            loads[key].wait()
    for tile in range(2):
        pair = pl.ds(2 * tile, 2)
        rows = pl.ds(256 * tile, 256)
        xt = at.v_x[c, pair].reshape(256, D)
        gates = masked_softmax(
            dot(xt, at.v_router[...]), at.routed[c, pair, :, :, :LANES].reshape(256, LANES).astype(F32)
        )
        total = None
        for e in range(2):
            gate = jnp.sum(gates * at.sel[e : e + 1], axis=1, keepdims=True)
            gu = dot(xt, at.v_wgu[e])
            at.v_gu[c, e, rows] = gu.astype(BF16)
            part, upper = gu[:, :F], gu[:, F:]
            hidden = part * jax.nn.sigmoid(part) * upper
            made = dot((hidden * gate).astype(BF16), at.v_wd[e])
            total = made if total is None else total + made
        at.es_made[c, pair] = total.astype(BF16).reshape(2, 4, 32, D)
    at.saves[2 + c].start()
    yield from chain_exp_scatter(
        at.es_made,
        c,
        at.es_temp,
        at.es_block,
        at.es_stage,
        at.es_ready,
        at.es_send,
        at.es_recv,
        at.y,
    )
    at.out[c] = (at.after[c] + at.y[c]).astype(BF16)
    at.saves[c].wait()
    at.saves[2 + c].wait()


def mask_chain(at, c):
    yield from chain_exp_gather(
        at.routed_own.at[c], at.routed, c, at.mg_send, at.mg_recv, width=LANES
    )


def pair_chain(at, loads):
    me = lax.axis_index("section")
    (peer,) = around("section")
    sends, reads, writes = [], [], []
    pieces = ((at.own_gu, at.held_gu, at.wgu), (at.own_d, at.held_d, at.wd))
    for n, (own, held, both) in enumerate(pieces):
        sends.append(
            remote(own.at[0], both.at[me], at.pair_sems.at[0, n], at.pair_sems.at[1, n], peer)
        )
        reads.append(pltpu.make_async_copy(own.at[0], held, at.pair_sems.at[2, n]))
        writes.append(pltpu.make_async_copy(held, both.at[me], at.pair_sems.at[3, n]))
        sends[-1].start()
        reads[-1].start()
    yield
    yield
    for n in range(2):
        reads[n].wait()
        writes[n].start()
    for _ in range(6):
        yield
    for n in range(2):
        writes[n].wait()
        sends[n].wait()
    loads["wgu"].start()
    loads["wd"].start()


def forward_pass(xin, layer, tables, sel, weights, routed_own, routed):
    cosine, sine, mask = tables
    wqkv, wo, gains, router, wgu, wd = weights
    swap = layer == 0
    v, a = in_vmem(), in_any()
    ins = dict(
        xin=(xin, v),
        gains=(gains, v),
        cosine=(cosine, v),
        sine=(sine, v),
        mask=(mask, v),
        sel=(sel, v),
        wqkv=(wqkv, a),
        wo=(wo, a),
        router=(router, a),
    )
    if swap:
        ins.update(routed_own=(routed_own, v), own_gu=(wgu, a), own_d=(wd, a))
    else:
        ins.update(routed=(routed, v), wgu=(wgu, a), wd=(wd, a))
    outs = dict(
        out=((2, 32, D), BF16, v),
        rows=((2, 128, D), BF16, v),
        qkv=((2, 128, 512), BF16, v),
        att=((2, 128, 256), BF16, v),
        after=((2, 32, D), F32, v),
        y=((2, 32, D), F32, v),
        x_all=((2, 4, 4, 32, D), BF16, a),
        gu=((2, 2, 512, 2 * F), BF16, a),
    )
    scratch = dict(
        normed=pltpu.VMEM((2, 32, D), BF16),
        normed_two=pltpu.VMEM((2, 32, D), BF16),
        part=pltpu.VMEM((2, 128, D), BF16),
        v_wqkv=pltpu.VMEM((D, 512), BF16),
        v_wo=pltpu.VMEM((256, D), BF16),
        v_router=pltpu.VMEM((D, LANES), BF16),
        v_wgu=pltpu.VMEM((2, D, 2 * F), BF16),
        v_wd=pltpu.VMEM((2, F, D), BF16),
        v_x=pltpu.VMEM((2, 4, 4, 32, D), BF16),
        v_gu=pltpu.VMEM((2, 2, 512, 2 * F), BF16),
        load_sems=pltpu.SemaphoreType.DMA((5,)),
        save_sems=pltpu.SemaphoreType.DMA((4,)),
        **TP_SCRATCH,
        **EXP_SCRATCH,
    )
    if swap:
        outs.update(
            wgu=((2, 2, D, 2 * F), BF16, a),
            wd=((2, 2, F, D), BF16, a),
            routed=((2, 4, 4, 32, 2 * LANES), BF16, v),
        )
        scratch.update(
            held_gu=pltpu.VMEM((2, D, 2 * F), BF16),
            held_d=pltpu.VMEM((2, F, D), BF16),
            pair_sems=pltpu.SemaphoreType.DMA((4, 2)),
            mg_send=pltpu.SemaphoreType.DMA((2, 2, 5, 4)),
            mg_recv=pltpu.SemaphoreType.DMA((2, 2, 5, 4)),
        )

    def chains(at):
        loads = {}
        for n, key in enumerate(("wqkv", "wo", "router", "wgu", "wd")):
            loads[key] = pltpu.make_async_copy(
                getattr(at, key).at[layer], getattr(at, "v_" + key), at.load_sems.at[n]
            )
        at.saves = [
            pltpu.make_async_copy(src.at[c], dst.at[c], at.save_sems.at[2 * n + c])
            for n, (src, dst) in enumerate(((at.v_x, at.x_all), (at.v_gu, at.gu)))
            for c in range(2)
        ]
        for key in ("wqkv", "wo", "router") if swap else loads:
            loads[key].start()
        running = [forward_chain(at, c, layer, loads) for c in range(2)]
        if swap:
            running = [pair_chain(at, loads), mask_chain(at, 0), mask_chain(at, 1)] + running
        return running

    axes = ["tp", "x", "z"] + (["section"] if swap else [])
    return one_kernel("forward%d" % layer, 10 + layer, axes, ins, outs, scratch, chains)


def layer_backward(grad, stored, layer, common, weights, pending):
    tables, mask_own, mask_all, sel = common
    wqkv, wo, gains, router, wgu, wd = weights
    layer_in, inverse_one, rows, qkv, att, after, inverse_two, normed_two, x_all, gu, y = stored
    done = []
    if layer == 1:
        (g_all,) = fuse([exp_gather_part(grad)], 4, "exp_gather")
    else:
        g_all, more = fuse([exp_gather_part(grad), expert_part(*pending[0])], 7, "gather_expert")
        done.append(more)
    g_all = g_all.reshape(1024, D)
    dx, dgu, dd, dr = experts_backward(x_all, g_all, gu, wgu, wd, router, mask_all, sel, layer)
    pending = [(dgu, 0), (dgu, 512), (dd, 0)]
    gates = masked_softmax(dot(normed_two, router[layer]), mask_own)
    gf = grad.astype(F32)
    gc = (gates * jnp.sum(gf * y, axis=1, keepdims=True)).astype(BF16)
    count = 2 if layer == 1 else 1
    results = fuse(
        [exp_scatter_part(dx)] + [expert_part(*piece) for piece in pending[:count]],
        8 + layer,
        "scatter_expert",
    )
    done += results[1:]
    pending = pending[count:]
    grad_n = results[0] - dot_nt(gc, router[layer])
    dr = dr - dot_tn(normed_two, gc)
    scaled = grad_n * gains[layer, 1:2]
    grad_after = (
        gf
        + inverse_two * scaled
        - after * inverse_two**3 * jnp.mean(after * scaled, axis=1, keepdims=True)
    )
    d_mixture = jnp.sum(grad_n * after * inverse_two, axis=0)
    ga = grad_after.astype(BF16).reshape(2, 32, D)
    ga = fuse([tp_gather_part(ga)], 2, "tp_gather")[0].reshape(256, D)
    dn, dw = attention_backward(rows, ga, qkv, att, wqkv, wo, tables, layer)
    grad_n = fuse([tp_scatter_part(dn)], 3, "tp_scatter")[0].reshape(64, D)
    scaled = grad_n * gains[layer, 0:1]
    grad_in = (
        grad_after
        + inverse_one * scaled
        - layer_in * inverse_one**3 * jnp.mean(layer_in * scaled, axis=1, keepdims=True)
    )
    d_attention = jnp.sum(grad_n * layer_in * inverse_one, axis=0)
    lane = jnp.arange(LANES)[None, :]
    small = jnp.where(lane == E, d_attention[:, None], jnp.where(lane == E + 1, d_mixture[:, None], dr))
    wide = jnp.concatenate([dw, small.astype(BF16)], axis=1)
    return grad_in, wide, done, pending


def rope_tables(seg_rows):
    length = seg_rows.shape[0]
    before = jnp.sum((seg_rows[None, :] < seg_rows[:, None]).astype(jnp.int32), axis=1)
    places = (jnp.arange(length, dtype=jnp.int32) - before).astype(F32)
    powers = jnp.arange(0, HD, 2, dtype=jnp.int32).astype(F32) / HD
    angles = places[:, None] * (ROPE_BASE ** (-powers))[None, :]
    cosine, sine = jnp.cos(angles), jnp.sin(angles)
    indices = jnp.arange(length, dtype=jnp.int32)
    allowed = (seg_rows[:, None] == seg_rows[None, :]) & (indices[None, :] <= indices[:, None])
    return (
        jnp.concatenate([cosine] * 4, axis=1),
        jnp.concatenate([-sine, sine, -sine, sine], axis=1),
        allowed.astype(F32),
    )


def routed(routes):
    labels = jnp.arange(LANES, dtype=jnp.int32)
    return jnp.sum((routes[:, :, None] == labels[None, None, :]).astype(F32), axis=1)


def per_device(
    activations,
    cotangent,
    segments,
    routes,
    attention_gain,
    query_weight,
    key_weight,
    value_weight,
    output_weight,
    mixture_gain,
    router_weight,
    expert_gate_up,
    expert_down,
):
    section = lax.axis_index("section")
    expert = lax.axis_index("exp")

    def own_batches(array):
        return lax.dynamic_slice_in_dim(array, 2 * section, 2, 0)

    def to_owner(first, second):
        sent = jnp.where(section == 0, second, first)
        kept = jnp.where(section == 0, first, second)
        return kept, lax.ppermute(sent, "section", [(0, 1), (1, 0)])

    def by_layer(first, second):
        kept, got = to_owner(first, second)
        kept, got = kept.reshape(2, 32, D), got.reshape(2, 32, D)
        return jnp.where(
            section == 0,
            jnp.concatenate([kept, got], axis=0),
            jnp.concatenate([got, kept], axis=0),
        )[None]

    qkv_own = jnp.concatenate([query_weight, key_weight, value_weight], axis=2)
    gains_own = jnp.concatenate(
        [attention_gain, mixture_gain, jnp.zeros((6, D), BF16)], axis=0
    ).astype(F32)[None]
    router_own = jnp.pad(router_weight, ((0, 0), (0, 0), (0, LANES - E)))
    (paired,) = fuse([pair_part([qkv_own, output_weight, gains_own, router_own])], 0, "pair")
    weights = tuple(paired) + (expert_gate_up, expert_down)

    cosine, sine, mask = jax.vmap(rope_tables)(own_batches(segments))
    tables = (cosine.reshape(256, LANES), sine.reshape(256, LANES), mask)
    routes_own = own_batches(routes).reshape(64, 8)
    lanes = lax.broadcasted_iota(jnp.int32, (8, LANES), 1)
    sel = (lanes == 2 * expert + lax.broadcasted_iota(jnp.int32, (8, LANES), 0)).astype(F32)
    routed_own = routed(routes_own)
    doubled = jnp.concatenate([routed_own] * 2, axis=1).astype(BF16).reshape(2, 32, 2 * LANES)

    start = own_batches(activations)
    made = forward_pass(start, 0, tables, sel, weights, doubled, None)
    out_first = made.out
    weights = tuple(paired) + (made.wgu, made.wd)
    routed_all = made.routed[..., :LANES]
    kept = forward_pass(out_first, 1, tables, sel, weights, None, made.routed)
    out_second = kept.out

    def old(made, layer_in):
        layer_in = layer_in.reshape(64, D).astype(F32)
        after = made.after.reshape(64, D)
        inverse_two = inverse_rms(after)
        return (
            layer_in,
            inverse_rms(layer_in),
            made.rows.reshape(256, D),
            made.qkv.reshape(256, 512),
            made.att.reshape(256, 256),
            after,
            inverse_two,
            (after * inverse_two * paired[2][0 if made is first_made else 1, 1:2]).astype(BF16),
            made.x_all.transpose(1, 2, 0, 3, 4).reshape(1024, D),
            made.gu.reshape(2, 2, 16, 32, D).transpose(1, 2, 0, 3, 4).reshape(2, 1024, D),
            made.y.reshape(64, D),
        )

    first_made = made
    kept_first, kept_second = old(made, start), old(kept, out_first)
    mask_all = routed_all.transpose(1, 2, 0, 3, 4).reshape(1024, LANES).astype(F32)
    common = (tables, routed_own, mask_all, sel)
    grad = own_batches(cotangent).reshape(64, D)
    grad_second, wide_second, done_second, pending = layer_backward(
        grad, kept_second, 1, common, weights, []
    )
    grad_first, wide_first, done_first, pending = layer_backward(
        grad_second.astype(BF16), kept_first, 0, common, weights, pending
    )
    done_second.append(done_first.pop(0))
    (dw, small), *rest = fuse(
        [settle_part(wide_first, wide_second)] + [expert_part(*piece) for piece in pending],
        6,
        "settle",
    )
    done_first += rest
    small = small.reshape(D, LANES)
    experts = []
    for first, second in zip(done_first, done_second):
        kept, got = to_owner(first, second)
        kept, got = kept.astype(F32), got.astype(F32)
        experts.append(
            jnp.where(section == 0, jnp.stack([kept, got]), jnp.stack([got, kept]))[None]
        )
    return (
        by_layer(out_first.reshape(64, D), out_second.reshape(64, D)),
        by_layer(grad_first, grad_second),
        small[:, E][None],
        dw[None, :, :256],
        dw[None, :, 256:384],
        dw[None, :, 384:512],
        dw[:, 512:].T[None],
        small[:, E + 1][None],
        small[None, :, :E],
        jnp.concatenate(experts[:2], axis=2),
        experts[2],
    )


def solution(mesh):
    placed = (
        P(None, ("exp", "tp"), None),
        P(None, ("exp", "tp"), None),
        P(None, "exp"),
        P(None, ("exp", "tp"), None),
        P("section", None),
        P("section", None, "tp"),
        P("section", None, "tp"),
        P("section", None, "tp"),
        P("section", "tp", None),
        P("section", None),
        P("section", None, None),
        P("section", "exp", None, None),
        P("section", "exp", None, None),
    )
    return jax.shard_map(
        per_device,
        mesh=mesh,
        in_specs=placed,
        out_specs=(
            P("section", None, ("exp", "tp"), None),
            P("section", None, ("exp", "tp"), None),
            P("section", None),
            P("section", "exp", "tp"),
            P("section", "exp", "tp"),
            P("section", "exp", "tp"),
            P("section", "tp", "exp"),
            P("section", None),
            P("section", None, None),
            P("section", "exp", None, "tp"),
            P("section", "exp", None, "tp"),
        ),
        check_vma=False,
    )
```

```python
import functools

import jax
import jax.numpy as jnp
from jax import lax
from jax.experimental import pallas as pl
from jax.experimental.pallas import tpu as pltpu
from jax.sharding import PartitionSpec as P

D = 1024
HD = 64
E = 32
F = 512
LANES = 128
EPSILON = 1e-06
ROPE_BASE = 10000.0
SCORE_SCALE = 0.125
MASKED = -1e30
MESH = pl.DeviceIdType.MESH
VMEM_LIMIT = 56 * 1024 * 1024
BF16 = jnp.bfloat16
F32 = jnp.float32


def dot(a, b):
    return jnp.dot(a, b, preferred_element_type=F32)


def dot_nt(a, b):
    return lax.dot_general(a, b, (((1,), (1,)), ((), ())), preferred_element_type=F32)


def dot_tn(a, b):
    return lax.dot_general(a, b, (((0,), (0,)), ((), ())), preferred_element_type=F32)


def in_vmem():
    return pl.BlockSpec(memory_space=pltpu.VMEM)


def in_any():
    return pl.BlockSpec(memory_space=pl.ANY)


def greet(peers):
    barrier = pltpu.get_barrier_semaphore()
    for peer in peers:
        pl.semaphore_signal(barrier, inc=1, device_id=peer, device_id_type=MESH)
    pl.semaphore_wait(barrier, len(peers))


def remote(src, dst, send_sem, recv_sem, peer):
    return pltpu.make_async_remote_copy(
        src_ref=src,
        dst_ref=dst,
        send_sem=send_sem,
        recv_sem=recv_sem,
        device_id=peer,
        device_id_type=MESH,
    )


def comm_params(number):
    return pltpu.CompilerParams(
        collective_id=number, has_side_effects=True, vmem_limit_bytes=VMEM_LIMIT
    )


class Part:
    def __init__(self, arrays, in_specs, out_shapes, out_specs, scratch, axes, body):
        self.arrays, self.in_specs = arrays, in_specs
        self.out_shapes, self.out_specs = out_shapes, out_specs
        self.scratch, self.axes, self.body = scratch, axes, body


def around(axis):
    if axis == "section":
        return [{"section": 1 - lax.axis_index("section")}]
    if axis == "tp":
        me = lax.axis_index("tp")
        return [{"tp": lax.rem(me + j, 4)} for j in (3, 1)]
    if axis == "tp_opposite":
        return [{"tp": lax.rem(lax.axis_index("tp") + 2, 4)}]
    me = lax.axis_index("exp")
    at_x, at_z = me // 4, lax.rem(me, 4)
    if axis == "x":
        return [{"exp": lax.rem(at_x + j, 4) * 4 + at_z} for j in (3, 1)]
    return [{"exp": at_x * 4 + lax.rem(at_z + j, 4)} for j in (3, 1)]


def fused_kernel(parts, *refs):
    refs = list(refs)

    def take(count):
        taken = refs[:count]
        del refs[:count]
        return taken

    ins = [take(len(part.arrays)) for part in parts]
    outs = [take(len(part.out_shapes)) for part in parts]
    scratch = [take(len(part.scratch)) for part in parts]
    axes = []
    for part in parts:
        axes += [axis for axis in part.axes if axis not in axes]
    greet([peer for axis in axes for peer in around(axis)])
    running = [part.body(i, o, s) for part, i, o, s in zip(parts, ins, outs, scratch)]
    while running:
        for one in list(running):
            if next(one, "end") == "end":
                running.remove(one)


def fuse(parts, number, name):
    outs = pl.pallas_call(
        functools.partial(fused_kernel, parts),
        out_shape=[o for part in parts for o in part.out_shapes],
        in_specs=[s for part in parts for s in part.in_specs],
        out_specs=[s for part in parts for s in part.out_specs],
        scratch_shapes=[s for part in parts for s in part.scratch],
        compiler_params=comm_params(number),
        name=name,
    )(*[a for part in parts for a in part.arrays])
    outs = list(outs)
    results = []
    for part in parts:
        count = len(part.out_shapes)
        results.append(outs[:count] if count > 1 else outs[0])
        outs = outs[count:]
    return results


def sems(*shape):
    return [pltpu.SemaphoreType.DMA(shape)] * 2


def pair_part(arrays):
    count = len(arrays)

    def body(ins, outs, scratch):
        held, (send, recv, read, write) = scratch[:count], scratch[count:]
        me = lax.axis_index("section")
        (peer,) = around("section")
        sends, reads, writes = [], [], []
        for at in range(count):
            sends.append(remote(ins[at].at[0], outs[at].at[me], send.at[at], recv.at[at], peer))
            reads.append(pltpu.make_async_copy(ins[at].at[0], held[at], read.at[at]))
            writes.append(pltpu.make_async_copy(held[at], outs[at].at[me], write.at[at]))
            sends[-1].start()
            reads[-1].start()
        yield
        for at in range(count):
            reads[at].wait()
            writes[at].start()
        yield
        yield
        yield
        for at in range(count):
            writes[at].wait()
            sends[at].wait()

    return Part(
        arrays,
        [in_any()] * count,
        [jax.ShapeDtypeStruct((2,) + a.shape[1:], a.dtype) for a in arrays],
        [in_any()] * count,
        [pltpu.VMEM(a.shape[1:], a.dtype) for a in arrays]
        + [pltpu.SemaphoreType.DMA((count,))] * 4,
        ["section"],
        body,
    )


class RingGather:
    def __init__(self, view, own, left, right, send, recv):
        self.view, self.own = view, own
        self.left, self.right, self.send, self.recv = left, right, send, recv
        self.copies = []

    def go(self, src, dst, at, peer):
        copy = remote(src, dst, self.send[at], self.recv[at], peer)
        copy.start()
        self.copies.append(copy)

    def start(self):
        own = self.view(0, None) if self.own is None else self.own
        self.go(own, self.view(0, None), 0, self.right)
        self.go(own, self.view(0, None), 1, self.left)

    def forward(self):
        self.copies[0].wait_recv()
        self.go(self.view(3, 0), self.view(3, 0), 2, self.right)
        self.copies[1].wait_recv()
        self.go(self.view(1, 1), self.view(1, 1), 3, self.left)

    def finish(self):
        self.copies[2].wait_recv()
        self.copies[3].wait_recv()

    def drain(self):
        for copy in self.copies:
            copy.wait_send()


class RingScatter:
    def __init__(self, view, temp, block, stage, left, right, send, recv):
        self.view, self.temp, self.block, self.stage = view, temp, block, stage
        self.left, self.right, self.send, self.recv = left, right, send, recv
        self.copies = []

    def go(self, src, dst, at, peer):
        copy = remote(src, dst, self.send[at], self.recv[at], peer)
        copy.start()
        self.copies.append(copy)

    def start(self):
        self.go(self.view(2, 0), self.temp(0), 0, self.right)
        self.go(self.view(2, 1), self.temp(1), 1, self.left)
        self.go(self.view(1, 1), self.block(0, 1), 2, self.right)
        self.go(self.view(3, 0), self.block(1, 0), 3, self.left)

    def middle(self):
        for side, nearer, peer in ((0, 1, self.right), (1, 3, self.left)):
            self.copies[side].wait_recv()
            term = self.view(nearer, side)[...].astype(F32) + self.temp(side)[...].astype(F32)
            self.stage(side)[...] = term.astype(BF16)
            self.go(self.stage(side), self.block(side, side), 4 + side, peer)

    def finish(self):
        for copy in self.copies[2:]:
            copy.wait_recv()

    def total(self, part):
        return (
            self.view(0, part)[...].astype(F32)
            + self.block(0, part)[...].astype(F32)
            + self.block(1, part)[...].astype(F32)
        )

    def drain(self):
        for copy in self.copies:
            copy.wait_send()


def exp_block(ref, half, i, j, part):
    me = lax.axis_index("exp")
    at_x, at_z = me // 4, lax.rem(me, 4)
    i, j = (i, j) if half == 0 else (j, i)
    rows = pl.ds(32 * half, 32) if part is None else pl.ds(32 * half + 16 * part, 16)
    return ref.at[lax.rem(at_x + i, 4), lax.rem(at_z + j, 4), rows]


def exp_gather_steps(x_ref, out_ref, send, recv):
    sides = [around("x"), around("z")]
    first, second = [], []
    for half in range(2):

        def ring(view, own, at, axis, half=half):
            return RingGather(
                view,
                own,
                sides[axis][0],
                sides[axis][1],
                [send.at[half, at, n] for n in range(4)],
                [recv.at[half, at, n] for n in range(4)],
            )

        def along(k, part, half=half):
            return exp_block(out_ref, half, k, 0, part)

        own = x_ref.at[pl.ds(32 * half, 32)]
        first.append(ring(along, own, 4, half))
        second.append([])
        for i in range(4):

            def across(k, part, half=half, i=i):
                return exp_block(out_ref, half, i, k, part)

            second[half].append(ring(across, own if i == 0 else None, i, 1 - half))
    for half in range(2):
        first[half].start()
    for half in range(2):
        second[half][0].start()
        exp_block(out_ref, half, 0, 0, None)[...] = x_ref[pl.ds(32 * half, 32)]
    yield
    for half in range(2):
        first[half].forward()
        second[half][3].start()
        second[half][1].start()
    yield
    for half in range(2):
        second[half][0].forward()
    yield
    for half in range(2):
        first[half].finish()
        second[half][2].start()
    yield
    for i in (3, 1):
        for half in range(2):
            second[half][i].forward()
    yield
    for half in range(2):
        second[half][2].forward()
    yield
    for half in range(2):
        for ring in second[half]:
            ring.finish()
        for ring in second[half] + [first[half]]:
            ring.drain()


def exp_scatter_steps(x_ref, out_ref, temp, block, stage, ready, send, recv):
    sides = [around("x"), around("z")]
    first, second = [], []
    for half in range(2):

        def ring(view, at, axis, half=half):
            return RingScatter(
                view,
                lambda side: temp.at[half, at, side],
                lambda side, part: block.at[half, at, side, pl.ds(16 * part, 16)],
                lambda side: stage.at[half, at, side],
                sides[axis][0],
                sides[axis][1],
                [send.at[half, at, n] for n in range(6)],
                [recv.at[half, at, n] for n in range(6)],
            )

        first.append([])
        for j in range(4):

            def along(k, part, half=half, j=j):
                return exp_block(x_ref, half, k, j, part)

            first[half].append(ring(along, j, half))

        def across(k, part, half=half):
            return ready.at[half, k, pl.ds(16 * part, 16)]

        second.append(ring(across, 4, 1 - half))
    order = (2, 1, 3, 0)
    for j in order:
        for half in range(2):
            first[half][j].start()
    yield
    for j in order:
        for half in range(2):
            first[half][j].middle()
        yield
    for j in order:
        for half in range(2):
            first[half][j].finish()
            for part in range(2):
                ready[half, j, pl.ds(16 * part, 16)] = first[half][j].total(part).astype(BF16)
            if j == 3:
                second[half].start()
    yield
    for half in range(2):
        second[half].middle()
    yield
    for half in range(2):
        second[half].finish()
        for part in range(2):
            out_ref[pl.ds(32 * half + 16 * part, 16)] = second[half].total(part)
    for half in range(2):
        for ring in first[half] + [second[half]]:
            ring.drain()


def exp_scatter_scratch(width):
    return [
        pltpu.VMEM((2, 5, 2, 16, width), BF16),
        pltpu.VMEM((2, 5, 2, 32, width), BF16),
        pltpu.VMEM((2, 5, 2, 16, width), BF16),
        pltpu.VMEM((2, 4, 32, width), BF16),
    ] + sems(2, 5, 6)


WIDE = 896


def settle_part(first, second):
    def body(ins, outs, scratch):
        first_ref, second_ref = ins
        out_ref, small_ref = outs
        got, x_ref, total, piece, held = scratch[:5]
        scatter, rest = scratch[5:11], scratch[11:]
        swap_send, swap_recv, tp_send, tp_recv, gather_send, gather_recv = rest
        me = lax.axis_index("section")
        (peer,) = around("section")
        copies = [
            remote(ref, got, swap_send.at[0], swap_recv.at[0], peer)
            for ref in (second_ref, first_ref)
        ]
        for layer in range(2):

            @pl.when(me == layer)
            def _():
                copies[layer].start()

        yield
        copies[0].wait_recv()
        for at_x in range(4):
            for at_z in range(4):
                mine = jnp.where(me == 0, first_ref[at_x, at_z], second_ref[at_x, at_z])
                summed = mine.astype(F32) + got[at_x, at_z].astype(F32)
                x_ref[at_x, at_z] = summed.astype(BF16)
        yield from exp_scatter_steps(x_ref, total, *scatter)
        out_ref[...] = total[:, :768]
        piece[...] = total[:, 768:]
        partners = around("tp") + around("tp_opposite")
        sent = [
            remote(piece, held.at[at], tp_send.at[at], tp_recv.at[at], partner)
            for at, partner in enumerate(partners)
        ]
        for copy in sent:
            copy.start()
        yield
        for copy in sent:
            copy.wait()
        piece[...] = piece[...] + ((held[0] + held[1]) + held[2])
        yield from exp_gather_steps(piece, small_ref, gather_send, gather_recv)
        copies[0].wait_send()

    return Part(
        [first.reshape(4, 4, 64, WIDE), second.reshape(4, 4, 64, WIDE)],
        [in_vmem()] * 2,
        [
            jax.ShapeDtypeStruct((64, 768), F32),
            jax.ShapeDtypeStruct((4, 4, 64, LANES), F32),
        ],
        [in_vmem()] * 2,
        [
            pltpu.VMEM((4, 4, 64, WIDE), BF16),
            pltpu.VMEM((4, 4, 64, WIDE), BF16),
            pltpu.VMEM((64, WIDE), F32),
            pltpu.VMEM((64, LANES), F32),
            pltpu.VMEM((3, 64, LANES), F32),
        ]
        + exp_scatter_scratch(WIDE)
        + [pltpu.SemaphoreType.DMA((1,))] * 2
        + sems(3)
        + sems(2, 5, 4),
        ["section", "x", "z", "tp", "tp_opposite"],
        body,
    )


def half_swapped(values):
    width = values.shape[1]
    lane = lax.broadcasted_iota(jnp.int32, values.shape, 1)
    ahead = pltpu.roll(values, width - 32, 1)
    behind = pltpu.roll(values, 32, 1)
    return jnp.where(lax.rem(lane, 64) < 32, ahead, behind)


def three(table):
    return jnp.concatenate([table, table, table], axis=1)


def head(values, batch, first):
    return values[batch * 128 : batch * 128 + 128, first : first + HD]


def layer_block(shape, layer):
    return pl.BlockSpec((1,) + shape, lambda i: (layer,) + (0,) * len(shape))


def whole(*shape):
    return pl.BlockSpec(shape, lambda i: (0,) * len(shape))


def local_params():
    return pltpu.CompilerParams(vmem_limit_bytes=VMEM_LIMIT)


def masked_softmax(logits, mask):
    routed = mask > 0.5
    shown = jnp.where(routed, logits, MASKED)
    lifted = jnp.where(routed, jnp.exp(shown - jnp.max(shown, axis=1, keepdims=True)), 0.0)
    return lifted / jnp.sum(lifted, axis=1, keepdims=True)


def inverse_rms(values):
    return lax.rsqrt(jnp.mean(values * values, axis=1, keepdims=True) + EPSILON)


class Names:
    pass


def take_turns(running):
    running = list(running)
    while running:
        for one in list(running):
            if next(one, "end") == "end":
                running.remove(one)


def one_kernel(name, number, axes, ins, outs, scratch, chains):
    names = list(ins) + list(outs) + list(scratch)

    def kernel(*refs):
        at = Names()
        for key, ref in zip(names, refs):
            setattr(at, key, ref)
        greet([peer for axis in axes for peer in around(axis)])
        take_turns(chains(at))

    results = pl.pallas_call(
        kernel,
        out_shape=[jax.ShapeDtypeStruct(o[0], o[1]) for o in outs.values()],
        in_specs=[i[1] for i in ins.values()],
        out_specs=[o[2] for o in outs.values()],
        scratch_shapes=list(scratch.values()),
        compiler_params=comm_params(number),
        name=name,
    )(*[i[0] for i in ins.values()])
    made = Names()
    for key, result in zip(outs, results):
        setattr(made, key, result)
    return made


def chain_tp_block(ref, c, k, part):
    place = lax.rem(lax.axis_index("tp") + k, 4)
    if part is None:
        return ref.at[c, pl.ds(pl.multiple_of(place * 32, 32), 32)]
    return ref.at[c, pl.ds(pl.multiple_of(place * 32 + 16 * part, 16), 16)]


def chain_tp_gather(own, ref, c, send, recv):
    left, right = around("tp")
    ring = RingGather(
        lambda k, part: chain_tp_block(ref, c, k, part),
        own,
        left,
        right,
        [send.at[c, i] for i in range(4)],
        [recv.at[c, i] for i in range(4)],
    )
    ring.start()
    chain_tp_block(ref, c, 0, None)[...] = own[...]
    yield
    ring.forward()
    yield
    ring.finish()
    ring.drain()


def chain_tp_scatter(ref, c, temp, block, stage, send, recv, out):
    left, right = around("tp")
    ring = RingScatter(
        lambda k, part: chain_tp_block(ref, c, k, part),
        lambda side: temp.at[c, side],
        lambda side, part: block.at[c, side, part],
        lambda side: stage.at[c, side],
        left,
        right,
        [send.at[c, i] for i in range(6)],
        [recv.at[c, i] for i in range(6)],
    )
    ring.start()
    yield
    ring.middle()
    yield
    ring.finish()
    for part in range(2):
        out[c, pl.ds(16 * part, 16)] = ring.total(part)
    ring.drain()


TP_SCRATCH = dict(
    tp_temp=pltpu.VMEM((2, 2, 16, D), BF16),
    tp_block=pltpu.VMEM((2, 2, 2, 16, D), BF16),
    tp_stage=pltpu.VMEM((2, 2, 16, D), BF16),
    tp_sum=pltpu.VMEM((2, 32, D), F32),
    tp_send=pltpu.SemaphoreType.DMA((2, 6)),
    tp_recv=pltpu.SemaphoreType.DMA((2, 6)),
    tg_send=pltpu.SemaphoreType.DMA((2, 4)),
    tg_recv=pltpu.SemaphoreType.DMA((2, 4)),
)


def chain_block(ref, c, half, i, j, part, width):
    me = lax.axis_index("exp")
    at_x, at_z = me // 4, lax.rem(me, 4)
    i, j = (i, j) if half == 0 else (j, i)
    rows = pl.ds(0, 32) if part is None else pl.ds(16 * part, 16)
    columns = pl.ds(width * half, width)
    return ref.at[c, lax.rem(at_x + i, 4), lax.rem(at_z + j, 4), rows, columns]


def chain_exp_gather(own, ref, c, send, recv, width=512):
    sides = [around("x"), around("z")]
    first, second = [], []
    for half in range(2):

        def ring(view, src, at, axis, half=half):
            return RingGather(
                view,
                src,
                sides[axis][0],
                sides[axis][1],
                [send.at[c, half, at, n] for n in range(4)],
                [recv.at[c, half, at, n] for n in range(4)],
            )

        def along(k, part, half=half):
            return chain_block(ref, c, half, k, 0, part, width)

        src = own.at[:, pl.ds(width * half, width)]
        first.append(ring(along, src, 4, half))
        second.append([])
        for i in range(4):

            def across(k, part, half=half, i=i):
                return chain_block(ref, c, half, i, k, part, width)

            second[half].append(ring(across, src if i == 0 else None, i, 1 - half))
    for half in range(2):
        first[half].start()
    for half in range(2):
        second[half][0].start()
        chain_block(ref, c, half, 0, 0, None, width)[...] = own[:, pl.ds(width * half, width)]
    yield
    for half in range(2):
        first[half].forward()
        second[half][3].start()
        second[half][1].start()
    yield
    for half in range(2):
        second[half][0].forward()
    for half in range(2):
        first[half].finish()
        second[half][2].start()
    yield
    for i in (3, 1):
        for half in range(2):
            second[half][i].forward()
    yield
    for half in range(2):
        second[half][2].forward()
    yield
    for half in range(2):
        for ring in second[half]:
            ring.finish()
        for ring in second[half] + [first[half]]:
            ring.drain()


def chain_exp_scatter(ref, c, temp, block, stage, ready, send, recv, out):
    sides = [around("x"), around("z")]
    first, second = [], []
    for half in range(2):

        def ring(view, at, axis, half=half):
            return RingScatter(
                view,
                lambda side: temp.at[c, half, at, side],
                lambda side, part: block.at[c, half, at, side, pl.ds(16 * part, 16)],
                lambda side: stage.at[c, half, at, side],
                sides[axis][0],
                sides[axis][1],
                [send.at[c, half, at, n] for n in range(6)],
                [recv.at[c, half, at, n] for n in range(6)],
            )

        first.append([])
        for j in range(4):

            def along(k, part, half=half, j=j):
                return chain_block(ref, c, half, k, j, part, 512)

            first[half].append(ring(along, j, half))

        def across(k, part, half=half):
            return ready.at[c, half, k, pl.ds(16 * part, 16)]

        second.append(ring(across, 4, 1 - half))
    order = (2, 1, 3, 0)
    for j in order:
        for half in range(2):
            first[half][j].start()
    yield
    for j in order:
        for half in range(2):
            first[half][j].middle()
    yield
    for j in order:
        for half in range(2):
            first[half][j].finish()
            for part in range(2):
                ready[c, half, j, pl.ds(16 * part, 16)] = first[half][j].total(part).astype(BF16)
            if j == 3:
                second[half].start()
    yield
    for half in range(2):
        second[half].middle()
    yield
    for half in range(2):
        second[half].finish()
        for part in range(2):
            out[c, pl.ds(16 * part, 16), pl.ds(512 * half, 512)] = second[half].total(part)
    for half in range(2):
        for ring in first[half] + [second[half]]:
            ring.drain()


EXP_SCRATCH = dict(
    es_temp=pltpu.VMEM((2, 2, 5, 2, 16, 512), BF16),
    es_block=pltpu.VMEM((2, 2, 5, 2, 32, 512), BF16),
    es_stage=pltpu.VMEM((2, 2, 5, 2, 16, 512), BF16),
    es_ready=pltpu.VMEM((2, 2, 4, 32, 512), BF16),
    es_made=pltpu.VMEM((2, 4, 4, 32, D), BF16),
    es_send=pltpu.SemaphoreType.DMA((2, 2, 5, 6)),
    es_recv=pltpu.SemaphoreType.DMA((2, 2, 5, 6)),
    eg_send=pltpu.SemaphoreType.DMA((2, 2, 5, 4)),
    eg_recv=pltpu.SemaphoreType.DMA((2, 2, 5, 4)),
)


def rope(values, cosine, sine):
    return values * three(cosine) + half_swapped(values) * three(sine)


def unrope(values, cosine, sine):
    return values * three(cosine) - half_swapped(values) * three(sine)


def shares(q, k, allowed):
    scores = jnp.where(allowed, dot_nt(q, k) * SCORE_SCALE, MASKED)
    lifted = jnp.exp(scores - jnp.max(scores, axis=1, keepdims=True))
    return lifted / jnp.sum(lifted, axis=1, keepdims=True)


def forward_chain(at, c, layer, loads):
    x = at.xin[c].astype(F32)
    at.normed[c] = (x * inverse_rms(x) * at.gains[layer, 0:1]).astype(BF16)
    yield from chain_tp_gather(at.normed.at[c], at.rows, c, at.tg_send, at.tg_recv)
    if c == 0:
        loads["wqkv"].wait()
        loads["wo"].wait()
    joined = dot(at.rows[c], at.v_wqkv[...])
    spot = slice(c * 128, c * 128 + 128)
    turned = rope(joined[:, :384], at.cosine[spot], at.sine[spot])
    qkv = jnp.concatenate([turned, joined[:, 384:]], axis=1).astype(BF16)
    at.qkv[c] = qkv
    allowed = at.mask[c] > 0.5
    outs = []
    for h in range(4):
        kv = h // 2
        share = shares(head(qkv, 0, h * HD), head(qkv, 0, 256 + kv * HD), allowed)
        outs.append(dot(share.astype(BF16), head(qkv, 0, 384 + kv * HD)))
    attended = jnp.concatenate(outs, axis=1).astype(BF16)
    at.att[c] = attended
    at.part[c] = dot(attended, at.v_wo[...]).astype(BF16)
    yield from chain_tp_scatter(
        at.part, c, at.tp_temp, at.tp_block, at.tp_stage, at.tp_send, at.tp_recv, at.tp_sum
    )
    after = x + at.tp_sum[c]
    at.after[c] = after
    at.normed_two[c] = (after * inverse_rms(after) * at.gains[layer, 1:2]).astype(BF16)
    yield from chain_exp_gather(at.normed_two.at[c], at.v_x, c, at.eg_send, at.eg_recv)
    at.saves[c].start()
    if c == 0:
        for key in ("router", "wgu", "wd"):
            loads[key].wait()
    for tile in range(2):
        pair = pl.ds(2 * tile, 2)
        rows = pl.ds(256 * tile, 256)
        xt = at.v_x[c, pair].reshape(256, D)
        gates = masked_softmax(
            dot(xt, at.v_router[...]), at.routed[c, pair, :, :, :LANES].reshape(256, LANES).astype(F32)
        )
        total = None
        for e in range(2):
            gate = jnp.sum(gates * at.sel[e : e + 1], axis=1, keepdims=True)
            gu = dot(xt, at.v_wgu[e])
            at.v_gu[c, e, rows] = gu.astype(BF16)
            part, upper = gu[:, :F], gu[:, F:]
            hidden = part * jax.nn.sigmoid(part) * upper
            made = dot((hidden * gate).astype(BF16), at.v_wd[e])
            total = made if total is None else total + made
        at.es_made[c, pair] = total.astype(BF16).reshape(2, 4, 32, D)
    at.saves[2 + c].start()
    yield from chain_exp_scatter(
        at.es_made,
        c,
        at.es_temp,
        at.es_block,
        at.es_stage,
        at.es_ready,
        at.es_send,
        at.es_recv,
        at.y,
    )
    at.out[c] = (at.after[c] + at.y[c]).astype(BF16)
    at.saves[c].wait()
    at.saves[2 + c].wait()


def mask_chain(at, c):
    yield from chain_exp_gather(
        at.routed_own.at[c], at.routed, c, at.mg_send, at.mg_recv, width=LANES
    )


def pair_chain(at, loads):
    me = lax.axis_index("section")
    (peer,) = around("section")
    sends, reads, writes = [], [], []
    pieces = ((at.own_gu, at.held_gu, at.wgu), (at.own_d, at.held_d, at.wd))
    for n, (own, held, both) in enumerate(pieces):
        sends.append(
            remote(own.at[0], both.at[me], at.pair_sems.at[0, n], at.pair_sems.at[1, n], peer)
        )
        reads.append(pltpu.make_async_copy(own.at[0], held, at.pair_sems.at[2, n]))
        writes.append(pltpu.make_async_copy(held, both.at[me], at.pair_sems.at[3, n]))
        sends[-1].start()
        reads[-1].start()
    yield
    yield
    for n in range(2):
        reads[n].wait()
        writes[n].start()
    for _ in range(6):
        yield
    for n in range(2):
        writes[n].wait()
        sends[n].wait()
    loads["wgu"].start()
    loads["wd"].start()


def forward_pass(xin, layer, tables, sel, weights, routed_own, routed):
    cosine, sine, mask = tables
    wqkv, wo, gains, router, wgu, wd = weights
    swap = layer == 0
    v, a = in_vmem(), in_any()
    ins = dict(
        xin=(xin, v),
        gains=(gains, v),
        cosine=(cosine, v),
        sine=(sine, v),
        mask=(mask, v),
        sel=(sel, v),
        wqkv=(wqkv, a),
        wo=(wo, a),
        router=(router, a),
    )
    if swap:
        ins.update(routed_own=(routed_own, v), own_gu=(wgu, a), own_d=(wd, a))
    else:
        ins.update(routed=(routed, v), wgu=(wgu, a), wd=(wd, a))
    outs = dict(
        out=((2, 32, D), BF16, v),
        rows=((2, 128, D), BF16, v),
        qkv=((2, 128, 512), BF16, v),
        att=((2, 128, 256), BF16, v),
        after=((2, 32, D), F32, v),
        y=((2, 32, D), F32, v),
        x_all=((2, 4, 4, 32, D), BF16, a),
        gu=((2, 2, 512, 2 * F), BF16, a),
    )
    scratch = dict(
        normed=pltpu.VMEM((2, 32, D), BF16),
        normed_two=pltpu.VMEM((2, 32, D), BF16),
        part=pltpu.VMEM((2, 128, D), BF16),
        v_wqkv=pltpu.VMEM((D, 512), BF16),
        v_wo=pltpu.VMEM((256, D), BF16),
        v_router=pltpu.VMEM((D, LANES), BF16),
        v_wgu=pltpu.VMEM((2, D, 2 * F), BF16),
        v_wd=pltpu.VMEM((2, F, D), BF16),
        v_x=pltpu.VMEM((2, 4, 4, 32, D), BF16),
        v_gu=pltpu.VMEM((2, 2, 512, 2 * F), BF16),
        load_sems=pltpu.SemaphoreType.DMA((5,)),
        save_sems=pltpu.SemaphoreType.DMA((4,)),
        **TP_SCRATCH,
        **EXP_SCRATCH,
    )
    if swap:
        outs.update(
            wgu=((2, 2, D, 2 * F), BF16, a),
            wd=((2, 2, F, D), BF16, a),
            routed=((2, 4, 4, 32, 2 * LANES), BF16, v),
        )
        scratch.update(
            held_gu=pltpu.VMEM((2, D, 2 * F), BF16),
            held_d=pltpu.VMEM((2, F, D), BF16),
            pair_sems=pltpu.SemaphoreType.DMA((4, 2)),
            mg_send=pltpu.SemaphoreType.DMA((2, 2, 5, 4)),
            mg_recv=pltpu.SemaphoreType.DMA((2, 2, 5, 4)),
        )

    def chains(at):
        loads = {}
        for n, key in enumerate(("wqkv", "wo", "router", "wgu", "wd")):
            loads[key] = pltpu.make_async_copy(
                getattr(at, key).at[layer], getattr(at, "v_" + key), at.load_sems.at[n]
            )
        at.saves = [
            pltpu.make_async_copy(src.at[c], dst.at[c], at.save_sems.at[2 * n + c])
            for n, (src, dst) in enumerate(((at.v_x, at.x_all), (at.v_gu, at.gu)))
            for c in range(2)
        ]
        for key in ("wqkv", "wo", "router") if swap else loads:
            loads[key].start()
        running = [forward_chain(at, c, layer, loads) for c in range(2)]
        if swap:
            running = [pair_chain(at, loads), mask_chain(at, 0), mask_chain(at, 1)] + running
        return running

    axes = ["tp", "x", "z"] + (["section"] if swap else [])
    return one_kernel("forward%d" % layer, 10 + layer, axes, ins, outs, scratch, chains)


def rms_back(q, values, gain):
    inverse = inverse_rms(values)
    scaled = q * gain
    back = inverse * scaled - values * inverse**3 * jnp.mean(values * scaled, axis=1, keepdims=True)
    return back, q * values * inverse


def backward_chain(at, c, layer, loads):
    gather = chain_exp_gather(at.grad.at[c], at.v_g, c, at.eg_send, at.eg_recv)
    next(gather)
    after = at.after[c]
    normed_two = (after * inverse_rms(after) * at.gains[layer, 1:2]).astype(BF16)
    if c == 0:
        loads["router"].wait()
    own_gates = masked_softmax(
        dot(normed_two, at.v_router[...]), at.routed_own[c, :, :LANES].astype(F32)
    )
    gf = at.grad[c].astype(F32)
    gc = (-own_gates * jnp.sum(gf * at.y[c], axis=1, keepdims=True)).astype(BF16)
    lane = lax.broadcasted_iota(jnp.int32, (32, LANES), 1)
    at.small_left[c, 0:32] = normed_two
    at.small_right[c, 0:32] = gc
    at.small_right[c, 32:64] = jnp.where(lane == E + 1, 1.0, 0.0).astype(BF16)
    at.small_right[c, 64:96] = jnp.where(lane == E, 1.0, 0.0).astype(BF16)
    yield
    yield from gather
    if c == 0:
        for key in ("x", "gu", "wd", "wgu"):
            loads[key].wait()
    for tile in range(2):
        pair = pl.ds(2 * tile, 2)
        rows = pl.ds(256 * tile, 256)
        both = pl.ds(512 * c + 256 * tile, 256)
        xt = at.v_x[c, pair].reshape(256, D)
        gt = at.v_g[c, pair].reshape(256, D)
        gates = masked_softmax(
            dot(xt, at.v_router[...]),
            at.routed[c, pair, :, :, :LANES].reshape(256, LANES).astype(F32),
        )
        gl, total = None, None
        for e in range(2):
            chosen = at.sel[e : e + 1]
            gate = jnp.sum(gates * chosen, axis=1, keepdims=True)
            gh = dot_nt(gt, at.v_wd[e])
            part = at.v_gu[c, e, rows, :F].astype(F32)
            upper = at.v_gu[c, e, rows, F:].astype(F32)
            s = jax.nn.sigmoid(part)
            act = part * s
            hidden = act * upper
            term = (gate * jnp.sum(hidden * gh, axis=1, keepdims=True)) * chosen
            gl = term if gl is None else gl + term
            at.hs[e, both] = (hidden * gate).astype(BF16)
            gh = gh * gate
            at.gj[e, both, :F] = (gh * upper * (s + act * (1.0 - s))).astype(BF16)
            at.gj[e, both, F:] = (gh * act).astype(BF16)
            dx = dot_nt(at.gj[e, both], at.v_wgu[e])
            total = dx if total is None else total + dx
        gl = gl.astype(BF16)
        at.gl[both] = gl
        total = total + dot_nt(gl, at.v_router[...])
        at.es_made[c, pair] = total.astype(BF16).reshape(2, 4, 32, D)
    yield from chain_exp_scatter(
        at.es_made,
        c,
        at.es_temp,
        at.es_block,
        at.es_stage,
        at.es_ready,
        at.es_send,
        at.es_recv,
        at.es_sum,
    )
    grad_n = at.es_sum[c] + dot_nt(at.small_right[c, 0:32], at.v_router[...])
    back, term = rms_back(grad_n, at.after[c], at.gains[layer, 1:2])
    at.small_left[c, 32:64] = term.astype(BF16)
    grad_after = at.grad[c].astype(F32) + back
    at.grad_after[c] = grad_after
    at.ga_own[c] = grad_after.astype(BF16)
    yield from chain_tp_gather(at.ga_own.at[c], at.ga, c, at.tg_send, at.tg_recv)
    if c == 0:
        loads["wqkv"].wait()
        loads["wo"].wait()
    gatt = dot_nt(at.ga[c], at.v_wo[...]).astype(BF16)
    qkv = at.qkv[c]
    allowed = at.mask[c] > 0.5
    gqs, gks, gvs = [], [None, None], [None, None]
    for h in range(4):
        kv = h // 2
        q = head(qkv, 0, h * HD)
        k = head(qkv, 0, 256 + kv * HD)
        v = head(qkv, 0, 384 + kv * HD)
        go = head(gatt, 0, h * HD)
        share = shares(q, k, allowed)
        gp = dot_nt(go, v)
        gs = (share * (gp - jnp.sum(share * gp, axis=1, keepdims=True))).astype(BF16)
        gqs.append(dot(gs, k) * SCORE_SCALE)
        gk = dot_tn(gs, q) * SCORE_SCALE
        gv = dot_tn(share.astype(BF16), go)
        gks[kv] = gk if gks[kv] is None else gks[kv] + gk
        gvs[kv] = gv if gvs[kv] is None else gvs[kv] + gv
    joined = jnp.concatenate(gqs + gks + gvs, axis=1)
    spot = slice(c * 128, c * 128 + 128)
    turned = unrope(joined[:, :384], at.cosine[spot], at.sine[spot])
    gqkv = jnp.concatenate([turned, joined[:, 384:]], axis=1).astype(BF16)
    at.gqkv[c] = gqkv
    at.part[c] = dot_nt(gqkv, at.v_wqkv[...]).astype(BF16)
    yield from chain_tp_scatter(
        at.part, c, at.tp_temp, at.tp_block, at.tp_stage, at.tp_send, at.tp_recv, at.tp_sum
    )
    back, term = rms_back(at.tp_sum[c], at.xin[c].astype(F32), at.gains[layer, 0:1])
    at.small_left[c, 64:96] = term.astype(BF16)
    at.grad_in[c] = at.grad_after[c] + back


def weight_chain(at):
    for _ in range(5):
        yield

    def joint(e, tile):
        columns = pl.ds(256 * tile, 256)
        x = at.v_x[:, :, :, :, columns].reshape(1024, 256)
        at.dgu[e, columns] = dot_tn(x, at.gj[e]).astype(BF16)

    for chunk in range(2):
        for e in range(2):
            for tile in range(2):
                joint(e, 2 * chunk + tile)
        yield
    for e in range(2):
        for tile in range(2):
            columns = pl.ds(256 * tile, 256)
            g = at.v_g[...].reshape(1024, D)
            at.dd[e, columns] = dot_tn(at.hs[e, :, columns], g).astype(BF16)
    yield
    x = at.v_x[...].reshape(1024, D)
    at.small[...] = dot_tn(x, at.gl[...])
    yield
    yield
    yield
    yield
    ga = at.ga[...].reshape(256, D)
    at.wide[:, 512:768] = dot_tn(ga, at.att[...].reshape(256, 256)).astype(BF16)
    rows = at.rows[...].reshape(256, D)
    at.wide[:, :512] = dot_tn(rows, at.gqkv[...].reshape(256, 512)).astype(BF16)
    yield
    yield
    left = at.small_left[...].reshape(192, D)
    right = at.small_right[...].reshape(192, LANES)
    at.wide[:, 768:] = (at.small[...] + dot_tn(left, right)).astype(BF16)


def expert_chain(at, n, source, out, first_row):
    for _ in range(5 + n):
        yield
    rows = pl.ds(first_row, 512)
    me = lax.axis_index("section")
    place = lax.axis_index("tp")
    left, right = around("tp")
    (peer,) = around("section")
    got = at.got.at[n]
    swap = remote(source.at[1 - me, rows], got, at.swap_sems.at[0, n], at.swap_sems.at[1, n], peer)
    swap.start()
    yield
    swap.wait_recv()

    @pl.loop(0, 8)
    def _(i):
        r = pl.ds(pl.multiple_of(i * 64, 64), 64)
        full = pl.ds(pl.multiple_of(first_row + i * 64, 64), 64)
        at.own[n, r] = (source[me, full].astype(F32) + got[r].astype(F32)).astype(BF16)

    def view(k, part):
        columns = pl.multiple_of(lax.rem(place + k, 4) * 256, 256)
        return at.own.at[n, pl.ds(256 * part, 256), pl.ds(columns, 256)]

    ring = RingScatter(
        view,
        lambda side: at.ex_temp.at[n, side],
        lambda side, part: at.ex_block.at[n, side, part],
        lambda side: at.ex_stage.at[n, side],
        left,
        right,
        [at.ex_send.at[n, i] for i in range(6)],
        [at.ex_recv.at[n, i] for i in range(6)],
    )
    ring.start()
    yield
    yield
    ring.middle()
    yield
    yield
    ring.finish()
    out[:256] = ring.total(0).astype(BF16)
    out[256:] = ring.total(1).astype(BF16)
    ring.drain()
    swap.wait_send()


def backward_pass(grad, kept, xin, layer, tables, sel, weights, routed_own, routed):
    cosine, sine, mask = tables
    wqkv, wo, gains, router, wgu, wd = weights
    v, a = in_vmem(), in_any()
    ins = dict(
        grad=(grad, v),
        xin=(xin, v),
        gains=(gains, v),
        cosine=(cosine, v),
        sine=(sine, v),
        mask=(mask, v),
        sel=(sel, v),
        rows=(kept.rows, v),
        qkv=(kept.qkv, v),
        att=(kept.att, v),
        after=(kept.after, v),
        y=(kept.y, v),
        routed=(routed, v),
        routed_own=(routed_own, v),
        x=(kept.x_all, a),
        gu=(kept.gu, a),
        wqkv=(wqkv, a),
        wo=(wo, a),
        router=(router, a),
        wgu=(wgu, a),
        wd=(wd, a),
    )
    outs = dict(
        grad_in=((2, 32, D), F32, v),
        wide=((D, WIDE), BF16, v),
        done0=((512, 256), BF16, v),
        done1=((512, 256), BF16, v),
        done2=((512, 256), BF16, v),
    )
    scratch = dict(
        v_x=pltpu.VMEM((2, 4, 4, 32, D), BF16),
        v_g=pltpu.VMEM((2, 4, 4, 32, D), BF16),
        v_gu=pltpu.VMEM((2, 2, 512, 2 * F), BF16),
        v_wqkv=pltpu.VMEM((D, 512), BF16),
        v_wo=pltpu.VMEM((256, D), BF16),
        v_router=pltpu.VMEM((D, LANES), BF16),
        v_wgu=pltpu.VMEM((2, D, 2 * F), BF16),
        v_wd=pltpu.VMEM((2, F, D), BF16),
        load_sems=pltpu.SemaphoreType.DMA((7,)),
        small_left=pltpu.VMEM((2, 96, D), BF16),
        small_right=pltpu.VMEM((2, 96, LANES), BF16),
        small=pltpu.VMEM((D, LANES), F32),
        hs=pltpu.VMEM((2, 1024, F), BF16),
        gj=pltpu.VMEM((2, 1024, 2 * F), BF16),
        gl=pltpu.VMEM((1024, LANES), BF16),
        dgu=pltpu.VMEM((2, D, 2 * F), BF16),
        dd=pltpu.VMEM((2, F, D), BF16),
        es_sum=pltpu.VMEM((2, 32, D), F32),
        grad_after=pltpu.VMEM((2, 32, D), F32),
        ga_own=pltpu.VMEM((2, 32, D), BF16),
        ga=pltpu.VMEM((2, 128, D), BF16),
        gqkv=pltpu.VMEM((2, 128, 512), BF16),
        part=pltpu.VMEM((2, 128, D), BF16),
        own=pltpu.VMEM((3, 512, D), BF16),
        got=pltpu.VMEM((3, 512, D), BF16),
        ex_temp=pltpu.VMEM((3, 2, 256, 256), BF16),
        ex_block=pltpu.VMEM((3, 2, 2, 256, 256), BF16),
        ex_stage=pltpu.VMEM((3, 2, 256, 256), BF16),
        ex_send=pltpu.SemaphoreType.DMA((3, 6)),
        ex_recv=pltpu.SemaphoreType.DMA((3, 6)),
        swap_sems=pltpu.SemaphoreType.DMA((2, 3)),
        **TP_SCRATCH,
        **EXP_SCRATCH,
    )

    def chains(at):
        loads = {}
        for n, key in enumerate(("router", "x", "gu", "wd", "wgu", "wqkv", "wo")):
            ref = getattr(at, key)
            loads[key] = pltpu.make_async_copy(
                ref if key in ("x", "gu") else ref.at[layer],
                getattr(at, "v_" + key),
                at.load_sems.at[n],
            )
            loads[key].start()
        return [
            backward_chain(at, 0, layer, loads),
            backward_chain(at, 1, layer, loads),
            weight_chain(at),
            expert_chain(at, 0, at.dgu, at.done0, 0),
            expert_chain(at, 1, at.dgu, at.done1, 512),
            expert_chain(at, 2, at.dd, at.done2, 0),
        ]

    axes = ["tp", "x", "z", "section"]
    return one_kernel("backward%d" % layer, 12 + layer, axes, ins, outs, scratch, chains)


def rope_tables(seg_rows):
    length = seg_rows.shape[0]
    before = jnp.sum((seg_rows[None, :] < seg_rows[:, None]).astype(jnp.int32), axis=1)
    places = (jnp.arange(length, dtype=jnp.int32) - before).astype(F32)
    powers = jnp.arange(0, HD, 2, dtype=jnp.int32).astype(F32) / HD
    angles = places[:, None] * (ROPE_BASE ** (-powers))[None, :]
    cosine, sine = jnp.cos(angles), jnp.sin(angles)
    indices = jnp.arange(length, dtype=jnp.int32)
    allowed = (seg_rows[:, None] == seg_rows[None, :]) & (indices[None, :] <= indices[:, None])
    return (
        jnp.concatenate([cosine] * 4, axis=1),
        jnp.concatenate([-sine, sine, -sine, sine], axis=1),
        allowed.astype(F32),
    )


def routed(routes):
    labels = jnp.arange(LANES, dtype=jnp.int32)
    return jnp.sum((routes[:, :, None] == labels[None, None, :]).astype(F32), axis=1)


def per_device(
    activations,
    cotangent,
    segments,
    routes,
    attention_gain,
    query_weight,
    key_weight,
    value_weight,
    output_weight,
    mixture_gain,
    router_weight,
    expert_gate_up,
    expert_down,
):
    section = lax.axis_index("section")
    expert = lax.axis_index("exp")

    def own_batches(array):
        return lax.dynamic_slice_in_dim(array, 2 * section, 2, 0)

    def to_owner(first, second):
        sent = jnp.where(section == 0, second, first)
        kept = jnp.where(section == 0, first, second)
        return kept, lax.ppermute(sent, "section", [(0, 1), (1, 0)])

    def by_layer(first, second):
        kept, got = to_owner(first, second)
        kept, got = kept.reshape(2, 32, D), got.reshape(2, 32, D)
        return jnp.where(
            section == 0,
            jnp.concatenate([kept, got], axis=0),
            jnp.concatenate([got, kept], axis=0),
        )[None]

    qkv_own = jnp.concatenate([query_weight, key_weight, value_weight], axis=2)
    gains_own = jnp.concatenate(
        [attention_gain, mixture_gain, jnp.zeros((6, D), BF16)], axis=0
    ).astype(F32)[None]
    router_own = jnp.pad(router_weight, ((0, 0), (0, 0), (0, LANES - E)))
    (paired,) = fuse([pair_part([qkv_own, output_weight, gains_own, router_own])], 0, "pair")
    weights = tuple(paired) + (expert_gate_up, expert_down)

    cosine, sine, mask = jax.vmap(rope_tables)(own_batches(segments))
    tables = (cosine.reshape(256, LANES), sine.reshape(256, LANES), mask)
    routes_own = own_batches(routes).reshape(64, 8)
    lanes = lax.broadcasted_iota(jnp.int32, (8, LANES), 1)
    sel = (lanes == 2 * expert + lax.broadcasted_iota(jnp.int32, (8, LANES), 0)).astype(F32)
    routed_own = routed(routes_own)
    doubled = jnp.concatenate([routed_own] * 2, axis=1).astype(BF16).reshape(2, 32, 2 * LANES)

    start = own_batches(activations)
    made = forward_pass(start, 0, tables, sel, weights, doubled, None)
    out_first = made.out
    weights = tuple(paired) + (made.wgu, made.wd)
    routed_all = made.routed[..., :LANES]
    kept = forward_pass(out_first, 1, tables, sel, weights, None, made.routed)
    out_second = kept.out

    shared = (tables, sel, weights, doubled, made.routed)
    grad = own_batches(cotangent)
    second = backward_pass(grad, kept, out_first, 1, *shared)
    grad_second = second.grad_in
    first = backward_pass(grad_second.astype(BF16), made, start, 0, *shared)
    grad_first = first.grad_in
    ((dw, small),) = fuse([settle_part(first.wide, second.wide)], 6, "settle")
    done_first = (first.done0, first.done1, first.done2)
    done_second = (second.done0, second.done1, second.done2)
    small = small.reshape(D, LANES)
    experts = []
    for one, two in zip(done_first, done_second):
        kept, got = to_owner(one, two)
        kept, got = kept.astype(F32), got.astype(F32)
        experts.append(
            jnp.where(section == 0, jnp.stack([kept, got]), jnp.stack([got, kept]))[None]
        )
    return (
        by_layer(out_first.reshape(64, D), out_second.reshape(64, D)),
        by_layer(grad_first.reshape(64, D), grad_second.reshape(64, D)),
        small[:, E][None],
        dw[None, :, :256],
        dw[None, :, 256:384],
        dw[None, :, 384:512],
        dw[:, 512:].T[None],
        small[:, E + 1][None],
        small[None, :, :E],
        jnp.concatenate(experts[:2], axis=2),
        experts[2],
    )


def solution(mesh):
    placed = (
        P(None, ("exp", "tp"), None),
        P(None, ("exp", "tp"), None),
        P(None, "exp"),
        P(None, ("exp", "tp"), None),
        P("section", None),
        P("section", None, "tp"),
        P("section", None, "tp"),
        P("section", None, "tp"),
        P("section", "tp", None),
        P("section", None),
        P("section", None, None),
        P("section", "exp", None, None),
        P("section", "exp", None, None),
    )
    return jax.shard_map(
        per_device,
        mesh=mesh,
        in_specs=placed,
        out_specs=(
            P("section", None, ("exp", "tp"), None),
            P("section", None, ("exp", "tp"), None),
            P("section", None),
            P("section", "exp", "tp"),
            P("section", "exp", "tp"),
            P("section", "exp", "tp"),
            P("section", "tp", "exp"),
            P("section", None),
            P("section", None, None),
            P("section", "exp", None, "tp"),
            P("section", "exp", None, "tp"),
        ),
        check_vma=False,
    )
```

```python
import functools

import jax
import jax.numpy as jnp
from jax import lax
from jax.experimental import pallas as pl
from jax.experimental.pallas import tpu as pltpu
from jax.sharding import PartitionSpec as P

D = 1024
HD = 64
E = 32
F = 512
LANES = 128
EPSILON = 1e-06
ROPE_BASE = 10000.0
SCORE_SCALE = 0.125
MASKED = -1e30
MESH = pl.DeviceIdType.MESH
VMEM_LIMIT = 62 * 1024 * 1024
BF16 = jnp.bfloat16
F32 = jnp.float32


def dot(a, b):
    return jnp.dot(a, b, preferred_element_type=F32)


def dot_nt(a, b):
    return lax.dot_general(a, b, (((1,), (1,)), ((), ())), preferred_element_type=F32)


def dot_tn(a, b):
    return lax.dot_general(a, b, (((0,), (0,)), ((), ())), preferred_element_type=F32)


def in_vmem():
    return pl.BlockSpec(memory_space=pltpu.VMEM)


def in_any():
    return pl.BlockSpec(memory_space=pl.ANY)


def greet(peers):
    barrier = pltpu.get_barrier_semaphore()
    for peer in peers:
        pl.semaphore_signal(barrier, inc=1, device_id=peer, device_id_type=MESH)
    pl.semaphore_wait(barrier, len(peers))


def remote(src, dst, send_sem, recv_sem, peer):
    return pltpu.make_async_remote_copy(
        src_ref=src,
        dst_ref=dst,
        send_sem=send_sem,
        recv_sem=recv_sem,
        device_id=peer,
        device_id_type=MESH,
    )


def comm_params(number):
    return pltpu.CompilerParams(
        collective_id=number, has_side_effects=True, vmem_limit_bytes=VMEM_LIMIT
    )


class Part:
    def __init__(self, arrays, in_specs, out_shapes, out_specs, scratch, axes, body):
        self.arrays, self.in_specs = arrays, in_specs
        self.out_shapes, self.out_specs = out_shapes, out_specs
        self.scratch, self.axes, self.body = scratch, axes, body


def around(axis):
    if axis == "section":
        return [{"section": 1 - lax.axis_index("section")}]
    if axis == "tp":
        return [{"tp": lax.rem(lax.axis_index("tp") + j, 4)} for j in (3, 1)]
    if axis == "tp_all":
        return tp_peers()
    at_x, at_z = axis_spots()
    line_only = [(i, 0) for i in (1, 2, 3)] + [(0, i) for i in (1, 2, 3)]
    others = [(i, j) for i in range(4) for j in range(4) if i or j]
    return [
        {"exp": lax.rem(at_x + i, 4) * 4 + lax.rem(at_z + j, 4)}
        for i, j in (line_only if axis == "exp_lines" else others)
    ]


def fused_kernel(parts, *refs):
    refs = list(refs)

    def take(count):
        taken = refs[:count]
        del refs[:count]
        return taken

    ins = [take(len(part.arrays)) for part in parts]
    outs = [take(len(part.out_shapes)) for part in parts]
    scratch = [take(len(part.scratch)) for part in parts]
    axes = []
    for part in parts:
        axes += [axis for axis in part.axes if axis not in axes]
    greet([peer for axis in axes for peer in around(axis)])
    running = [part.body(i, o, s) for part, i, o, s in zip(parts, ins, outs, scratch)]
    while running:
        for one in list(running):
            if next(one, "end") == "end":
                running.remove(one)


def fuse(parts, number, name):
    outs = pl.pallas_call(
        functools.partial(fused_kernel, parts),
        out_shape=[o for part in parts for o in part.out_shapes],
        in_specs=[s for part in parts for s in part.in_specs],
        out_specs=[s for part in parts for s in part.out_specs],
        scratch_shapes=[s for part in parts for s in part.scratch],
        compiler_params=comm_params(number),
        name=name,
    )(*[a for part in parts for a in part.arrays])
    outs = list(outs)
    results = []
    for part in parts:
        count = len(part.out_shapes)
        results.append(outs[:count] if count > 1 else outs[0])
        outs = outs[count:]
    return results


def sems(*shape):
    return [pltpu.SemaphoreType.DMA(shape)] * 2


def pair_part(arrays):
    count = len(arrays)

    def body(ins, outs, scratch):
        held, (send, recv, read, write) = scratch[:count], scratch[count:]
        me = lax.axis_index("section")
        (peer,) = around("section")
        sends, reads, writes = [], [], []
        for at in range(count):
            sends.append(remote(ins[at].at[0], outs[at].at[me], send.at[at], recv.at[at], peer))
            reads.append(pltpu.make_async_copy(ins[at].at[0], held[at], read.at[at]))
            writes.append(pltpu.make_async_copy(held[at], outs[at].at[me], write.at[at]))
            sends[-1].start()
            reads[-1].start()
        yield
        for at in range(count):
            reads[at].wait()
            writes[at].start()
        yield
        yield
        yield
        for at in range(count):
            writes[at].wait()
            sends[at].wait()

    return Part(
        arrays,
        [in_any()] * count,
        [jax.ShapeDtypeStruct((2,) + a.shape[1:], a.dtype) for a in arrays],
        [in_any()] * count,
        [pltpu.VMEM(a.shape[1:], a.dtype) for a in arrays]
        + [pltpu.SemaphoreType.DMA((count,))] * 4,
        ["section"],
        body,
    )


class RingScatter:
    def __init__(self, view, temp, block, stage, left, right, send, recv):
        self.view, self.temp, self.block, self.stage = view, temp, block, stage
        self.left, self.right, self.send, self.recv = left, right, send, recv
        self.copies = []

    def go(self, src, dst, at, peer):
        copy = remote(src, dst, self.send[at], self.recv[at], peer)
        copy.start()
        self.copies.append(copy)

    def start(self):
        self.go(self.view(2, 0), self.temp(0), 0, self.right)
        self.go(self.view(2, 1), self.temp(1), 1, self.left)
        self.go(self.view(1, 1), self.block(0, 1), 2, self.right)
        self.go(self.view(3, 0), self.block(1, 0), 3, self.left)

    def middle(self):
        for side, nearer, peer in ((0, 1, self.right), (1, 3, self.left)):
            self.copies[side].wait_recv()
            term = self.view(nearer, side)[...].astype(F32) + self.temp(side)[...].astype(F32)
            self.stage(side)[...] = term.astype(BF16)
            self.go(self.stage(side), self.block(side, side), 4 + side, peer)

    def finish(self):
        for copy in self.copies[2:]:
            copy.wait_recv()

    def total(self, part):
        return (
            self.view(0, part)[...].astype(F32)
            + self.block(0, part)[...].astype(F32)
            + self.block(1, part)[...].astype(F32)
        )

    def drain(self):
        for copy in self.copies:
            copy.wait_send()


def half_swapped(values):
    width = values.shape[1]
    lane = lax.broadcasted_iota(jnp.int32, values.shape, 1)
    ahead = pltpu.roll(values, width - 32, 1)
    behind = pltpu.roll(values, 32, 1)
    return jnp.where(lax.rem(lane, 64) < 32, ahead, behind)


def three(table):
    return jnp.concatenate([table, table, table], axis=1)


def head(values, batch, first):
    return values[batch * 128 : batch * 128 + 128, first : first + HD]


def masked_softmax(logits, mask):
    routed = mask > 0.5
    shown = jnp.where(routed, logits, MASKED)
    lifted = jnp.where(routed, jnp.exp(shown - jnp.max(shown, axis=1, keepdims=True)), 0.0)
    return lifted / jnp.sum(lifted, axis=1, keepdims=True)


def inverse_rms(values):
    return lax.rsqrt(jnp.mean(values * values, axis=1, keepdims=True) + EPSILON)


class Names:
    pass


def take_turns(running):
    running = list(running)
    while running:
        for one in list(running):
            if next(one, "end") == "end":
                running.remove(one)


def one_kernel(name, number, axes, ins, outs, scratch, chains):
    names = list(ins) + list(outs) + list(scratch)

    def kernel(*refs):
        at = Names()
        for key, ref in zip(names, refs):
            setattr(at, key, ref)
        greet([peer for axis in axes for peer in around(axis)])
        take_turns(chains(at))

    results = pl.pallas_call(
        kernel,
        out_shape=[jax.ShapeDtypeStruct(o[0], o[1]) for o in outs.values()],
        in_specs=[i[1] for i in ins.values()],
        out_specs=[o[2] for o in outs.values()],
        scratch_shapes=list(scratch.values()),
        compiler_params=comm_params(number),
        name=name,
    )(*[i[0] for i in ins.values()])
    made = Names()
    for key, result in zip(outs, results):
        setattr(made, key, result)
    return made


def chain_tp_block(ref, c, k, part):
    place = lax.rem(lax.axis_index("tp") + k, 4)
    if part is None:
        return ref.at[c, pl.ds(pl.multiple_of(place * 32, 32), 32)]
    return ref.at[c, pl.ds(pl.multiple_of(place * 32 + 16 * part, 16), 16)]


def tp_peers():
    me = lax.axis_index("tp")
    return [{"tp": lax.rem(me + j, 4)} for j in (1, 3, 2)]


def chain_tp_gather(own, ref, c, send, recv):
    spot = chain_tp_block(ref, c, 0, None)
    copies = [
        remote(own, spot, send.at[c, n], recv.at[c, n], peer) for n, peer in enumerate(tp_peers())
    ]
    for copy in copies:
        copy.start()
    spot[...] = own[...]
    yield
    for copy in copies:
        copy.wait()


def chain_tp_scatter(ref, c, held, send, recv, out):
    copies = []
    for n, (by, peer) in enumerate(zip((1, 3, 2), tp_peers())):
        block = chain_tp_block(ref, c, by, None)
        copies.append(remote(block, held.at[c, n], send.at[c, n], recv.at[c, n], peer))
        copies[-1].start()
    yield
    total = chain_tp_block(ref, c, 0, None)[...].astype(F32)
    for n in range(3):
        copies[n].wait_recv()
        total = total + held[c, n].astype(F32)
    out[c] = total
    for copy in copies:
        copy.wait_send()


TP_SCRATCH = dict(
    tp_held=pltpu.VMEM((2, 3, 32, D), BF16),
    tp_sum=pltpu.VMEM((2, 32, D), F32),
    tp_send=pltpu.SemaphoreType.DMA((2, 3)),
    tp_recv=pltpu.SemaphoreType.DMA((2, 3)),
    tg_send=pltpu.SemaphoreType.DMA((2, 3)),
    tg_recv=pltpu.SemaphoreType.DMA((2, 3)),
)


def chain_block(ref, c, half, i, j, part, width):
    me = lax.axis_index("exp")
    at_x, at_z = me // 4, lax.rem(me, 4)
    i, j = (i, j) if half == 0 else (j, i)
    rows = pl.ds(0, 32) if part is None else pl.ds(16 * part, 16)
    columns = pl.ds(width * half, width)
    return ref.at[c, lax.rem(at_x + i, 4), lax.rem(at_z + j, 4), rows, columns]


def axis_spots():
    me = lax.axis_index("exp")
    return me // 4, lax.rem(me, 4)


def axis_peers(axis):
    at_x, at_z = axis_spots()
    if axis == 0:
        return [{"exp": lax.rem(at_x + j, 4) * 4 + at_z} for j in (1, 3, 2)]
    return [{"exp": at_x * 4 + lax.rem(at_z + j, 4)} for j in (1, 3, 2)]


def line(ref, c, half, columns, by=None):
    spot = axis_spots()[half]
    spot = spot if by is None else lax.rem(spot + by, 4)
    if half == 0:
        return ref.at[c, spot, :, :, columns]
    return ref.at[c, :, spot, :, columns]


def direct_gather(own, ref, c, send, recv, width=512):
    first, second = [], []
    for half in range(2):
        columns = pl.ds(width * half, width)
        spot = chain_block(ref, c, half, 0, 0, None, width)
        peers = axis_peers(half)
        for n in range(3):
            copy = remote(
                own.at[:, columns], spot, send.at[c, half, 0, n], recv.at[c, half, 0, n], peers[n]
            )
            copy.start()
            first.append(copy)
        spot[...] = own[:, columns]
    yield
    for half in range(2):
        columns = pl.ds(width * half, width)
        for copy in first[3 * half : 3 * half + 3]:
            copy.wait_recv()
        blocks = line(ref, c, 1 - half, columns)
        peers = axis_peers(1 - half)
        for n in range(3):
            copy = remote(
                blocks, blocks, send.at[c, half, 1, n], recv.at[c, half, 1, n], peers[n]
            )
            copy.start()
            second.append(copy)
    yield
    for copy in second:
        copy.wait_recv()
    for copy in first + second:
        copy.wait_send()


def direct_scatter(ref, c, held, ready, last, send, recv, out, slot=None):
    slot = c if slot is None else slot
    first, second = [], []
    for half in range(2):
        columns = pl.ds(512 * half, 512)
        peers = axis_peers(half)
        for n, by in enumerate((1, 3, 2)):
            copy = remote(
                line(ref, slot, half, columns, by),
                held.at[c, half, n],
                send.at[c, half, 0, n],
                recv.at[c, half, 0, n],
                peers[n],
            )
            copy.start()
            first.append(copy)
    yield
    for half in range(2):
        columns = pl.ds(512 * half, 512)
        for copy in first[3 * half : 3 * half + 3]:
            copy.wait_recv()
        total = line(ref, slot, half, columns)[...].astype(F32)
        for n in range(3):
            total = total + held[c, half, n].astype(F32)
        ready[c, half] = total.astype(BF16)
        peers = axis_peers(1 - half)
        spot = axis_spots()[1 - half]
        for n, by in enumerate((1, 3, 2)):
            copy = remote(
                ready.at[c, half, lax.rem(spot + by, 4)],
                last.at[c, half, n],
                send.at[c, half, 1, n],
                recv.at[c, half, 1, n],
                peers[n],
            )
            copy.start()
            second.append(copy)
    yield
    for half in range(2):
        total = ready[c, half, axis_spots()[1 - half]].astype(F32)
        for n in range(3):
            second[3 * half + n].wait_recv()
            total = total + last[c, half, n].astype(F32)
        out[c, :, pl.ds(512 * half, 512)] = total
    for copy in first + second:
        copy.wait_send()


EXP_SCRATCH = dict(
    es_held=pltpu.VMEM((2, 2, 3, 4, 32, 512), BF16),
    es_line=pltpu.VMEM((2, 2, 4, 32, 512), BF16),
    es_last=pltpu.VMEM((2, 2, 3, 32, 512), BF16),
    es_made=pltpu.VMEM((2, 4, 4, 32, D), BF16),
    es_send=pltpu.SemaphoreType.DMA((2, 2, 2, 3)),
    es_recv=pltpu.SemaphoreType.DMA((2, 2, 2, 3)),
    eg_send=pltpu.SemaphoreType.DMA((2, 2, 2, 3)),
    eg_recv=pltpu.SemaphoreType.DMA((2, 2, 2, 3)),
)
def rope(values, cosine, sine):
    return values * three(cosine) + half_swapped(values) * three(sine)


def unrope(values, cosine, sine):
    return values * three(cosine) - half_swapped(values) * three(sine)


def shares(q, k, allowed):
    scores = jnp.where(allowed, dot_nt(q, k) * SCORE_SCALE, MASKED)
    lifted = jnp.exp(scores - jnp.max(scores, axis=1, keepdims=True))
    return lifted / jnp.sum(lifted, axis=1, keepdims=True)


def forward_chain(at, c, layer, loads):
    x = at.xin[c].astype(F32)
    at.normed[c] = (x * inverse_rms(x) * at.gains[layer, 0:1]).astype(BF16)
    yield from chain_tp_gather(at.normed.at[c], at.rows, c, at.tg_send, at.tg_recv)
    if c == 0:
        loads["wqkv"].wait()
        loads["wo"].wait()
    joined = dot(at.rows[c], at.v_wqkv[...])
    spot = slice(c * 128, c * 128 + 128)
    turned = rope(joined[:, :384], at.cosine[spot], at.sine[spot])
    qkv = jnp.concatenate([turned, joined[:, 384:]], axis=1).astype(BF16)
    at.qkv[c] = qkv
    allowed = at.mask[c] > 0.5
    outs = []
    for h in range(4):
        kv = h // 2
        share = shares(head(qkv, 0, h * HD), head(qkv, 0, 256 + kv * HD), allowed)
        outs.append(dot(share.astype(BF16), head(qkv, 0, 384 + kv * HD)))
    attended = jnp.concatenate(outs, axis=1).astype(BF16)
    at.att[c] = attended
    at.part[c] = dot(attended, at.v_wo[...]).astype(BF16)
    yield from chain_tp_scatter(
        at.part, c, at.tp_held, at.tp_send, at.tp_recv, at.tp_sum
    )
    after = x + at.tp_sum[c]
    at.after[c] = after
    at.normed_two[c] = (after * inverse_rms(after) * at.gains[layer, 1:2]).astype(BF16)
    yield from direct_gather(at.normed_two.at[c], at.v_x, c, at.eg_send, at.eg_recv)
    at.saves[c].start()
    if c == 0:
        for key in ("router", "wgu", "wd"):
            loads[key].wait()
    for tile in range(2):
        pair = pl.ds(2 * tile, 2)
        rows = pl.ds(256 * tile, 256)
        xt = at.v_x[c, pair].reshape(256, D)
        gates = masked_softmax(
            dot(xt, at.v_router[...]), at.routed[c, pair, :, :, :LANES].reshape(256, LANES).astype(F32)
        )
        total = None
        for e in range(2):
            gate = jnp.sum(gates * at.sel[e : e + 1], axis=1, keepdims=True)
            gu = dot(xt, at.v_wgu[e])
            at.v_gu[c, e, rows] = gu.astype(BF16)
            part, upper = gu[:, :F], gu[:, F:]
            hidden = part * jax.nn.sigmoid(part) * upper
            made = dot((hidden * gate).astype(BF16), at.v_wd[e])
            total = made if total is None else total + made
        at.es_made[c, pair] = total.astype(BF16).reshape(2, 4, 32, D)
    at.saves[2 + c].start()
    yield from direct_scatter(
        at.es_made, c, at.es_held, at.es_line, at.es_last, at.es_send, at.es_recv, at.y
    )
    at.out[c] = (at.after[c] + at.y[c]).astype(BF16)
    at.saves[c].wait()
    at.saves[2 + c].wait()


def mask_chain(at, c):
    yield from direct_gather(
        at.routed_own.at[c], at.routed, c, at.mg_send, at.mg_recv, width=LANES
    )


def pair_chain(at, loads):
    me = lax.axis_index("section")
    (peer,) = around("section")
    sends, reads, writes = [], [], []
    pieces = ((at.own_gu, at.held_gu, at.wgu), (at.own_d, at.held_d, at.wd))
    for n, (own, held, both) in enumerate(pieces):
        sends.append(
            remote(own.at[0], both.at[me], at.pair_sems.at[0, n], at.pair_sems.at[1, n], peer)
        )
        reads.append(pltpu.make_async_copy(own.at[0], held, at.pair_sems.at[2, n]))
        writes.append(pltpu.make_async_copy(held, both.at[me], at.pair_sems.at[3, n]))
        sends[-1].start()
        reads[-1].start()
    yield
    for n in range(2):
        reads[n].wait()
        writes[n].start()
    yield
    yield
    for n in range(2):
        writes[n].wait()
        sends[n].wait()
    loads["wgu"].start()
    loads["wd"].start()


def forward_pass(xin, layer, tables, sel, weights, routed_own, routed):
    cosine, sine, mask = tables
    wqkv, wo, gains, router, wgu, wd = weights
    swap = layer == 0
    v, a = in_vmem(), in_any()
    ins = dict(
        xin=(xin, v),
        gains=(gains, v),
        cosine=(cosine, v),
        sine=(sine, v),
        mask=(mask, v),
        sel=(sel, v),
        wqkv=(wqkv, a),
        wo=(wo, a),
        router=(router, a),
    )
    if swap:
        ins.update(routed_own=(routed_own, v), own_gu=(wgu, a), own_d=(wd, a))
    else:
        ins.update(routed=(routed, v), wgu=(wgu, a), wd=(wd, a))
    outs = dict(
        out=((2, 32, D), BF16, v),
        rows=((2, 128, D), BF16, v),
        qkv=((2, 128, 512), BF16, v),
        att=((2, 128, 256), BF16, v),
        after=((2, 32, D), F32, v),
        y=((2, 32, D), F32, v),
        x_all=((2, 4, 4, 32, D), BF16, a),
        gu=((2, 2, 512, 2 * F), BF16, a),
    )
    scratch = dict(
        normed=pltpu.VMEM((2, 32, D), BF16),
        normed_two=pltpu.VMEM((2, 32, D), BF16),
        part=pltpu.VMEM((2, 128, D), BF16),
        v_wqkv=pltpu.VMEM((D, 512), BF16),
        v_wo=pltpu.VMEM((256, D), BF16),
        v_router=pltpu.VMEM((D, LANES), BF16),
        v_wgu=pltpu.VMEM((2, D, 2 * F), BF16),
        v_wd=pltpu.VMEM((2, F, D), BF16),
        v_x=pltpu.VMEM((2, 4, 4, 32, D), BF16),
        v_gu=pltpu.VMEM((2, 2, 512, 2 * F), BF16),
        load_sems=pltpu.SemaphoreType.DMA((5,)),
        save_sems=pltpu.SemaphoreType.DMA((4,)),
        **TP_SCRATCH,
        **EXP_SCRATCH,
    )
    if swap:
        outs.update(
            wgu=((2, 2, D, 2 * F), BF16, a),
            wd=((2, 2, F, D), BF16, a),
            routed=((2, 4, 4, 32, 2 * LANES), BF16, v),
        )
        scratch.update(
            held_gu=pltpu.VMEM((2, D, 2 * F), BF16),
            held_d=pltpu.VMEM((2, F, D), BF16),
            pair_sems=pltpu.SemaphoreType.DMA((4, 2)),
            mg_send=pltpu.SemaphoreType.DMA((2, 2, 2, 3)),
            mg_recv=pltpu.SemaphoreType.DMA((2, 2, 2, 3)),
        )

    def chains(at):
        loads = {}
        for n, key in enumerate(("wqkv", "wo", "router", "wgu", "wd")):
            loads[key] = pltpu.make_async_copy(
                getattr(at, key).at[layer], getattr(at, "v_" + key), at.load_sems.at[n]
            )
        at.saves = [
            pltpu.make_async_copy(src.at[c], dst.at[c], at.save_sems.at[2 * n + c])
            for n, (src, dst) in enumerate(((at.v_x, at.x_all), (at.v_gu, at.gu)))
            for c in range(2)
        ]
        for key in ("wqkv", "wo", "router") if swap else loads:
            loads[key].start()
        running = [forward_chain(at, c, layer, loads) for c in range(2)]
        if swap:
            running = [pair_chain(at, loads), mask_chain(at, 0), mask_chain(at, 1)] + running
        return running

    axes = ["tp_all", "exp_lines"] + (["section"] if swap else [])
    return one_kernel("forward%d" % layer, 10 + layer, axes, ins, outs, scratch, chains)


def rms_back(q, values, gain):
    inverse = inverse_rms(values)
    scaled = q * gain
    back = inverse * scaled - values * inverse**3 * jnp.mean(values * scaled, axis=1, keepdims=True)
    return back, q * values * inverse


def backward_chain(at, c, layer, loads):
    gather = direct_gather(at.grad.at[c], at.v_g, c, at.eg_send, at.eg_recv)
    next(gather)
    after = at.after[c]
    normed_two = (after * inverse_rms(after) * at.gains[layer, 1:2]).astype(BF16)
    if c == 0:
        loads["router"].wait()
    own_gates = masked_softmax(
        dot(normed_two, at.v_router[...]), at.routed_own[c, :, :LANES].astype(F32)
    )
    gf = at.grad[c].astype(F32)
    gc = (-own_gates * jnp.sum(gf * at.y[c], axis=1, keepdims=True)).astype(BF16)
    lane = lax.broadcasted_iota(jnp.int32, (32, LANES), 1)
    at.small_left[c, 0:32] = normed_two
    at.small_right[c, 0:32] = gc
    at.small_right[c, 32:64] = jnp.where(lane == E + 1, 1.0, 0.0).astype(BF16)
    at.small_right[c, 64:96] = jnp.where(lane == E, 1.0, 0.0).astype(BF16)
    yield
    yield from gather
    if c == 0:
        for key in ("x", "gu", "wd", "wgu"):
            loads[key].wait()
    for tile in range(2):
        pair = pl.ds(2 * tile, 2)
        rows = pl.ds(256 * tile, 256)
        both = pl.ds(512 * c + 256 * tile, 256)
        xt = at.v_x[c, pair].reshape(256, D)
        gt = at.v_g[c, pair].reshape(256, D)
        gates = masked_softmax(
            dot(xt, at.v_router[...]),
            at.routed[c, pair, :, :, :LANES].reshape(256, LANES).astype(F32),
        )
        gl, total = None, None
        for e in range(2):
            chosen = at.sel[e : e + 1]
            gate = jnp.sum(gates * chosen, axis=1, keepdims=True)
            gh = dot_nt(gt, at.v_wd[e])
            part = at.v_gu[c, e, rows, :F].astype(F32)
            upper = at.v_gu[c, e, rows, F:].astype(F32)
            s = jax.nn.sigmoid(part)
            act = part * s
            hidden = act * upper
            term = (gate * jnp.sum(hidden * gh, axis=1, keepdims=True)) * chosen
            gl = term if gl is None else gl + term
            at.hs[e, both] = (hidden * gate).astype(BF16)
            gh = gh * gate
            at.gj[e, both, :F] = (gh * upper * (s + act * (1.0 - s))).astype(BF16)
            at.gj[e, both, F:] = (gh * act).astype(BF16)
            dx = dot_nt(at.gj[e, both], at.v_wgu[e])
            total = dx if total is None else total + dx
        gl = gl.astype(BF16)
        at.gl[both] = gl
        total = total + dot_nt(gl, at.v_router[...])
        at.es_made[c, pair] = total.astype(BF16).reshape(2, 4, 32, D)
    yield from direct_scatter(
        at.es_made, c, at.es_held, at.es_line, at.es_last, at.es_send, at.es_recv, at.es_sum
    )
    grad_n = at.es_sum[c] + dot_nt(at.small_right[c, 0:32], at.v_router[...])
    back, term = rms_back(grad_n, at.after[c], at.gains[layer, 1:2])
    at.small_left[c, 32:64] = term.astype(BF16)
    grad_after = at.grad[c].astype(F32) + back
    at.grad_after[c] = grad_after
    at.ga_own[c] = grad_after.astype(BF16)
    yield from chain_tp_gather(at.ga_own.at[c], at.ga, c, at.tg_send, at.tg_recv)
    if c == 0:
        loads["wqkv"].wait()
        loads["wo"].wait()
    gatt = dot_nt(at.ga[c], at.v_wo[...]).astype(BF16)
    qkv = at.qkv[c]
    allowed = at.mask[c] > 0.5
    gqs, gks, gvs = [], [None, None], [None, None]
    for h in range(4):
        kv = h // 2
        q = head(qkv, 0, h * HD)
        k = head(qkv, 0, 256 + kv * HD)
        v = head(qkv, 0, 384 + kv * HD)
        go = head(gatt, 0, h * HD)
        share = shares(q, k, allowed)
        gp = dot_nt(go, v)
        gs = (share * (gp - jnp.sum(share * gp, axis=1, keepdims=True))).astype(BF16)
        gqs.append(dot(gs, k) * SCORE_SCALE)
        gk = dot_tn(gs, q) * SCORE_SCALE
        gv = dot_tn(share.astype(BF16), go)
        gks[kv] = gk if gks[kv] is None else gks[kv] + gk
        gvs[kv] = gv if gvs[kv] is None else gvs[kv] + gv
    joined = jnp.concatenate(gqs + gks + gvs, axis=1)
    spot = slice(c * 128, c * 128 + 128)
    turned = unrope(joined[:, :384], at.cosine[spot], at.sine[spot])
    gqkv = jnp.concatenate([turned, joined[:, 384:]], axis=1).astype(BF16)
    at.gqkv[c] = gqkv
    at.part[c] = dot_nt(gqkv, at.v_wqkv[...]).astype(BF16)
    yield from chain_tp_scatter(
        at.part, c, at.tp_held, at.tp_send, at.tp_recv, at.tp_sum
    )
    back, term = rms_back(at.tp_sum[c], at.xin[c].astype(F32), at.gains[layer, 0:1])
    at.small_left[c, 64:96] = term.astype(BF16)
    at.grad_in[c] = at.grad_after[c] + back


def weight_chain(at):
    yield
    yield

    def joint(e, tile):
        columns = pl.ds(256 * tile, 256)
        x = at.v_x[:, :, :, :, columns].reshape(1024, 256)
        at.dgu[e, columns] = dot_tn(x, at.gj[e]).astype(BF16)

    for chunk in range(2):
        for e in range(2):
            for tile in range(2):
                joint(e, 2 * chunk + tile)
        yield
    for e in range(2):
        for tile in range(2):
            columns = pl.ds(256 * tile, 256)
            g = at.v_g[...].reshape(1024, D)
            at.dd[e, columns] = dot_tn(at.hs[e, :, columns], g).astype(BF16)
    yield
    x = at.v_x[...].reshape(1024, D)
    at.small[...] = dot_tn(x, at.gl[...])

    def put(first, last, value):
        value = value.astype(BF16).reshape(4, 4, 2, 32, last - first)
        for half in range(2):
            at.wide[half, :, :, :, first:last] = value[:, :, half]

    ga = at.ga[...].reshape(256, D)
    put(512, 768, dot_tn(ga, at.att[...].reshape(256, 256)))
    rows = at.rows[...].reshape(256, D)
    put(0, 512, dot_tn(rows, at.gqkv[...].reshape(256, 512)))
    yield
    left = at.small_left[...].reshape(192, D)
    right = at.small_right[...].reshape(192, LANES)
    put(768, 896, at.small[...] + dot_tn(left, right))
    put(896, 1024, jnp.zeros((D, LANES), F32))


def settle_chain(at, n, wide, summed, wait):
    for _ in range(wait):
        yield
    me = lax.axis_index("section")
    (peer,) = around("section")
    swap = remote(
        wide.at[1 - me], at.se_got, at.se_swap.at[0, n], at.se_swap.at[1, n], peer
    )
    swap.start()
    own = pltpu.make_async_copy(wide.at[me], summed.at[0], at.se_swap.at[2, n])
    own.start()
    yield
    own.wait()
    swap.wait_recv()

    @pl.loop(0, 4)
    def _(x):
        summed[0, x] = (summed[0, x].astype(F32) + at.se_got[x].astype(F32)).astype(BF16)

    yield from direct_scatter(
        summed,
        n,
        at.se_held,
        at.se_line,
        at.se_last,
        at.se_send,
        at.se_recv,
        at.se_out,
        slot=0,
    )
    swap.wait_send()
    piece = at.se_piece.at[n]
    piece[...] = at.se_out[n, :, 768:896]
    partners = tp_peers()
    sent = [
        remote(piece, at.sp_held.at[n, k], at.sp_send.at[n, k], at.sp_recv.at[n, k], partner)
        for k, partner in enumerate(partners)
    ]
    for copy in sent:
        copy.start()
    yield
    for copy in sent:
        copy.wait()
    at.se_total[n] = piece[...] + ((at.sp_held[n, 0] + at.sp_held[n, 1]) + at.sp_held[n, 2])
    expert = lax.axis_index("exp")
    whole_small = at.se_small.at[n]
    sent = [
        remote(
            at.se_total.at[n],
            whole_small.at[expert],
            at.sg_send.at[n, k],
            at.sg_recv.at[n, k],
            {"exp": lax.rem(expert + k + 1, 16)},
        )
        for k in range(15)
    ]
    for copy in sent:
        copy.start()
    whole_small[expert] = at.se_total[n]
    yield
    for copy in sent:
        copy.wait()


def swap_chain(at, k, wait, kept, got, write):
    for _ in range(wait):
        yield
    me = lax.axis_index("section")
    (peer,) = around("section")
    if k < 3:
        at.late[k].wait()
    swap = remote(kept.at[1 - me], got, at.last_swap.at[0, k], at.last_swap.at[1, k], peer)
    swap.start()
    write(me, kept.at[me])
    yield
    swap.wait_recv()
    write(1 - me, got)
    swap.wait_send()


def rows_swap(at, k, wait, out):
    kept, got = (at.all_out, at.got_out) if k == 0 else (at.all_grad, at.got_grad)

    def write(core, ref):
        out[pl.ds(2 * core, 2)] = ref[...]

    return swap_chain(at, k, wait, kept, got, write)


def expert_swap(at, wait):
    def write(core, ref):
        at.grad_gu[core] = ref[0:1024].astype(F32)
        at.grad_d[core] = ref[1024:1536].astype(F32)

    return swap_chain(at, 2, wait, at.all_done, at.got_done, write)


def attention_swap(at, wait):
    def write(core, ref):
        at.grad_wide[pl.ds(pl.multiple_of(32 * core, 32), 32)] = ref[...]

    return swap_chain(at, 3, wait, at.se_out, at.got_wide, write)


def small_swap(at, wait):
    def write(core, ref):
        at.grad_small[:, pl.ds(pl.multiple_of(32 * core, 32), 32)] = ref[...]

    return swap_chain(at, 4, wait, at.se_small, at.got_small, write)


def expert_chain(at, n, source, out, first_row):
    for _ in range(2 + n):
        yield
    rows = pl.ds(first_row, 512)
    me = lax.axis_index("section")
    place = lax.axis_index("tp")
    left, right = around("tp")
    (peer,) = around("section")
    got = at.got.at[n]
    swap = remote(source.at[1 - me, rows], got, at.swap_sems.at[0, n], at.swap_sems.at[1, n], peer)
    swap.start()
    yield
    swap.wait_recv()

    @pl.loop(0, 8)
    def _(i):
        r = pl.ds(pl.multiple_of(i * 64, 64), 64)
        full = pl.ds(pl.multiple_of(first_row + i * 64, 64), 64)
        source[me, full] = (source[me, full].astype(F32) + got[r].astype(F32)).astype(BF16)

    def view(k, part):
        columns = pl.multiple_of(lax.rem(place + k, 4) * 256, 256)
        return source.at[me, pl.ds(first_row + 256 * part, 256), pl.ds(columns, 256)]

    ring = RingScatter(
        view,
        lambda side: at.ex_temp.at[n, side],
        lambda side, part: at.ex_block.at[n, side, part],
        lambda side: at.ex_stage.at[n, side],
        left,
        right,
        [at.ex_send.at[n, i] for i in range(6)],
        [at.ex_recv.at[n, i] for i in range(6)],
    )
    ring.start()
    yield
    ring.middle()
    yield
    ring.finish()
    out[:256] = ring.total(0).astype(BF16)
    out[256:] = ring.total(1).astype(BF16)
    ring.drain()
    swap.wait_send()


def backward_pass(grad, kept, xin, layer, tables, sel, weights, routed_own, routed, late=None):
    cosine, sine, mask = tables
    wqkv, wo, gains, router, wgu, wd = weights
    v, a = in_vmem(), in_any()
    ins = dict(
        grad=(grad, v),
        xin=(xin, v),
        gains=(gains, v),
        cosine=(cosine, v),
        sine=(sine, v),
        mask=(mask, v),
        sel=(sel, v),
        rows=(kept.rows, v),
        qkv=(kept.qkv, v),
        att=(kept.att, v),
        after=(kept.after, v),
        y=(kept.y, v),
        routed=(routed, v),
        routed_own=(routed_own, v),
        x=(kept.x_all, a),
        gu=(kept.gu, a),
        wqkv=(wqkv, a),
        wo=(wo, a),
        router=(router, a),
        wgu=(wgu, a),
        wd=(wd, a),
    )
    last = late is not None
    if last:
        outs = dict(
            section_output=((4, 32, D), BF16, v),
            section_grad=((4, 32, D), F32, v),
            grad_wide=((64, D), F32, v),
            grad_small=((16, 64, LANES), F32, v),
            grad_gu=((2, D, 256), F32, v),
            grad_d=((2, F, 256), F32, v),
        )
        ins.update(
            late_wide=(late.wide, a),
            late_done=(late.done, a),
            late_grad=(late.grad_in, a),
            late_out=(late.out, a),
        )
    else:
        outs = dict(
            grad_in=((2, 32, D), F32, v),
            wide=((2, 4, 4, 32, D), BF16, v),
            done=((1536, 256), BF16, v),
        )
    scratch = dict(
        v_x=pltpu.VMEM((2, 4, 4, 32, D), BF16),
        v_g=pltpu.VMEM((2, 4, 4, 32, D), BF16),
        v_gu=pltpu.VMEM((2, 2, 512, 2 * F), BF16),
        v_wqkv=pltpu.VMEM((D, 512), BF16),
        v_wo=pltpu.VMEM((256, D), BF16),
        v_router=pltpu.VMEM((D, LANES), BF16),
        v_wgu=pltpu.VMEM((2, D, 2 * F), BF16),
        v_wd=pltpu.VMEM((2, F, D), BF16),
        load_sems=pltpu.SemaphoreType.DMA((7,)),
        small_left=pltpu.VMEM((2, 96, D), BF16),
        small_right=pltpu.VMEM((2, 96, LANES), BF16),
        small=pltpu.VMEM((D, LANES), F32),
        hs=pltpu.VMEM((2, 1024, F), BF16),
        gj=pltpu.VMEM((2, 1024, 2 * F), BF16),
        gl=pltpu.VMEM((1024, LANES), BF16),
        dgu=pltpu.VMEM((2, D, 2 * F), BF16),
        dd=pltpu.VMEM((2, F, D), BF16),
        es_sum=pltpu.VMEM((2, 32, D), F32),
        grad_after=pltpu.VMEM((2, 32, D), F32),
        ga_own=pltpu.VMEM((2, 32, D), BF16),
        ga=pltpu.VMEM((2, 128, D), BF16),
        gqkv=pltpu.VMEM((2, 128, 512), BF16),
        part=pltpu.VMEM((2, 128, D), BF16),
        got=pltpu.VMEM((3, 512, D), BF16),
        ex_temp=pltpu.VMEM((3, 2, 256, 256), BF16),
        ex_block=pltpu.VMEM((3, 2, 2, 256, 256), BF16),
        ex_stage=pltpu.VMEM((3, 2, 256, 256), BF16),
        ex_send=pltpu.SemaphoreType.DMA((3, 6)),
        ex_recv=pltpu.SemaphoreType.DMA((3, 6)),
        swap_sems=pltpu.SemaphoreType.DMA((2, 3)),
        **TP_SCRATCH,
        **EXP_SCRATCH,
    )
    if last:
        scratch.update(
            all_out=pltpu.VMEM((2, 2, 32, D), BF16),
            got_out=pltpu.VMEM((2, 32, D), BF16),
            all_grad=pltpu.VMEM((2, 2, 32, D), F32),
            got_grad=pltpu.VMEM((2, 32, D), F32),
            all_done=pltpu.VMEM((2, 1536, 256), BF16),
            got_done=pltpu.VMEM((1536, 256), BF16),
            got_wide=pltpu.VMEM((32, D), F32),
            got_small=pltpu.VMEM((16, 32, LANES), F32),
            last_swap=pltpu.SemaphoreType.DMA((2, 5)),
            se_got=pltpu.VMEM((4, 4, 32, D), BF16),
            se_sum=pltpu.VMEM((1, 4, 4, 32, D), BF16),
            se_held=pltpu.VMEM((2, 2, 3, 4, 32, 512), BF16),
            se_line=pltpu.VMEM((2, 2, 4, 32, 512), BF16),
            se_last=pltpu.VMEM((2, 2, 3, 32, 512), BF16),
            se_out=pltpu.VMEM((2, 32, D), F32),
            se_piece=pltpu.VMEM((2, 32, LANES), F32),
            sp_held=pltpu.VMEM((2, 3, 32, LANES), F32),
            se_total=pltpu.VMEM((2, 32, LANES), F32),
            se_small=pltpu.VMEM((2, 16, 32, LANES), F32),
            se_swap=pltpu.SemaphoreType.DMA((3, 2)),
            late_sems=pltpu.SemaphoreType.DMA((3,)),
            se_send=pltpu.SemaphoreType.DMA((2, 2, 2, 3)),
            se_recv=pltpu.SemaphoreType.DMA((2, 2, 2, 3)),
            sp_send=pltpu.SemaphoreType.DMA((2, 3)),
            sp_recv=pltpu.SemaphoreType.DMA((2, 3)),
            sg_send=pltpu.SemaphoreType.DMA((2, 15)),
            sg_recv=pltpu.SemaphoreType.DMA((2, 15)),
        )

    def chains(at):
        loads = {}
        for n, key in enumerate(("router", "x", "gu", "wd", "wgu", "wqkv", "wo")):
            ref = getattr(at, key)
            loads[key] = pltpu.make_async_copy(
                ref if key in ("x", "gu") else ref.at[layer],
                getattr(at, "v_" + key),
                at.load_sems.at[n],
            )
            loads[key].start()
        done = at.all_done.at[0] if last else at.done
        running = []
        if last:
            at.late = [
                pltpu.make_async_copy(src, dst, at.late_sems.at[n])
                for n, (src, dst) in enumerate(
                    (
                        (at.late_out, at.all_out),
                        (at.late_grad, at.all_grad.at[1]),
                        (at.late_done, at.all_done.at[1]),
                    )
                )
            ]
            for copy in at.late:
                copy.start()
            at.grad_in = at.all_grad.at[0]
            at.wide = at.v_g
        running += [
            backward_chain(at, 0, layer, loads),
            backward_chain(at, 1, layer, loads),
            weight_chain(at),
            expert_chain(at, 0, at.dgu, done.at[pl.ds(0, 512)], 0),
            expert_chain(at, 1, at.dgu, done.at[pl.ds(512, 512)], 512),
            expert_chain(at, 2, at.dd, done.at[pl.ds(1024, 512)], 0),
        ]
        if last:
            running += [
                settle_chain(at, 1, at.late_wide, at.se_sum, 2),
                settle_chain(at, 0, at.wide, at.es_made.at[pl.ds(0, 1)], 6),
                rows_swap(at, 0, 1, at.section_output),
                rows_swap(at, 1, 6, at.section_grad),
                expert_swap(at, 7),
                attention_swap(at, 9),
                small_swap(at, 11),
            ]
        return running

    axes = ["tp_all", "section", "exp_all" if last else "exp_lines"]
    return one_kernel("backward%d" % layer, 12 + layer, axes, ins, outs, scratch, chains)


def rope_tables(seg_rows):
    length = seg_rows.shape[0]
    before = jnp.sum((seg_rows[None, :] < seg_rows[:, None]).astype(jnp.int32), axis=1)
    places = (jnp.arange(length, dtype=jnp.int32) - before).astype(F32)
    powers = jnp.arange(0, HD, 2, dtype=jnp.int32).astype(F32) / HD
    angles = places[:, None] * (ROPE_BASE ** (-powers))[None, :]
    cosine, sine = jnp.cos(angles), jnp.sin(angles)
    indices = jnp.arange(length, dtype=jnp.int32)
    allowed = (seg_rows[:, None] == seg_rows[None, :]) & (indices[None, :] <= indices[:, None])
    return (
        jnp.concatenate([cosine] * 4, axis=1),
        jnp.concatenate([-sine, sine, -sine, sine], axis=1),
        allowed.astype(F32),
    )


def routed(routes):
    labels = jnp.arange(LANES, dtype=jnp.int32)
    return jnp.sum((routes[:, :, None] == labels[None, None, :]).astype(F32), axis=1)


def per_device(
    activations,
    cotangent,
    segments,
    routes,
    attention_gain,
    query_weight,
    key_weight,
    value_weight,
    output_weight,
    mixture_gain,
    router_weight,
    expert_gate_up,
    expert_down,
):
    section = lax.axis_index("section")
    expert = lax.axis_index("exp")

    def own_batches(array):
        return lax.dynamic_slice_in_dim(array, 2 * section, 2, 0)

    qkv_own = jnp.concatenate([query_weight, key_weight, value_weight], axis=2)
    gains_own = jnp.concatenate(
        [attention_gain, mixture_gain, jnp.zeros((6, D), BF16)], axis=0
    ).astype(F32)[None]
    router_own = jnp.pad(router_weight, ((0, 0), (0, 0), (0, LANES - E)))
    (paired,) = fuse([pair_part([qkv_own, output_weight, gains_own, router_own])], 0, "pair")
    weights = tuple(paired) + (expert_gate_up, expert_down)

    cosine, sine, mask = jax.vmap(rope_tables)(own_batches(segments))
    tables = (cosine.reshape(256, LANES), sine.reshape(256, LANES), mask)
    routes_own = own_batches(routes).reshape(64, 8)
    lanes = lax.broadcasted_iota(jnp.int32, (8, LANES), 1)
    sel = (lanes == 2 * expert + lax.broadcasted_iota(jnp.int32, (8, LANES), 0)).astype(F32)
    routed_own = routed(routes_own)
    doubled = jnp.concatenate([routed_own] * 2, axis=1).astype(BF16).reshape(2, 32, 2 * LANES)

    start = own_batches(activations)
    made = forward_pass(start, 0, tables, sel, weights, doubled, None)
    out_first = made.out
    weights = tuple(paired) + (made.wgu, made.wd)
    routed_all = made.routed[..., :LANES]
    kept = forward_pass(out_first, 1, tables, sel, weights, None, made.routed)
    out_second = kept.out

    shared = (tables, sel, weights, doubled, made.routed)
    grad = own_batches(cotangent)
    second = backward_pass(grad, kept, out_first, 1, *shared)
    second.out = jnp.stack([out_first, out_second])
    last = backward_pass(second.grad_in.astype(BF16), made, start, 0, *shared, late=second)
    wide, small = last.grad_wide, last.grad_small.reshape(D, LANES)
    return (
        last.section_output[None],
        last.section_grad[None],
        small[:, E][None],
        wide[None, :, :256],
        wide[None, :, 256:384],
        wide[None, :, 384:512],
        wide[:, 512:768].T[None],
        small[:, E + 1][None],
        small[None, :, :E],
        last.grad_gu[None],
        last.grad_d[None],
    )


def solution(mesh):
    placed = (
        P(None, ("exp", "tp"), None),
        P(None, ("exp", "tp"), None),
        P(None, "exp"),
        P(None, ("exp", "tp"), None),
        P("section", None),
        P("section", None, "tp"),
        P("section", None, "tp"),
        P("section", None, "tp"),
        P("section", "tp", None),
        P("section", None),
        P("section", None, None),
        P("section", "exp", None, None),
        P("section", "exp", None, None),
    )
    return jax.shard_map(
        per_device,
        mesh=mesh,
        in_specs=placed,
        out_specs=(
            P("section", None, ("exp", "tp"), None),
            P("section", None, ("exp", "tp"), None),
            P("section", None),
            P("section", "exp", "tp"),
            P("section", "exp", "tp"),
            P("section", "exp", "tp"),
            P("section", "tp", "exp"),
            P("section", None),
            P("section", None, None),
            P("section", "exp", None, "tp"),
            P("section", "exp", None, "tp"),
        ),
        check_vma=False,
    )
```

```python
import functools

import jax
import jax.numpy as jnp
from jax import lax
from jax.experimental import pallas as pl
from jax.experimental.pallas import tpu as pltpu
from jax.sharding import PartitionSpec as P

D = 1024
HD = 64
E = 32
F = 512
LANES = 128
EPSILON = 1e-06
ROPE_BASE = 10000.0
SCORE_SCALE = 0.125
MASKED = -1e30
MESH = pl.DeviceIdType.MESH
VMEM_LIMIT = 62 * 1024 * 1024
BF16 = jnp.bfloat16
F32 = jnp.float32


def dot(a, b):
    return jnp.dot(a, b, preferred_element_type=F32)


def dot_nt(a, b):
    return lax.dot_general(a, b, (((1,), (1,)), ((), ())), preferred_element_type=F32)


def dot_tn(a, b):
    return lax.dot_general(a, b, (((0,), (0,)), ((), ())), preferred_element_type=F32)


def in_vmem():
    return pl.BlockSpec(memory_space=pltpu.VMEM)


def in_any():
    return pl.BlockSpec(memory_space=pl.ANY)


def greet(peers):
    barrier = pltpu.get_barrier_semaphore()
    for peer in peers:
        pl.semaphore_signal(barrier, inc=1, device_id=peer, device_id_type=MESH)
    pl.semaphore_wait(barrier, len(peers))


def remote(src, dst, send_sem, recv_sem, peer):
    return pltpu.make_async_remote_copy(
        src_ref=src,
        dst_ref=dst,
        send_sem=send_sem,
        recv_sem=recv_sem,
        device_id=peer,
        device_id_type=MESH,
    )


def comm_params(number):
    return pltpu.CompilerParams(
        collective_id=number, has_side_effects=True, vmem_limit_bytes=VMEM_LIMIT
    )


class Part:
    def __init__(self, arrays, in_specs, out_shapes, out_specs, scratch, axes, body):
        self.arrays, self.in_specs = arrays, in_specs
        self.out_shapes, self.out_specs = out_shapes, out_specs
        self.scratch, self.axes, self.body = scratch, axes, body


def around(axis):
    if axis == "section":
        return [{"section": 1 - lax.axis_index("section")}]
    if axis == "tp":
        return [{"tp": lax.rem(lax.axis_index("tp") + j, 4)} for j in (3, 1)]
    if axis == "tp_all":
        return tp_peers()
    at_x, at_z = axis_spots()
    line_only = [(i, 0) for i in (1, 2, 3)] + [(0, i) for i in (1, 2, 3)]
    others = [(i, j) for i in range(4) for j in range(4) if i or j]
    return [
        {"exp": lax.rem(at_x + i, 4) * 4 + lax.rem(at_z + j, 4)}
        for i, j in (line_only if axis == "exp_lines" else others)
    ]


def fused_kernel(parts, *refs):
    refs = list(refs)

    def take(count):
        taken = refs[:count]
        del refs[:count]
        return taken

    ins = [take(len(part.arrays)) for part in parts]
    outs = [take(len(part.out_shapes)) for part in parts]
    scratch = [take(len(part.scratch)) for part in parts]
    axes = []
    for part in parts:
        axes += [axis for axis in part.axes if axis not in axes]
    greet([peer for axis in axes for peer in around(axis)])
    running = [part.body(i, o, s) for part, i, o, s in zip(parts, ins, outs, scratch)]
    while running:
        for one in list(running):
            if next(one, "end") == "end":
                running.remove(one)


def fuse(parts, number, name):
    outs = pl.pallas_call(
        functools.partial(fused_kernel, parts),
        out_shape=[o for part in parts for o in part.out_shapes],
        in_specs=[s for part in parts for s in part.in_specs],
        out_specs=[s for part in parts for s in part.out_specs],
        scratch_shapes=[s for part in parts for s in part.scratch],
        compiler_params=comm_params(number),
        name=name,
    )(*[a for part in parts for a in part.arrays])
    outs = list(outs)
    results = []
    for part in parts:
        count = len(part.out_shapes)
        results.append(outs[:count] if count > 1 else outs[0])
        outs = outs[count:]
    return results


def sems(*shape):
    return [pltpu.SemaphoreType.DMA(shape)] * 2


def pair_part(arrays):
    count = len(arrays)

    def body(ins, outs, scratch):
        held, (send, recv, read, write) = scratch[:count], scratch[count:]
        me = lax.axis_index("section")
        (peer,) = around("section")
        sends, reads, writes = [], [], []
        for at in range(count):
            sends.append(remote(ins[at].at[0], outs[at].at[me], send.at[at], recv.at[at], peer))
            reads.append(pltpu.make_async_copy(ins[at].at[0], held[at], read.at[at]))
            writes.append(pltpu.make_async_copy(held[at], outs[at].at[me], write.at[at]))
            sends[-1].start()
            reads[-1].start()
        yield
        for at in range(count):
            reads[at].wait()
            writes[at].start()
        yield
        yield
        yield
        for at in range(count):
            writes[at].wait()
            sends[at].wait()

    return Part(
        arrays,
        [in_any()] * count,
        [jax.ShapeDtypeStruct((2,) + a.shape[1:], a.dtype) for a in arrays],
        [in_any()] * count,
        [pltpu.VMEM(a.shape[1:], a.dtype) for a in arrays]
        + [pltpu.SemaphoreType.DMA((count,))] * 4,
        ["section"],
        body,
    )


class RingScatter:
    def __init__(self, view, temp, block, stage, left, right, send, recv):
        self.view, self.temp, self.block, self.stage = view, temp, block, stage
        self.left, self.right, self.send, self.recv = left, right, send, recv
        self.copies = []

    def go(self, src, dst, at, peer):
        copy = remote(src, dst, self.send[at], self.recv[at], peer)
        copy.start()
        self.copies.append(copy)

    def start(self):
        self.go(self.view(2, 0), self.temp(0), 0, self.right)
        self.go(self.view(2, 1), self.temp(1), 1, self.left)
        self.go(self.view(1, 1), self.block(0, 1), 2, self.right)
        self.go(self.view(3, 0), self.block(1, 0), 3, self.left)

    def middle(self):
        for side, nearer, peer in ((0, 1, self.right), (1, 3, self.left)):
            self.copies[side].wait_recv()
            term = self.view(nearer, side)[...].astype(F32) + self.temp(side)[...].astype(F32)
            self.stage(side)[...] = term.astype(BF16)
            self.go(self.stage(side), self.block(side, side), 4 + side, peer)

    def finish(self):
        for copy in self.copies[2:]:
            copy.wait_recv()

    def total(self, part):
        return (
            self.view(0, part)[...].astype(F32)
            + self.block(0, part)[...].astype(F32)
            + self.block(1, part)[...].astype(F32)
        )

    def drain(self):
        for copy in self.copies:
            copy.wait_send()


def half_swapped(values):
    width = values.shape[1]
    lane = lax.broadcasted_iota(jnp.int32, values.shape, 1)
    ahead = pltpu.roll(values, width - 32, 1)
    behind = pltpu.roll(values, 32, 1)
    return jnp.where(lax.rem(lane, 64) < 32, ahead, behind)


def three(table):
    return jnp.concatenate([table, table, table], axis=1)


def head(values, batch, first):
    return values[batch * 128 : batch * 128 + 128, first : first + HD]


def masked_softmax(logits, mask):
    routed = mask > 0.5
    shown = jnp.where(routed, logits, MASKED)
    lifted = jnp.where(routed, jnp.exp(shown - jnp.max(shown, axis=1, keepdims=True)), 0.0)
    return lifted / jnp.sum(lifted, axis=1, keepdims=True)


def inverse_rms(values):
    return lax.rsqrt(jnp.mean(values * values, axis=1, keepdims=True) + EPSILON)


class Names:
    pass


def take_turns(running):
    running = list(running)
    while running:
        for one in list(running):
            if next(one, "end") == "end":
                running.remove(one)


def one_kernel(name, number, axes, ins, outs, scratch, chains):
    names = list(ins) + list(outs) + list(scratch)

    def kernel(*refs):
        at = Names()
        for key, ref in zip(names, refs):
            setattr(at, key, ref)
        greet([peer for axis in axes for peer in around(axis)])
        take_turns(chains(at))

    results = pl.pallas_call(
        kernel,
        out_shape=[jax.ShapeDtypeStruct(o[0], o[1]) for o in outs.values()],
        in_specs=[i[1] for i in ins.values()],
        out_specs=[o[2] for o in outs.values()],
        scratch_shapes=list(scratch.values()),
        compiler_params=comm_params(number),
        name=name,
    )(*[i[0] for i in ins.values()])
    made = Names()
    for key, result in zip(outs, results):
        setattr(made, key, result)
    return made


def chain_tp_block(ref, c, k, part):
    place = lax.rem(lax.axis_index("tp") + k, 4)
    if part is None:
        return ref.at[c, pl.ds(pl.multiple_of(place * 32, 32), 32)]
    return ref.at[c, pl.ds(pl.multiple_of(place * 32 + 16 * part, 16), 16)]


def tp_peers():
    me = lax.axis_index("tp")
    return [{"tp": lax.rem(me + j, 4)} for j in (1, 3, 2)]


def chain_tp_gather(own, ref, c, send, recv):
    spot = chain_tp_block(ref, c, 0, None)
    copies = [
        remote(own, spot, send.at[c, n], recv.at[c, n], peer) for n, peer in enumerate(tp_peers())
    ]
    for copy in copies:
        copy.start()
    spot[...] = own[...]
    yield
    for copy in copies:
        copy.wait()


def chain_tp_scatter(ref, c, held, send, recv, out):
    copies = []
    for n, (by, peer) in enumerate(zip((1, 3, 2), tp_peers())):
        block = chain_tp_block(ref, c, by, None)
        copies.append(remote(block, held.at[c, n], send.at[c, n], recv.at[c, n], peer))
        copies[-1].start()
    yield
    total = chain_tp_block(ref, c, 0, None)[...].astype(F32)
    for n in range(3):
        copies[n].wait_recv()
        total = total + held[c, n].astype(F32)
    out[c] = total
    for copy in copies:
        copy.wait_send()


TP_SCRATCH = dict(
    tp_held=pltpu.VMEM((2, 3, 32, D), BF16),
    tp_sum=pltpu.VMEM((2, 32, D), F32),
    tp_send=pltpu.SemaphoreType.DMA((2, 3)),
    tp_recv=pltpu.SemaphoreType.DMA((2, 3)),
    tg_send=pltpu.SemaphoreType.DMA((2, 3)),
    tg_recv=pltpu.SemaphoreType.DMA((2, 3)),
)


def chain_block(ref, c, half, i, j, part, width):
    me = lax.axis_index("exp")
    at_x, at_z = me // 4, lax.rem(me, 4)
    i, j = (i, j) if half == 0 else (j, i)
    rows = pl.ds(0, 32) if part is None else pl.ds(16 * part, 16)
    columns = pl.ds(width * half, width)
    return ref.at[c, lax.rem(at_x + i, 4), lax.rem(at_z + j, 4), rows, columns]


def axis_spots():
    me = lax.axis_index("exp")
    return me // 4, lax.rem(me, 4)


def axis_peers(axis):
    at_x, at_z = axis_spots()
    if axis == 0:
        return [{"exp": lax.rem(at_x + j, 4) * 4 + at_z} for j in (1, 3, 2)]
    return [{"exp": at_x * 4 + lax.rem(at_z + j, 4)} for j in (1, 3, 2)]


def line(ref, c, half, columns, by=None):
    spot = axis_spots()[half]
    spot = spot if by is None else lax.rem(spot + by, 4)
    if half == 0:
        return ref.at[c, spot, :, :, columns]
    return ref.at[c, :, spot, :, columns]


def direct_gather(own, ref, c, send, recv, width=512):
    first, second = [], []
    for half in range(2):
        columns = pl.ds(width * half, width)
        spot = chain_block(ref, c, half, 0, 0, None, width)
        peers = axis_peers(half)
        for n in range(3):
            copy = remote(
                own.at[:, columns], spot, send.at[c, half, 0, n], recv.at[c, half, 0, n], peers[n]
            )
            copy.start()
            first.append(copy)
        spot[...] = own[:, columns]
    yield
    for half in range(2):
        columns = pl.ds(width * half, width)
        for copy in first[3 * half : 3 * half + 3]:
            copy.wait_recv()
        blocks = line(ref, c, 1 - half, columns)
        peers = axis_peers(1 - half)
        for n in range(3):
            copy = remote(
                blocks, blocks, send.at[c, half, 1, n], recv.at[c, half, 1, n], peers[n]
            )
            copy.start()
            second.append(copy)
    yield
    for copy in second:
        copy.wait_recv()
    for copy in first + second:
        copy.wait_send()


def direct_scatter(ref, c, held, ready, last, send, recv, out, slot=None):
    slot = c if slot is None else slot
    first, second = [], []
    for half in range(2):
        columns = pl.ds(512 * half, 512)
        peers = axis_peers(half)
        for n, by in enumerate((1, 3, 2)):
            copy = remote(
                line(ref, slot, half, columns, by),
                held.at[c, half, n],
                send.at[c, half, 0, n],
                recv.at[c, half, 0, n],
                peers[n],
            )
            copy.start()
            first.append(copy)
    yield
    for half in range(2):
        columns = pl.ds(512 * half, 512)
        for copy in first[3 * half : 3 * half + 3]:
            copy.wait_recv()
        total = line(ref, slot, half, columns)[...].astype(F32)
        for n in range(3):
            total = total + held[c, half, n].astype(F32)
        ready[c, half] = total.astype(BF16)
        peers = axis_peers(1 - half)
        spot = axis_spots()[1 - half]
        for n, by in enumerate((1, 3, 2)):
            copy = remote(
                ready.at[c, half, lax.rem(spot + by, 4)],
                last.at[c, half, n],
                send.at[c, half, 1, n],
                recv.at[c, half, 1, n],
                peers[n],
            )
            copy.start()
            second.append(copy)
    yield
    for half in range(2):
        total = ready[c, half, axis_spots()[1 - half]].astype(F32)
        for n in range(3):
            second[3 * half + n].wait_recv()
            total = total + last[c, half, n].astype(F32)
        out[c, :, pl.ds(512 * half, 512)] = total
    for copy in first + second:
        copy.wait_send()


EXP_SCRATCH = dict(
    es_held=pltpu.VMEM((2, 2, 3, 4, 32, 512), BF16),
    es_line=pltpu.VMEM((2, 2, 4, 32, 512), BF16),
    es_last=pltpu.VMEM((2, 2, 3, 32, 512), BF16),
    es_made=pltpu.VMEM((2, 4, 4, 32, D), BF16),
    es_send=pltpu.SemaphoreType.DMA((2, 2, 2, 3)),
    es_recv=pltpu.SemaphoreType.DMA((2, 2, 2, 3)),
    eg_send=pltpu.SemaphoreType.DMA((2, 2, 2, 3)),
    eg_recv=pltpu.SemaphoreType.DMA((2, 2, 2, 3)),
)
def rope(values, cosine, sine):
    return values * three(cosine) + half_swapped(values) * three(sine)


def unrope(values, cosine, sine):
    return values * three(cosine) - half_swapped(values) * three(sine)


def shares(q, k, allowed):
    scores = jnp.where(allowed, dot_nt(q, k) * SCORE_SCALE, MASKED)
    lifted = jnp.exp(scores - jnp.max(scores, axis=1, keepdims=True))
    return lifted / jnp.sum(lifted, axis=1, keepdims=True)


def forward_chain(at, c, layer, loads):
    x = at.xin[c].astype(F32)
    at.normed[c] = (x * inverse_rms(x) * at.gains[layer, 0:1]).astype(BF16)
    yield from chain_tp_gather(at.normed.at[c], at.rows, c, at.tg_send, at.tg_recv)
    if c == 0:
        loads["wqkv"].wait()
        loads["wo"].wait()
    joined = dot(at.rows[c], at.v_wqkv[...])
    spot = slice(c * 128, c * 128 + 128)
    turned = rope(joined[:, :384], at.cosine[spot], at.sine[spot])
    qkv = jnp.concatenate([turned, joined[:, 384:]], axis=1).astype(BF16)
    at.qkv[c] = qkv
    allowed = at.mask[c] > 0.5
    outs = []
    for h in range(4):
        kv = h // 2
        share = shares(head(qkv, 0, h * HD), head(qkv, 0, 256 + kv * HD), allowed)
        outs.append(dot(share.astype(BF16), head(qkv, 0, 384 + kv * HD)))
    attended = jnp.concatenate(outs, axis=1).astype(BF16)
    at.att[c] = attended
    at.part[c] = dot(attended, at.v_wo[...]).astype(BF16)
    yield from chain_tp_scatter(
        at.part, c, at.tp_held, at.tp_send, at.tp_recv, at.tp_sum
    )
    after = x + at.tp_sum[c]
    at.after[c] = after
    at.normed_two[c] = (after * inverse_rms(after) * at.gains[layer, 1:2]).astype(BF16)
    yield from direct_gather(at.normed_two.at[c], at.v_x, c, at.eg_send, at.eg_recv)
    at.saves[c].start()
    if c == 0:
        for key in ("router", "wgu", "wd"):
            loads[key].wait()
    tall = 128
    for tile in range(512 // tall):
        pair = pl.ds(tall // 128 * tile, tall // 128)
        rows = pl.ds(tall * tile, tall)
        xt = at.v_x[c, pair].reshape(tall, D)
        gates = masked_softmax(
            dot(xt, at.v_router[...]), at.routed[c, pair, :, :, :LANES].reshape(tall, LANES).astype(F32)
        )
        total = None
        for e in range(2):
            gate = jnp.sum(gates * at.sel[e : e + 1], axis=1, keepdims=True)
            gu = dot(xt, at.v_wgu[e])
            at.v_gu[c, e, rows] = gu.astype(BF16)
            part, upper = gu[:, :F], gu[:, F:]
            hidden = part * jax.nn.sigmoid(part) * upper
            made = dot((hidden * gate).astype(BF16), at.v_wd[e])
            total = made if total is None else total + made
        at.es_made[c, pair] = total.astype(BF16).reshape(tall // 128, 4, 32, D)
    at.saves[2 + c].start()
    yield from direct_scatter(
        at.es_made, c, at.es_held, at.es_line, at.es_last, at.es_send, at.es_recv, at.y
    )
    at.out[c] = (at.after[c] + at.y[c]).astype(BF16)
    at.saves[c].wait()
    at.saves[2 + c].wait()


def mask_chain(at, c):
    yield from direct_gather(
        at.routed_own.at[c], at.routed, c, at.mg_send, at.mg_recv, width=LANES
    )


def pair_chain(at, loads):
    me = lax.axis_index("section")
    (peer,) = around("section")
    sends, reads, writes = [], [], []
    pieces = ((at.own_gu, at.held_gu, at.wgu), (at.own_d, at.held_d, at.wd))
    for n, (own, held, both) in enumerate(pieces):
        sends.append(
            remote(own.at[0], both.at[me], at.pair_sems.at[0, n], at.pair_sems.at[1, n], peer)
        )
        reads.append(pltpu.make_async_copy(own.at[0], held, at.pair_sems.at[2, n]))
        writes.append(pltpu.make_async_copy(held, both.at[me], at.pair_sems.at[3, n]))
        sends[-1].start()
        reads[-1].start()
    yield
    for n in range(2):
        reads[n].wait()
        writes[n].start()
    yield
    yield
    for n in range(2):
        writes[n].wait()
        sends[n].wait()
    loads["wgu"].start()
    loads["wd"].start()


def forward_pass(xin, layer, tables, sel, weights, routed_own, routed):
    cosine, sine, mask = tables
    wqkv, wo, gains, router, wgu, wd = weights
    swap = layer == 0
    v, a = in_vmem(), in_any()
    ins = dict(
        xin=(xin, v),
        gains=(gains, v),
        cosine=(cosine, v),
        sine=(sine, v),
        mask=(mask, v),
        sel=(sel, v),
        wqkv=(wqkv, a),
        wo=(wo, a),
        router=(router, a),
    )
    if swap:
        ins.update(routed_own=(routed_own, v), own_gu=(wgu, a), own_d=(wd, a))
    else:
        ins.update(routed=(routed, v), wgu=(wgu, a), wd=(wd, a))
    outs = dict(
        out=((2, 32, D), BF16, v),
        rows=((2, 128, D), BF16, v),
        qkv=((2, 128, 512), BF16, v),
        att=((2, 128, 256), BF16, v),
        after=((2, 32, D), F32, v),
        y=((2, 32, D), F32, v),
        x_all=((2, 4, 4, 32, D), BF16, a),
        gu=((2, 2, 512, 2 * F), BF16, a),
    )
    scratch = dict(
        normed=pltpu.VMEM((2, 32, D), BF16),
        normed_two=pltpu.VMEM((2, 32, D), BF16),
        part=pltpu.VMEM((2, 128, D), BF16),
        v_wqkv=pltpu.VMEM((D, 512), BF16),
        v_wo=pltpu.VMEM((256, D), BF16),
        v_router=pltpu.VMEM((D, LANES), BF16),
        v_wgu=pltpu.VMEM((2, D, 2 * F), BF16),
        v_wd=pltpu.VMEM((2, F, D), BF16),
        v_x=pltpu.VMEM((2, 4, 4, 32, D), BF16),
        v_gu=pltpu.VMEM((2, 2, 512, 2 * F), BF16),
        load_sems=pltpu.SemaphoreType.DMA((5,)),
        save_sems=pltpu.SemaphoreType.DMA((4,)),
        **TP_SCRATCH,
        **EXP_SCRATCH,
    )
    if swap:
        outs.update(
            wgu=((2, 2, D, 2 * F), BF16, a),
            wd=((2, 2, F, D), BF16, a),
            routed=((2, 4, 4, 32, 2 * LANES), BF16, v),
        )
        scratch.update(
            held_gu=pltpu.VMEM((2, D, 2 * F), BF16),
            held_d=pltpu.VMEM((2, F, D), BF16),
            pair_sems=pltpu.SemaphoreType.DMA((4, 2)),
            mg_send=pltpu.SemaphoreType.DMA((2, 2, 2, 3)),
            mg_recv=pltpu.SemaphoreType.DMA((2, 2, 2, 3)),
        )

    def chains(at):
        loads = {}
        for n, key in enumerate(("wqkv", "wo", "router", "wgu", "wd")):
            loads[key] = pltpu.make_async_copy(
                getattr(at, key).at[layer], getattr(at, "v_" + key), at.load_sems.at[n]
            )
        at.saves = [
            pltpu.make_async_copy(src.at[c], dst.at[c], at.save_sems.at[2 * n + c])
            for n, (src, dst) in enumerate(((at.v_x, at.x_all), (at.v_gu, at.gu)))
            for c in range(2)
        ]
        for key in ("wqkv", "wo", "router") if swap else loads:
            loads[key].start()
        running = [forward_chain(at, c, layer, loads) for c in range(2)]
        if swap:
            running = [pair_chain(at, loads), mask_chain(at, 0), mask_chain(at, 1)] + running
        return running

    axes = ["tp_all", "exp_lines"] + (["section"] if swap else [])
    return one_kernel("forward%d" % layer, 10 + layer, axes, ins, outs, scratch, chains)


def rms_back(q, values, gain):
    inverse = inverse_rms(values)
    scaled = q * gain
    back = inverse * scaled - values * inverse**3 * jnp.mean(values * scaled, axis=1, keepdims=True)
    return back, q * values * inverse


def backward_chain(at, c, layer, loads):
    gather = direct_gather(at.grad.at[c], at.v_g, c, at.eg_send, at.eg_recv)
    next(gather)
    after = at.after[c]
    normed_two = (after * inverse_rms(after) * at.gains[layer, 1:2]).astype(BF16)
    if c == 0:
        loads["router"].wait()
    own_gates = masked_softmax(
        dot(normed_two, at.v_router[...]), at.routed_own[c, :, :LANES].astype(F32)
    )
    gf = at.grad[c].astype(F32)
    gc = (-own_gates * jnp.sum(gf * at.y[c], axis=1, keepdims=True)).astype(BF16)
    lane = lax.broadcasted_iota(jnp.int32, (32, LANES), 1)
    at.small_left[c, 0:32] = normed_two
    at.small_right[c, 0:32] = gc
    at.small_right[c, 32:64] = jnp.where(lane == E + 1, 1.0, 0.0).astype(BF16)
    at.small_right[c, 64:96] = jnp.where(lane == E, 1.0, 0.0).astype(BF16)
    yield
    yield from gather
    if c == 0:
        for key in ("x", "gu", "wd", "wgu"):
            loads[key].wait()
    tall = 512
    for tile in range(512 // tall):
        pair = pl.ds(tall // 128 * tile, tall // 128)
        rows = pl.ds(tall * tile, tall)
        both = pl.ds(512 * c + tall * tile, tall)
        xt = at.v_x[c, pair].reshape(tall, D)
        gt = at.v_g[c, pair].reshape(tall, D)
        gates = masked_softmax(
            dot(xt, at.v_router[...]),
            at.routed[c, pair, :, :, :LANES].reshape(tall, LANES).astype(F32),
        )
        gl, total = None, None
        for e in range(2):
            chosen = at.sel[e : e + 1]
            gate = jnp.sum(gates * chosen, axis=1, keepdims=True)
            gh = dot_nt(gt, at.v_wd[e])
            part = at.v_gu[c, e, rows, :F].astype(F32)
            upper = at.v_gu[c, e, rows, F:].astype(F32)
            s = jax.nn.sigmoid(part)
            act = part * s
            hidden = act * upper
            term = (gate * jnp.sum(hidden * gh, axis=1, keepdims=True)) * chosen
            gl = term if gl is None else gl + term
            at.hs[e, both] = (hidden * gate).astype(BF16)
            gh = gh * gate
            at.gj[e, both, :F] = (gh * upper * (s + act * (1.0 - s))).astype(BF16)
            at.gj[e, both, F:] = (gh * act).astype(BF16)
            dx = dot_nt(at.gj[e, both], at.v_wgu[e])
            total = dx if total is None else total + dx
        gl = gl.astype(BF16)
        at.gl[both] = gl
        total = total + dot_nt(gl, at.v_router[...])
        at.es_made[c, pair] = total.astype(BF16).reshape(tall // 128, 4, 32, D)
    yield from direct_scatter(
        at.es_made, c, at.es_held, at.es_line, at.es_last, at.es_send, at.es_recv, at.es_sum
    )
    grad_n = at.es_sum[c] + dot_nt(at.small_right[c, 0:32], at.v_router[...])
    back, term = rms_back(grad_n, at.after[c], at.gains[layer, 1:2])
    at.small_left[c, 32:64] = term.astype(BF16)
    grad_after = at.grad[c].astype(F32) + back
    at.grad_after[c] = grad_after
    at.ga_own[c] = grad_after.astype(BF16)
    yield from chain_tp_gather(at.ga_own.at[c], at.ga, c, at.tg_send, at.tg_recv)
    if c == 0:
        loads["wqkv"].wait()
        loads["wo"].wait()
    gatt = dot_nt(at.ga[c], at.v_wo[...]).astype(BF16)
    qkv = at.qkv[c]
    allowed = at.mask[c] > 0.5
    gqs, gks, gvs = [], [None, None], [None, None]
    for h in range(4):
        kv = h // 2
        q = head(qkv, 0, h * HD)
        k = head(qkv, 0, 256 + kv * HD)
        v = head(qkv, 0, 384 + kv * HD)
        go = head(gatt, 0, h * HD)
        share = shares(q, k, allowed)
        gp = dot_nt(go, v)
        gs = (share * (gp - jnp.sum(share * gp, axis=1, keepdims=True))).astype(BF16)
        gqs.append(dot(gs, k) * SCORE_SCALE)
        gk = dot_tn(gs, q) * SCORE_SCALE
        gv = dot_tn(share.astype(BF16), go)
        gks[kv] = gk if gks[kv] is None else gks[kv] + gk
        gvs[kv] = gv if gvs[kv] is None else gvs[kv] + gv
    joined = jnp.concatenate(gqs + gks + gvs, axis=1)
    spot = slice(c * 128, c * 128 + 128)
    turned = unrope(joined[:, :384], at.cosine[spot], at.sine[spot])
    gqkv = jnp.concatenate([turned, joined[:, 384:]], axis=1).astype(BF16)
    at.gqkv[c] = gqkv
    at.part[c] = dot_nt(gqkv, at.v_wqkv[...]).astype(BF16)
    yield from chain_tp_scatter(
        at.part, c, at.tp_held, at.tp_send, at.tp_recv, at.tp_sum
    )
    back, term = rms_back(at.tp_sum[c], at.xin[c].astype(F32), at.gains[layer, 0:1])
    at.small_left[c, 64:96] = term.astype(BF16)
    at.grad_in[c] = at.grad_after[c] + back


def weight_chain(at):
    moves = getattr(at, "moves", [])

    def move(n):
        if moves:
            moves[n].start()

    yield
    yield

    def joint(e, tile):
        columns = pl.ds(256 * tile, 256)
        x = at.v_x[:, :, :, :, columns].reshape(1024, 256)
        at.dgu[e, columns] = dot_tn(x, at.gj[e]).astype(BF16)

    for chunk in range(2):
        for e in range(2):
            for tile in range(2):
                joint(e, 2 * chunk + tile)
        move(chunk)
        yield
    for e in range(2):
        for tile in range(2):
            columns = pl.ds(256 * tile, 256)
            g = at.v_g[...].reshape(1024, D)
            at.dd[e, columns] = dot_tn(at.hs[e, :, columns], g).astype(BF16)
    move(2)
    yield
    x = at.v_x[...].reshape(1024, D)
    at.small[...] = dot_tn(x, at.gl[...])

    def put(first, last, value):
        value = value.astype(BF16).reshape(4, 4, 2, 32, last - first)
        for half in range(2):
            at.wide[half, :, :, :, first:last] = value[:, :, half]

    ga = at.ga[...].reshape(256, D)
    put(512, 768, dot_tn(ga, at.att[...].reshape(256, 256)))
    rows = at.rows[...].reshape(256, D)
    put(0, 512, dot_tn(rows, at.gqkv[...].reshape(256, 512)))
    yield
    left = at.small_left[...].reshape(192, D)
    right = at.small_right[...].reshape(192, LANES)
    put(768, 896, at.small[...] + dot_tn(left, right))
    put(896, 1024, jnp.zeros((D, LANES), F32))
    for copy in moves:
        copy.wait()


def settle_chain(at, n, wide, summed, wait):
    for _ in range(wait):
        yield
    me = lax.axis_index("section")
    (peer,) = around("section")
    swap = remote(
        wide.at[1 - me], at.se_got, at.se_swap.at[0, n], at.se_swap.at[1, n], peer
    )
    swap.start()
    own = pltpu.make_async_copy(wide.at[me], summed.at[0], at.se_swap.at[2, n])
    own.start()
    yield
    own.wait()
    swap.wait_recv()

    @pl.loop(0, 4)
    def _(x):
        summed[0, x] = (summed[0, x].astype(F32) + at.se_got[x].astype(F32)).astype(BF16)

    yield from direct_scatter(
        summed,
        n,
        at.se_held,
        at.se_line,
        at.se_last,
        at.se_send,
        at.se_recv,
        at.se_out,
        slot=0,
    )
    swap.wait_send()
    piece = at.se_piece.at[n]
    piece[...] = at.se_out[n, :, 768:896]
    partners = tp_peers()
    sent = [
        remote(piece, at.sp_held.at[n, k], at.sp_send.at[n, k], at.sp_recv.at[n, k], partner)
        for k, partner in enumerate(partners)
    ]
    for copy in sent:
        copy.start()
    yield
    for copy in sent:
        copy.wait()
    at.se_total[n] = piece[...] + ((at.sp_held[n, 0] + at.sp_held[n, 1]) + at.sp_held[n, 2])
    expert = lax.axis_index("exp")
    whole_small = at.se_small.at[n]
    sent = [
        remote(
            at.se_total.at[n],
            whole_small.at[expert],
            at.sg_send.at[n, k],
            at.sg_recv.at[n, k],
            {"exp": lax.rem(expert + k + 1, 16)},
        )
        for k in range(15)
    ]
    for copy in sent:
        copy.start()
    whole_small[expert] = at.se_total[n]
    yield
    for copy in sent:
        copy.wait()


def swap_chain(at, k, wait, kept, got, write):
    for _ in range(wait):
        yield
    me = lax.axis_index("section")
    (peer,) = around("section")
    if k < 2:
        at.late[k].wait()
    swap = remote(kept.at[1 - me], got, at.last_swap.at[0, k], at.last_swap.at[1, k], peer)
    swap.start()
    write(me, kept.at[me])
    yield
    swap.wait_recv()
    write(1 - me, got)
    swap.wait_send()


def rows_swap(at, k, wait, out):
    kept, got = (at.all_out, at.got_out) if k == 0 else (at.all_grad, at.got_grad)

    def write(core, ref):
        out[pl.ds(2 * core, 2)] = ref[...]

    return swap_chain(at, k, wait, kept, got, write)


def expert_swap(at, wait):
    def write(core, ref):
        at.grad_expert[core] = ref[...]

    return swap_chain(at, 2, wait, at.all_done, at.got_done, write)


def attention_swap(at, wait):
    def write(core, ref):
        at.grad_wide[pl.ds(pl.multiple_of(32 * core, 32), 32)] = ref[...]

    return swap_chain(at, 3, wait, at.se_out, at.got_wide, write)


def small_swap(at, wait):
    def write(core, ref):
        at.grad_small[:, pl.ds(pl.multiple_of(32 * core, 32), 32)] = ref[...]

    return swap_chain(at, 4, wait, at.se_small, at.got_small, write)


def expert_ring(at, n, own, out):
    place = lax.axis_index("tp")
    left, right = around("tp")

    def view(k, part):
        columns = pl.multiple_of(lax.rem(place + k, 4) * 256, 256)
        return own.at[pl.ds(256 * part, 256), pl.ds(columns, 256)]

    return RingScatter(
        view,
        lambda side: at.ex_temp.at[n, side],
        lambda side, part: at.ex_block.at[n, side, part],
        lambda side: at.ex_stage.at[n, side],
        left,
        right,
        [at.ex_send.at[n, i] for i in range(6)],
        [at.ex_recv.at[n, i] for i in range(6)],
    )


def add_into(own, got):
    @pl.loop(0, 8)
    def _(i):
        r = pl.ds(pl.multiple_of(i * 64, 64), 64)
        own[r] = (own[r].astype(F32) + got[r].astype(F32)).astype(BF16)


def end_ring(ring, out):
    ring.finish()
    out[:256] = ring.total(0).astype(BF16)
    out[256:] = ring.total(1).astype(BF16)
    ring.drain()


def early_expert_chain(at, n):
    me = lax.axis_index("section")
    (peer,) = around("section")
    source = (at.late_gu, at.late_gu, at.late_d)[n]
    rows = pl.ds((0, 512, 0)[n], 512)
    own = (at.dd.at[0], at.dd.at[1], at.dgu.at[0, pl.ds(512, 512)])[n]
    got = at.gj.at[n // 2, pl.ds(512 * (n % 2), 512)]
    out = at.all_done.at[1, pl.ds(512 * n, 512)]
    sems = at.swap_sems
    swap = remote(source.at[1 - me, rows], got, sems.at[0, n], sems.at[1, n], peer)
    swap.start()
    kept = pltpu.make_async_copy(source.at[me, rows], own, sems.at[2, n])
    kept.start()
    yield
    kept.wait()
    swap.wait()
    add_into(own, got)
    ring = expert_ring(at, n, own, out)
    ring.start()
    yield
    ring.middle()
    yield
    end_ring(ring, out)


def expert_chain(at, n):
    for _ in range(2 + n):
        yield
    me = lax.axis_index("section")
    (peer,) = around("section")
    source = (at.dgu, at.dgu, at.dd)[n]
    rows = pl.ds((0, 512, 0)[n], 512)
    own, got = source.at[me, rows], at.got.at[n]
    out = at.all_done.at[0, pl.ds(512 * n, 512)]
    sems = at.swap_sems
    swap = remote(source.at[1 - me, rows], got, sems.at[3, n], sems.at[4, n], peer)
    swap.start()
    for _ in range(3 - n):
        yield
    swap.wait()
    add_into(own, got)
    ring = expert_ring(at, n, own, out)
    ring.start()
    yield
    yield
    ring.middle()
    yield
    end_ring(ring, out)


def backward_pass(grad, kept, xin, layer, tables, sel, weights, routed_own, routed, late=None):
    cosine, sine, mask = tables
    wqkv, wo, gains, router, wgu, wd = weights
    v, a = in_vmem(), in_any()
    ins = dict(
        grad=(grad, v),
        xin=(xin, v),
        gains=(gains, v),
        cosine=(cosine, v),
        sine=(sine, v),
        mask=(mask, v),
        sel=(sel, v),
        rows=(kept.rows, v),
        qkv=(kept.qkv, v),
        att=(kept.att, v),
        after=(kept.after, v),
        y=(kept.y, v),
        routed=(routed, v),
        routed_own=(routed_own, v),
        x=(kept.x_all, a),
        gu=(kept.gu, a),
        wqkv=(wqkv, a),
        wo=(wo, a),
        router=(router, a),
        wgu=(wgu, a),
        wd=(wd, a),
    )
    last = late is not None
    if last:
        outs = dict(
            section_output=((4, 32, D), BF16, v),
            section_grad=((4, 32, D), F32, v),
            grad_wide=((64, D), F32, v),
            grad_small=((16, 64, LANES), F32, v),
            grad_expert=((2, 1536, 256), BF16, v),
        )
        ins.update(
            late_wide=(late.wide, a),
            late_gu=(late.dgu, a),
            late_d=(late.dd, a),
            late_grad=(late.grad_in, a),
            late_out=(late.out, a),
        )
    else:
        outs = dict(
            grad_in=((2, 32, D), F32, v),
            wide=((2, 4, 4, 32, D), BF16, v),
            dgu_out=((2, D, 2 * F), BF16, a),
            dd_out=((2, F, D), BF16, a),
        )
    scratch = dict(
        v_x=pltpu.VMEM((2, 4, 4, 32, D), BF16),
        v_g=pltpu.VMEM((2, 4, 4, 32, D), BF16),
        v_gu=pltpu.VMEM((2, 2, 512, 2 * F), BF16),
        v_wqkv=pltpu.VMEM((D, 512), BF16),
        v_wo=pltpu.VMEM((256, D), BF16),
        v_router=pltpu.VMEM((D, LANES), BF16),
        v_wgu=pltpu.VMEM((2, D, 2 * F), BF16),
        v_wd=pltpu.VMEM((2, F, D), BF16),
        load_sems=pltpu.SemaphoreType.DMA((7,)),
        small_left=pltpu.VMEM((2, 96, D), BF16),
        small_right=pltpu.VMEM((2, 96, LANES), BF16),
        small=pltpu.VMEM((D, LANES), F32),
        hs=pltpu.VMEM((2, 1024, F), BF16),
        gj=pltpu.VMEM((2, 1024, 2 * F), BF16),
        gl=pltpu.VMEM((1024, LANES), BF16),
        dgu=pltpu.VMEM((2, D, 2 * F), BF16),
        dd=pltpu.VMEM((2, F, D), BF16),
        es_sum=pltpu.VMEM((2, 32, D), F32),
        grad_after=pltpu.VMEM((2, 32, D), F32),
        ga_own=pltpu.VMEM((2, 32, D), BF16),
        ga=pltpu.VMEM((2, 128, D), BF16),
        gqkv=pltpu.VMEM((2, 128, 512), BF16),
        part=pltpu.VMEM((2, 128, D), BF16),
        **TP_SCRATCH,
        **EXP_SCRATCH,
    )
    if not last:
        scratch.update(move_sems=pltpu.SemaphoreType.DMA((3,)))
    else:
        scratch.update(
            got=pltpu.VMEM((3, 512, D), BF16),
            ex_temp=pltpu.VMEM((3, 2, 256, 256), BF16),
            ex_block=pltpu.VMEM((3, 2, 2, 256, 256), BF16),
            ex_stage=pltpu.VMEM((3, 2, 256, 256), BF16),
            ex_send=pltpu.SemaphoreType.DMA((3, 6)),
            ex_recv=pltpu.SemaphoreType.DMA((3, 6)),
            swap_sems=pltpu.SemaphoreType.DMA((5, 3)),
            all_out=pltpu.VMEM((2, 2, 32, D), BF16),
            got_out=pltpu.VMEM((2, 32, D), BF16),
            all_grad=pltpu.VMEM((2, 2, 32, D), F32),
            got_grad=pltpu.VMEM((2, 32, D), F32),
            all_done=pltpu.VMEM((2, 1536, 256), BF16),
            got_done=pltpu.VMEM((1536, 256), BF16),
            got_wide=pltpu.VMEM((32, D), F32),
            got_small=pltpu.VMEM((16, 32, LANES), F32),
            last_swap=pltpu.SemaphoreType.DMA((2, 5)),
            se_got=pltpu.VMEM((4, 4, 32, D), BF16),
            se_sum=pltpu.VMEM((1, 4, 4, 32, D), BF16),
            se_held=pltpu.VMEM((2, 2, 3, 4, 32, 512), BF16),
            se_line=pltpu.VMEM((2, 2, 4, 32, 512), BF16),
            se_last=pltpu.VMEM((2, 2, 3, 32, 512), BF16),
            se_out=pltpu.VMEM((2, 32, D), F32),
            se_piece=pltpu.VMEM((2, 32, LANES), F32),
            sp_held=pltpu.VMEM((2, 3, 32, LANES), F32),
            se_total=pltpu.VMEM((2, 32, LANES), F32),
            se_small=pltpu.VMEM((2, 16, 32, LANES), F32),
            se_swap=pltpu.SemaphoreType.DMA((3, 2)),
            late_sems=pltpu.SemaphoreType.DMA((3,)),
            se_send=pltpu.SemaphoreType.DMA((2, 2, 2, 3)),
            se_recv=pltpu.SemaphoreType.DMA((2, 2, 2, 3)),
            sp_send=pltpu.SemaphoreType.DMA((2, 3)),
            sp_recv=pltpu.SemaphoreType.DMA((2, 3)),
            sg_send=pltpu.SemaphoreType.DMA((2, 15)),
            sg_recv=pltpu.SemaphoreType.DMA((2, 15)),
        )

    def chains(at):
        loads = {}
        for n, key in enumerate(("router", "x", "gu", "wd", "wgu", "wqkv", "wo")):
            ref = getattr(at, key)
            loads[key] = pltpu.make_async_copy(
                ref if key in ("x", "gu") else ref.at[layer],
                getattr(at, "v_" + key),
                at.load_sems.at[n],
            )
            loads[key].start()
        running = []
        if last:
            at.late = [
                pltpu.make_async_copy(src, dst, at.late_sems.at[n])
                for n, (src, dst) in enumerate(
                    (
                        (at.late_out, at.all_out),
                        (at.late_grad, at.all_grad.at[1]),
                    )
                )
            ]
            for copy in at.late:
                copy.start()
            at.grad_in = at.all_grad.at[0]
            at.wide = at.v_g
        else:
            at.moves = [
                pltpu.make_async_copy(src.at[:, rows], dst.at[:, rows], at.move_sems.at[n])
                for n, (src, dst, rows) in enumerate(
                    (
                        (at.dgu, at.dgu_out, pl.ds(0, 512)),
                        (at.dgu, at.dgu_out, pl.ds(512, 512)),
                        (at.dd, at.dd_out, pl.ds(0, 512)),
                    )
                )
            ]
        running += [backward_chain(at, c, layer, loads) for c in range(2)]
        if last:
            running += [early_expert_chain(at, n) for n in range(3)]
        running.append(weight_chain(at))
        if last:
            running += [expert_chain(at, n) for n in range(3)]
            running += [
                settle_chain(at, 1, at.late_wide, at.se_sum, 2),
                settle_chain(at, 0, at.wide, at.es_made.at[pl.ds(0, 1)], 6),
                rows_swap(at, 0, 1, at.section_output),
                rows_swap(at, 1, 6, at.section_grad),
                expert_swap(at, 9),
                attention_swap(at, 9),
                small_swap(at, 11),
            ]
        return running

    axes = ["tp_all", "section", "exp_all" if last else "exp_lines"]
    return one_kernel("backward%d" % layer, 12 + layer, axes, ins, outs, scratch, chains)


def rope_tables(seg_rows):
    length = seg_rows.shape[0]
    before = jnp.sum((seg_rows[None, :] < seg_rows[:, None]).astype(jnp.int32), axis=1)
    places = (jnp.arange(length, dtype=jnp.int32) - before).astype(F32)
    powers = jnp.arange(0, HD, 2, dtype=jnp.int32).astype(F32) / HD
    angles = places[:, None] * (ROPE_BASE ** (-powers))[None, :]
    cosine, sine = jnp.cos(angles), jnp.sin(angles)
    indices = jnp.arange(length, dtype=jnp.int32)
    allowed = (seg_rows[:, None] == seg_rows[None, :]) & (indices[None, :] <= indices[:, None])
    return (
        jnp.concatenate([cosine] * 4, axis=1),
        jnp.concatenate([-sine, sine, -sine, sine], axis=1),
        allowed.astype(F32),
    )


def routed(routes):
    labels = jnp.arange(LANES, dtype=jnp.int32)
    return jnp.sum((routes[:, :, None] == labels[None, None, :]).astype(F32), axis=1)


def per_device(
    activations,
    cotangent,
    segments,
    routes,
    attention_gain,
    query_weight,
    key_weight,
    value_weight,
    output_weight,
    mixture_gain,
    router_weight,
    expert_gate_up,
    expert_down,
):
    section = lax.axis_index("section")
    expert = lax.axis_index("exp")

    def own_batches(array):
        return lax.dynamic_slice_in_dim(array, 2 * section, 2, 0)

    qkv_own = jnp.concatenate([query_weight, key_weight, value_weight], axis=2)
    gains_own = jnp.concatenate(
        [attention_gain, mixture_gain, jnp.zeros((6, D), BF16)], axis=0
    ).astype(F32)[None]
    router_own = jnp.pad(router_weight, ((0, 0), (0, 0), (0, LANES - E)))
    (paired,) = fuse([pair_part([qkv_own, output_weight, gains_own, router_own])], 0, "pair")
    weights = tuple(paired) + (expert_gate_up, expert_down)

    cosine, sine, mask = jax.vmap(rope_tables)(own_batches(segments))
    tables = (cosine.reshape(256, LANES), sine.reshape(256, LANES), mask)
    routes_own = own_batches(routes).reshape(64, 8)
    lanes = lax.broadcasted_iota(jnp.int32, (8, LANES), 1)
    sel = (lanes == 2 * expert + lax.broadcasted_iota(jnp.int32, (8, LANES), 0)).astype(F32)
    routed_own = routed(routes_own)
    doubled = jnp.concatenate([routed_own] * 2, axis=1).astype(BF16).reshape(2, 32, 2 * LANES)

    start = own_batches(activations)
    made = forward_pass(start, 0, tables, sel, weights, doubled, None)
    out_first = made.out
    weights = tuple(paired) + (made.wgu, made.wd)
    routed_all = made.routed[..., :LANES]
    kept = forward_pass(out_first, 1, tables, sel, weights, None, made.routed)
    out_second = kept.out

    shared = (tables, sel, weights, doubled, made.routed)
    grad = own_batches(cotangent)
    second = backward_pass(grad, kept, out_first, 1, *shared)
    second.out = jnp.stack([out_first, out_second])
    second.dgu, second.dd = second.dgu_out, second.dd_out
    last = backward_pass(second.grad_in.astype(BF16), made, start, 0, *shared, late=second)
    wide, small = last.grad_wide, last.grad_small.reshape(D, LANES)
    return (
        last.section_output[None],
        last.section_grad[None],
        small[:, E][None],
        wide[None, :, :256],
        wide[None, :, 256:384],
        wide[None, :, 384:512],
        wide[:, 512:768].T[None],
        small[:, E + 1][None],
        small[None, :, :E],
        last.grad_expert[None, :, :D].astype(F32),
        last.grad_expert[None, :, D:].astype(F32),
    )


def solution(mesh):
    placed = (
        P(None, ("exp", "tp"), None),
        P(None, ("exp", "tp"), None),
        P(None, "exp"),
        P(None, ("exp", "tp"), None),
        P("section", None),
        P("section", None, "tp"),
        P("section", None, "tp"),
        P("section", None, "tp"),
        P("section", "tp", None),
        P("section", None),
        P("section", None, None),
        P("section", "exp", None, None),
        P("section", "exp", None, None),
    )
    return jax.shard_map(
        per_device,
        mesh=mesh,
        in_specs=placed,
        out_specs=(
            P("section", None, ("exp", "tp"), None),
            P("section", None, ("exp", "tp"), None),
            P("section", None),
            P("section", "exp", "tp"),
            P("section", "exp", "tp"),
            P("section", "exp", "tp"),
            P("section", "tp", "exp"),
            P("section", None),
            P("section", None, None),
            P("section", "exp", None, "tp"),
            P("section", "exp", None, "tp"),
        ),
        check_vma=False,
    )
```

```python
import functools

import jax
import jax.numpy as jnp
from jax import lax
from jax.experimental import pallas as pl
from jax.experimental.pallas import tpu as pltpu
from jax.sharding import PartitionSpec as P

D = 1024
HD = 64
E = 32
F = 512
LANES = 128
EPSILON = 1e-06
ROPE_BASE = 10000.0
SCORE_SCALE = 0.125
MASKED = -1e30
MESH = pl.DeviceIdType.MESH
VMEM_LIMIT = 62 * 1024 * 1024
BF16 = jnp.bfloat16
F32 = jnp.float32


def dot(a, b):
    return jnp.dot(a, b, preferred_element_type=F32)


def dot_nt(a, b):
    return lax.dot_general(a, b, (((1,), (1,)), ((), ())), preferred_element_type=F32)


def dot_tn(a, b):
    return lax.dot_general(a, b, (((0,), (0,)), ((), ())), preferred_element_type=F32)


def in_vmem():
    return pl.BlockSpec(memory_space=pltpu.VMEM)


def in_any():
    return pl.BlockSpec(memory_space=pl.ANY)


def greet(peers):
    barrier = pltpu.get_barrier_semaphore()
    for peer in peers:
        pl.semaphore_signal(barrier, inc=1, device_id=peer, device_id_type=MESH)
    pl.semaphore_wait(barrier, len(peers))


def remote(src, dst, send_sem, recv_sem, peer):
    return pltpu.make_async_remote_copy(
        src_ref=src,
        dst_ref=dst,
        send_sem=send_sem,
        recv_sem=recv_sem,
        device_id=peer,
        device_id_type=MESH,
    )


def comm_params(number):
    return pltpu.CompilerParams(
        collective_id=number, has_side_effects=True, vmem_limit_bytes=VMEM_LIMIT
    )


class Part:
    def __init__(self, arrays, in_specs, out_shapes, out_specs, scratch, axes, body):
        self.arrays, self.in_specs = arrays, in_specs
        self.out_shapes, self.out_specs = out_shapes, out_specs
        self.scratch, self.axes, self.body = scratch, axes, body


def around(axis):
    if axis == "section":
        return [{"section": 1 - lax.axis_index("section")}]
    if axis == "tp":
        return [{"tp": lax.rem(lax.axis_index("tp") + j, 4)} for j in (3, 1)]
    if axis == "tp_all":
        return tp_peers()
    at_x, at_z = axis_spots()
    line_only = [(i, 0) for i in (1, 2, 3)] + [(0, i) for i in (1, 2, 3)]
    others = [(i, j) for i in range(4) for j in range(4) if i or j]
    return [
        {"exp": lax.rem(at_x + i, 4) * 4 + lax.rem(at_z + j, 4)}
        for i, j in (line_only if axis == "exp_lines" else others)
    ]


def fused_kernel(parts, *refs):
    refs = list(refs)

    def take(count):
        taken = refs[:count]
        del refs[:count]
        return taken

    ins = [take(len(part.arrays)) for part in parts]
    outs = [take(len(part.out_shapes)) for part in parts]
    scratch = [take(len(part.scratch)) for part in parts]
    axes = []
    for part in parts:
        axes += [axis for axis in part.axes if axis not in axes]
    greet([peer for axis in axes for peer in around(axis)])
    running = [part.body(i, o, s) for part, i, o, s in zip(parts, ins, outs, scratch)]
    while running:
        for one in list(running):
            if next(one, "end") == "end":
                running.remove(one)


def fuse(parts, number, name):
    outs = pl.pallas_call(
        functools.partial(fused_kernel, parts),
        out_shape=[o for part in parts for o in part.out_shapes],
        in_specs=[s for part in parts for s in part.in_specs],
        out_specs=[s for part in parts for s in part.out_specs],
        scratch_shapes=[s for part in parts for s in part.scratch],
        compiler_params=comm_params(number),
        name=name,
    )(*[a for part in parts for a in part.arrays])
    outs = list(outs)
    results = []
    for part in parts:
        count = len(part.out_shapes)
        results.append(outs[:count] if count > 1 else outs[0])
        outs = outs[count:]
    return results


def sems(*shape):
    return [pltpu.SemaphoreType.DMA(shape)] * 2


def pair_part(arrays, spots, shapes):
    count = len(arrays)

    def body(ins, outs, scratch):
        held, (send, recv, read, write) = scratch[:count], scratch[count:]
        me = lax.axis_index("section")
        (peer,) = around("section")
        sends, reads, writes = [], [], []
        for at, (out, column) in enumerate(spots):
            spot = outs[out].at[me, :, pl.ds(column, arrays[at].shape[2])]
            sends.append(remote(ins[at].at[0], spot, send.at[at], recv.at[at], peer))
            reads.append(pltpu.make_async_copy(ins[at].at[0], held[at], read.at[at]))
            writes.append(pltpu.make_async_copy(held[at], spot, write.at[at]))
            sends[-1].start()
            reads[-1].start()
        yield
        for at in range(count):
            reads[at].wait()
            writes[at].start()
        yield
        for at in range(count):
            writes[at].wait()
            sends[at].wait()

    return Part(
        arrays,
        [in_any()] * count,
        [jax.ShapeDtypeStruct((2,) + shape, dtype) for shape, dtype in shapes],
        [in_any()] * len(shapes),
        [pltpu.VMEM(a.shape[1:], a.dtype) for a in arrays]
        + [pltpu.SemaphoreType.DMA((count,))] * 4,
        ["section"],
        body,
    )


class RingScatter:
    def __init__(self, view, temp, block, stage, left, right, send, recv):
        self.view, self.temp, self.block, self.stage = view, temp, block, stage
        self.left, self.right, self.send, self.recv = left, right, send, recv
        self.copies = []

    def go(self, src, dst, at, peer):
        copy = remote(src, dst, self.send[at], self.recv[at], peer)
        copy.start()
        self.copies.append(copy)

    def start(self):
        self.go(self.view(2, 0), self.temp(0), 0, self.right)
        self.go(self.view(2, 1), self.temp(1), 1, self.left)
        self.go(self.view(1, 1), self.block(0, 1), 2, self.right)
        self.go(self.view(3, 0), self.block(1, 0), 3, self.left)

    def middle(self):
        for side, nearer, peer in ((0, 1, self.right), (1, 3, self.left)):
            self.copies[side].wait_recv()
            term = self.view(nearer, side)[...].astype(F32) + self.temp(side)[...].astype(F32)
            self.stage(side)[...] = term.astype(BF16)
            self.go(self.stage(side), self.block(side, side), 4 + side, peer)

    def finish(self):
        for copy in self.copies[2:]:
            copy.wait_recv()

    def total(self, part):
        return (
            self.view(0, part)[...].astype(F32)
            + self.block(0, part)[...].astype(F32)
            + self.block(1, part)[...].astype(F32)
        )

    def drain(self):
        for copy in self.copies:
            copy.wait_send()


def half_swapped(values):
    width = values.shape[1]
    lane = lax.broadcasted_iota(jnp.int32, values.shape, 1)
    ahead = pltpu.roll(values, width - 32, 1)
    behind = pltpu.roll(values, 32, 1)
    return jnp.where(lax.rem(lane, 64) < 32, ahead, behind)


def three(table):
    return jnp.concatenate([table, table, table], axis=1)


def head(values, batch, first):
    return values[batch * 128 : batch * 128 + 128, first : first + HD]


def masked_softmax(logits, mask):
    routed = mask > 0.5
    shown = jnp.where(routed, logits, MASKED)
    lifted = jnp.where(routed, jnp.exp(shown - jnp.max(shown, axis=1, keepdims=True)), 0.0)
    return lifted / jnp.sum(lifted, axis=1, keepdims=True)


def inverse_rms(values):
    return lax.rsqrt(jnp.mean(values * values, axis=1, keepdims=True) + EPSILON)


class Names:
    pass


def take_turns(running):
    running = list(running)
    while running:
        for one in list(running):
            if next(one, "end") == "end":
                running.remove(one)


def one_kernel(name, number, axes, ins, outs, scratch, chains):
    names = list(ins) + list(outs) + list(scratch)

    def kernel(*refs):
        at = Names()
        for key, ref in zip(names, refs):
            setattr(at, key, ref)
        greet([peer for axis in axes for peer in around(axis)])
        take_turns(chains(at))

    results = pl.pallas_call(
        kernel,
        out_shape=[jax.ShapeDtypeStruct(o[0], o[1]) for o in outs.values()],
        in_specs=[i[1] for i in ins.values()],
        out_specs=[o[2] for o in outs.values()],
        scratch_shapes=list(scratch.values()),
        compiler_params=comm_params(number),
        name=name,
    )(*[i[0] for i in ins.values()])
    made = Names()
    for key, result in zip(outs, results):
        setattr(made, key, result)
    return made


def chain_tp_block(ref, c, k, part):
    place = lax.rem(lax.axis_index("tp") + k, 4)
    if part is None:
        return ref.at[c, pl.ds(pl.multiple_of(place * 32, 32), 32)]
    return ref.at[c, pl.ds(pl.multiple_of(place * 32 + 16 * part, 16), 16)]


def tp_peers():
    me = lax.axis_index("tp")
    return [{"tp": lax.rem(me + j, 4)} for j in (1, 3, 2)]


def chain_tp_gather(own, ref, c, send, recv):
    spot = chain_tp_block(ref, c, 0, None)
    copies = [
        remote(own, spot, send.at[c, n], recv.at[c, n], peer) for n, peer in enumerate(tp_peers())
    ]
    for copy in copies:
        copy.start()
    spot[...] = own[...]
    yield
    for copy in copies:
        copy.wait()


def chain_tp_scatter(ref, c, held, send, recv, out):
    copies = []
    for n, (by, peer) in enumerate(zip((1, 3, 2), tp_peers())):
        block = chain_tp_block(ref, c, by, None)
        copies.append(remote(block, held.at[c, n], send.at[c, n], recv.at[c, n], peer))
        copies[-1].start()
    yield
    total = chain_tp_block(ref, c, 0, None)[...].astype(F32)
    for n in range(3):
        copies[n].wait_recv()
        total = total + held[c, n].astype(F32)
    out[c] = total
    for copy in copies:
        copy.wait_send()


TP_SCRATCH = dict(
    tp_held=pltpu.VMEM((2, 3, 32, D), BF16),
    tp_sum=pltpu.VMEM((2, 32, D), F32),
    tp_send=pltpu.SemaphoreType.DMA((2, 3)),
    tp_recv=pltpu.SemaphoreType.DMA((2, 3)),
    tg_send=pltpu.SemaphoreType.DMA((2, 3)),
    tg_recv=pltpu.SemaphoreType.DMA((2, 3)),
)


def chain_block(ref, c, half, i, j, part, width):
    me = lax.axis_index("exp")
    at_x, at_z = me // 4, lax.rem(me, 4)
    i, j = (i, j) if half == 0 else (j, i)
    rows = pl.ds(0, 32) if part is None else pl.ds(16 * part, 16)
    columns = pl.ds(width * half, width)
    return ref.at[c, lax.rem(at_x + i, 4), lax.rem(at_z + j, 4), rows, columns]


def axis_spots():
    me = lax.axis_index("exp")
    return me // 4, lax.rem(me, 4)


def axis_peers(axis):
    at_x, at_z = axis_spots()
    if axis == 0:
        return [{"exp": lax.rem(at_x + j, 4) * 4 + at_z} for j in (1, 3, 2)]
    return [{"exp": at_x * 4 + lax.rem(at_z + j, 4)} for j in (1, 3, 2)]


def line(ref, c, half, columns, by=None):
    spot = axis_spots()[half]
    spot = spot if by is None else lax.rem(spot + by, 4)
    if half == 0:
        return ref.at[c, spot, :, :, columns]
    return ref.at[c, :, spot, :, columns]


def direct_gather(own, ref, c, send, recv, width=512):
    first, second = [], []
    for half in range(2):
        columns = pl.ds(width * half, width)
        spot = chain_block(ref, c, half, 0, 0, None, width)
        peers = axis_peers(half)
        for n in range(3):
            copy = remote(
                own.at[:, columns], spot, send.at[c, half, 0, n], recv.at[c, half, 0, n], peers[n]
            )
            copy.start()
            first.append(copy)
        spot[...] = own[:, columns]
    yield
    for half in range(2):
        columns = pl.ds(width * half, width)
        for copy in first[3 * half : 3 * half + 3]:
            copy.wait_recv()
        blocks = line(ref, c, 1 - half, columns)
        peers = axis_peers(1 - half)
        for n in range(3):
            copy = remote(
                blocks, blocks, send.at[c, half, 1, n], recv.at[c, half, 1, n], peers[n]
            )
            copy.start()
            second.append(copy)
    yield
    for copy in second:
        copy.wait_recv()
    for copy in first + second:
        copy.wait_send()


def direct_scatter(ref, c, held, ready, last, send, recv, out, slot=None):
    slot = c if slot is None else slot
    first, second = [], []
    for half in range(2):
        columns = pl.ds(512 * half, 512)
        peers = axis_peers(half)
        for n, by in enumerate((1, 3, 2)):
            copy = remote(
                line(ref, slot, half, columns, by),
                held.at[c, half, n],
                send.at[c, half, 0, n],
                recv.at[c, half, 0, n],
                peers[n],
            )
            copy.start()
            first.append(copy)
    yield
    for half in range(2):
        columns = pl.ds(512 * half, 512)
        for copy in first[3 * half : 3 * half + 3]:
            copy.wait_recv()
        total = line(ref, slot, half, columns)[...].astype(F32)
        for n in range(3):
            total = total + held[c, half, n].astype(F32)
        ready[c, half] = total.astype(BF16)
        peers = axis_peers(1 - half)
        spot = axis_spots()[1 - half]
        for n, by in enumerate((1, 3, 2)):
            copy = remote(
                ready.at[c, half, lax.rem(spot + by, 4)],
                last.at[c, half, n],
                send.at[c, half, 1, n],
                recv.at[c, half, 1, n],
                peers[n],
            )
            copy.start()
            second.append(copy)
    yield
    for half in range(2):
        total = ready[c, half, axis_spots()[1 - half]].astype(F32)
        for n in range(3):
            second[3 * half + n].wait_recv()
            total = total + last[c, half, n].astype(F32)
        out[c, :, pl.ds(512 * half, 512)] = total
    for copy in first + second:
        copy.wait_send()


EXP_SCRATCH = dict(
    es_held=pltpu.VMEM((2, 2, 3, 4, 32, 512), BF16),
    es_line=pltpu.VMEM((2, 2, 4, 32, 512), BF16),
    es_last=pltpu.VMEM((2, 2, 3, 32, 512), BF16),
    es_made=pltpu.VMEM((2, 4, 4, 32, D), BF16),
    es_send=pltpu.SemaphoreType.DMA((2, 2, 2, 3)),
    es_recv=pltpu.SemaphoreType.DMA((2, 2, 2, 3)),
    eg_send=pltpu.SemaphoreType.DMA((2, 2, 2, 3)),
    eg_recv=pltpu.SemaphoreType.DMA((2, 2, 2, 3)),
)
def rope(values, cosine, sine):
    return values * three(cosine) + half_swapped(values) * three(sine)


def unrope(values, cosine, sine):
    return values * three(cosine) - half_swapped(values) * three(sine)


def shares(q, k, allowed):
    scores = jnp.where(allowed, dot_nt(q, k) * SCORE_SCALE, MASKED)
    lifted = jnp.exp(scores - jnp.max(scores, axis=1, keepdims=True))
    return lifted / jnp.sum(lifted, axis=1, keepdims=True)


def forward_chain(at, c, layer, loads):
    x = at.xin[c].astype(F32)
    at.normed[c] = (x * inverse_rms(x) * at.gains[layer, 0:1]).astype(BF16)
    yield from chain_tp_gather(at.normed.at[c], at.rows, c, at.tg_send, at.tg_recv)
    if c == 0:
        loads["wqkv"].wait()
        loads["wo"].wait()
    joined = dot(at.rows[c], at.v_wqkv[...])
    spot = slice(c * 128, c * 128 + 128)
    turned = rope(joined[:, :384], at.cosine[spot], at.sine[spot])
    qkv = jnp.concatenate([turned, joined[:, 384:]], axis=1).astype(BF16)
    at.qkv[c] = qkv
    allowed = at.mask[c] > 0.5
    outs = []
    for h in range(4):
        kv = h // 2
        share = shares(head(qkv, 0, h * HD), head(qkv, 0, 256 + kv * HD), allowed)
        outs.append(dot(share.astype(BF16), head(qkv, 0, 384 + kv * HD)))
    attended = jnp.concatenate(outs, axis=1).astype(BF16)
    at.att[c] = attended
    at.part[c] = dot(attended, at.v_wo[...]).astype(BF16)
    yield from chain_tp_scatter(
        at.part, c, at.tp_held, at.tp_send, at.tp_recv, at.tp_sum
    )
    after = x + at.tp_sum[c]
    at.after[c] = after
    at.normed_two[c] = (after * inverse_rms(after) * at.gains[layer, 1:2]).astype(BF16)
    yield from direct_gather(at.normed_two.at[c], at.v_x, c, at.eg_send, at.eg_recv)
    at.saves[c].start()
    if c == 0:
        for key in ("router", "wgu", "wd"):
            loads[key].wait()
    tall = 128
    for tile in range(512 // tall):
        pair = pl.ds(tall // 128 * tile, tall // 128)
        rows = pl.ds(tall * tile, tall)
        xt = at.v_x[c, pair].reshape(tall, D)
        gates = masked_softmax(
            dot(xt, at.v_router[...]), at.routed[c, pair, :, :, :LANES].reshape(tall, LANES).astype(F32)
        )
        total = None
        for e in range(2):
            gate = jnp.sum(gates * at.sel[e : e + 1], axis=1, keepdims=True)
            gu = dot(xt, at.v_wgu[e])
            at.v_gu[c, e, rows] = gu.astype(BF16)
            part, upper = gu[:, :F], gu[:, F:]
            hidden = part * jax.nn.sigmoid(part) * upper
            made = dot((hidden * gate).astype(BF16), at.v_wd[e])
            total = made if total is None else total + made
        at.es_made[c, pair] = total.astype(BF16).reshape(tall // 128, 4, 32, D)
    at.saves[2 + c].start()
    yield from direct_scatter(
        at.es_made, c, at.es_held, at.es_line, at.es_last, at.es_send, at.es_recv, at.y
    )
    at.out[c] = (at.after[c] + at.y[c]).astype(BF16)
    at.saves[c].wait()
    at.saves[2 + c].wait()


def mask_chain(at):
    at_x, at_z = axis_spots()
    spot = at.routed.at[:, at_x, at_z]
    blocks = at.routed.at[:, :, at_z]
    first = [
        remote(at.routed_own, spot, at.mg_send.at[0, n], at.mg_recv.at[0, n], peer)
        for n, peer in enumerate(axis_peers(0))
    ]
    for copy in first:
        copy.start()
    spot[...] = at.routed_own[...]
    yield
    for copy in first:
        copy.wait()
    second = [
        remote(blocks, blocks, at.mg_send.at[1, n], at.mg_recv.at[1, n], peer)
        for n, peer in enumerate(axis_peers(1))
    ]
    for copy in second:
        copy.start()
    yield
    for copy in second:
        copy.wait()


def pair_chain(at, loads):
    me = lax.axis_index("section")
    (peer,) = around("section")
    sends, reads, writes = [], [], []
    pieces = ((at.own_gu, at.held_gu, at.wgu), (at.own_d, at.held_d, at.wd))
    for n, (own, held, both) in enumerate(pieces):
        sends.append(
            remote(own.at[0], both.at[me], at.pair_sems.at[0, n], at.pair_sems.at[1, n], peer)
        )
        reads.append(pltpu.make_async_copy(own.at[0], held, at.pair_sems.at[2, n]))
        writes.append(pltpu.make_async_copy(held, both.at[me], at.pair_sems.at[3, n]))
        sends[-1].start()
        reads[-1].start()
    yield
    for n in range(2):
        reads[n].wait()
        writes[n].start()
    yield
    yield
    for n in range(2):
        writes[n].wait()
        sends[n].wait()
    loads["wgu"].start()
    loads["wd"].start()


def forward_pass(xin, layer, tables, sel, weights, routed_own, routed):
    cosine, sine, mask = tables
    wqkv, wo, gains, router, wgu, wd = weights
    swap = layer == 0
    v, a = in_vmem(), in_any()
    ins = dict(
        xin=(xin, v),
        gains=(gains, v),
        cosine=(cosine, v),
        sine=(sine, v),
        mask=(mask, v),
        sel=(sel, v),
        wqkv=(wqkv, a),
        wo=(wo, a),
        router=(router, a),
    )
    if swap:
        ins.update(routed_own=(routed_own, v), own_gu=(wgu, a), own_d=(wd, a))
    else:
        ins.update(routed=(routed, v), wgu=(wgu, a), wd=(wd, a))
    outs = dict(
        out=((2, 32, D), BF16, v),
        rows=((2, 128, D), BF16, v),
        qkv=((2, 128, 512), BF16, v),
        att=((2, 128, 256), BF16, v),
        after=((2, 32, D), F32, v),
        y=((2, 32, D), F32, v),
        x_all=((2, 4, 4, 32, D), BF16, a),
        gu=((2, 2, 512, 2 * F), BF16, a),
    )
    scratch = dict(
        normed=pltpu.VMEM((2, 32, D), BF16),
        normed_two=pltpu.VMEM((2, 32, D), BF16),
        part=pltpu.VMEM((2, 128, D), BF16),
        v_wqkv=pltpu.VMEM((D, 512), BF16),
        v_wo=pltpu.VMEM((256, D), BF16),
        v_router=pltpu.VMEM((D, LANES), BF16),
        v_wgu=pltpu.VMEM((2, D, 2 * F), BF16),
        v_wd=pltpu.VMEM((2, F, D), BF16),
        v_x=pltpu.VMEM((2, 4, 4, 32, D), BF16),
        v_gu=pltpu.VMEM((2, 2, 512, 2 * F), BF16),
        load_sems=pltpu.SemaphoreType.DMA((5,)),
        save_sems=pltpu.SemaphoreType.DMA((4,)),
        **TP_SCRATCH,
        **EXP_SCRATCH,
    )
    if swap:
        outs.update(
            wgu=((2, 2, D, 2 * F), BF16, a),
            wd=((2, 2, F, D), BF16, a),
            routed=((2, 4, 4, 32, LANES), BF16, v),
        )
        scratch.update(
            held_gu=pltpu.VMEM((2, D, 2 * F), BF16),
            held_d=pltpu.VMEM((2, F, D), BF16),
            pair_sems=pltpu.SemaphoreType.DMA((4, 2)),
            mg_send=pltpu.SemaphoreType.DMA((2, 3)),
            mg_recv=pltpu.SemaphoreType.DMA((2, 3)),
        )

    def chains(at):
        loads = {}
        for n, key in enumerate(("wqkv", "wo", "router", "wgu", "wd")):
            loads[key] = pltpu.make_async_copy(
                getattr(at, key).at[layer], getattr(at, "v_" + key), at.load_sems.at[n]
            )
        at.saves = [
            pltpu.make_async_copy(src.at[c], dst.at[c], at.save_sems.at[2 * n + c])
            for n, (src, dst) in enumerate(((at.v_x, at.x_all), (at.v_gu, at.gu)))
            for c in range(2)
        ]
        for key in ("wqkv", "wo", "router") if swap else loads:
            loads[key].start()
        running = [forward_chain(at, c, layer, loads) for c in range(2)]
        if swap:
            running = [pair_chain(at, loads), mask_chain(at)] + running
        return running

    axes = ["tp_all", "exp_lines"] + (["section"] if swap else [])
    return one_kernel("forward%d" % layer, 10 + layer, axes, ins, outs, scratch, chains)


def rms_back(q, values, gain):
    inverse = inverse_rms(values)
    scaled = q * gain
    back = inverse * scaled - values * inverse**3 * jnp.mean(values * scaled, axis=1, keepdims=True)
    return back, q * values * inverse


def backward_chain(at, c, layer, loads):
    gather = direct_gather(at.grad.at[c], at.v_g, c, at.eg_send, at.eg_recv)
    next(gather)
    after = at.after[c]
    normed_two = (after * inverse_rms(after) * at.gains[layer, 1:2]).astype(BF16)
    if c == 0:
        loads["router"].wait()
    own_gates = masked_softmax(
        dot(normed_two, at.v_router[...]), at.routed_own[c, :, :LANES].astype(F32)
    )
    gf = at.grad[c].astype(F32)
    gc = (-own_gates * jnp.sum(gf * at.y[c], axis=1, keepdims=True)).astype(BF16)
    lane = lax.broadcasted_iota(jnp.int32, (32, LANES), 1)
    at.small_left[c, 0:32] = normed_two
    at.small_right[c, 0:32] = gc
    at.small_right[c, 32:64] = jnp.where(lane == E + 1, 1.0, 0.0).astype(BF16)
    at.small_right[c, 64:96] = jnp.where(lane == E, 1.0, 0.0).astype(BF16)
    yield
    yield from gather
    if c == 0:
        for key in ("x", "gu", "wd", "wgu"):
            loads[key].wait()
    tall = 512
    for tile in range(512 // tall):
        pair = pl.ds(tall // 128 * tile, tall // 128)
        rows = pl.ds(tall * tile, tall)
        both = pl.ds(512 * c + tall * tile, tall)
        xt = at.v_x[c, pair].reshape(tall, D)
        gt = at.v_g[c, pair].reshape(tall, D)
        gates = masked_softmax(
            dot(xt, at.v_router[...]),
            at.routed[c, pair, :, :, :LANES].reshape(tall, LANES).astype(F32),
        )
        gl, total = None, None
        for e in range(2):
            chosen = at.sel[e : e + 1]
            gate = jnp.sum(gates * chosen, axis=1, keepdims=True)
            gh = dot_nt(gt, at.v_wd[e])
            part = at.v_gu[c, e, rows, :F].astype(F32)
            upper = at.v_gu[c, e, rows, F:].astype(F32)
            s = jax.nn.sigmoid(part)
            act = part * s
            hidden = act * upper
            term = (gate * jnp.sum(hidden * gh, axis=1, keepdims=True)) * chosen
            gl = term if gl is None else gl + term
            at.hs[e, both] = (hidden * gate).astype(BF16)
            gh = gh * gate
            at.gj[e, both, :F] = (gh * upper * (s + act * (1.0 - s))).astype(BF16)
            at.gj[e, both, F:] = (gh * act).astype(BF16)
            dx = dot_nt(at.gj[e, both], at.v_wgu[e])
            total = dx if total is None else total + dx
        gl = gl.astype(BF16)
        at.gl[both] = gl
        total = total + dot_nt(gl, at.v_router[...])
        at.es_made[c, pair] = total.astype(BF16).reshape(tall // 128, 4, 32, D)
    yield from direct_scatter(
        at.es_made, c, at.es_held, at.es_line, at.es_last, at.es_send, at.es_recv, at.es_sum
    )
    grad_n = at.es_sum[c] + dot_nt(at.small_right[c, 0:32], at.v_router[...])
    back, term = rms_back(grad_n, at.after[c], at.gains[layer, 1:2])
    at.small_left[c, 32:64] = term.astype(BF16)
    grad_after = at.grad[c].astype(F32) + back
    at.grad_after[c] = grad_after
    at.ga_own[c] = grad_after.astype(BF16)
    yield from chain_tp_gather(at.ga_own.at[c], at.ga, c, at.tg_send, at.tg_recv)
    if c == 0:
        loads["wqkv"].wait()
        loads["wo"].wait()
    gatt = dot_nt(at.ga[c], at.v_wo[...]).astype(BF16)
    qkv = at.qkv[c]
    allowed = at.mask[c] > 0.5
    gqs, gks, gvs = [], [None, None], [None, None]
    for h in range(4):
        kv = h // 2
        q = head(qkv, 0, h * HD)
        k = head(qkv, 0, 256 + kv * HD)
        v = head(qkv, 0, 384 + kv * HD)
        go = head(gatt, 0, h * HD)
        share = shares(q, k, allowed)
        gp = dot_nt(go, v)
        gs = (share * (gp - jnp.sum(share * gp, axis=1, keepdims=True))).astype(BF16)
        gqs.append(dot(gs, k) * SCORE_SCALE)
        gk = dot_tn(gs, q) * SCORE_SCALE
        gv = dot_tn(share.astype(BF16), go)
        gks[kv] = gk if gks[kv] is None else gks[kv] + gk
        gvs[kv] = gv if gvs[kv] is None else gvs[kv] + gv
    joined = jnp.concatenate(gqs + gks + gvs, axis=1)
    spot = slice(c * 128, c * 128 + 128)
    turned = unrope(joined[:, :384], at.cosine[spot], at.sine[spot])
    gqkv = jnp.concatenate([turned, joined[:, 384:]], axis=1).astype(BF16)
    at.gqkv[c] = gqkv
    at.part[c] = dot_nt(gqkv, at.v_wqkv[...]).astype(BF16)
    yield from chain_tp_scatter(
        at.part, c, at.tp_held, at.tp_send, at.tp_recv, at.tp_sum
    )
    back, term = rms_back(at.tp_sum[c], at.xin[c].astype(F32), at.gains[layer, 0:1])
    at.small_left[c, 64:96] = term.astype(BF16)
    grad_in = at.grad_after[c] + back
    at.grad_in[c] = grad_in
    if layer == 1:
        at.grad_low[c] = grad_in.astype(BF16)


def weight_chain(at):
    moves = getattr(at, "moves", [])

    def move(n):
        if moves:
            moves[n].start()

    yield
    yield

    def joint(e, tile):
        columns = pl.ds(256 * tile, 256)
        x = at.v_x[:, :, :, :, columns].reshape(1024, 256)
        at.dgu[e, columns] = dot_tn(x, at.gj[e]).astype(BF16)

    for chunk in range(2):
        for e in range(2):
            for tile in range(2):
                joint(e, 2 * chunk + tile)
        move(chunk)
        yield
    for e in range(2):
        for tile in range(2):
            columns = pl.ds(256 * tile, 256)
            g = at.v_g[...].reshape(1024, D)
            at.dd[e, columns] = dot_tn(at.hs[e, :, columns], g).astype(BF16)
    move(2)
    yield
    x = at.v_x[...].reshape(1024, D)
    at.small[...] = dot_tn(x, at.gl[...])

    def put(first, last, value):
        value = value.astype(BF16).reshape(4, 4, 2, 32, last - first)
        for half in range(2):
            at.wide[half, :, :, :, first:last] = value[:, :, half]

    ga = at.ga[...].reshape(256, D)
    put(512, 768, dot_tn(ga, at.att[...].reshape(256, 256)))
    rows = at.rows[...].reshape(256, D)
    put(0, 512, dot_tn(rows, at.gqkv[...].reshape(256, 512)))
    yield
    left = at.small_left[...].reshape(192, D)
    right = at.small_right[...].reshape(192, LANES)
    put(768, 896, at.small[...] + dot_tn(left, right))
    put(896, 1024, jnp.zeros((D, LANES), F32))
    for copy in moves:
        copy.wait()


def settle_chain(at, n, wide, summed, wait):
    for _ in range(wait):
        yield
    me = lax.axis_index("section")
    (peer,) = around("section")
    swap = remote(
        wide.at[1 - me], at.se_got, at.se_swap.at[0, n], at.se_swap.at[1, n], peer
    )
    swap.start()
    own = pltpu.make_async_copy(wide.at[me], summed.at[0], at.se_swap.at[2, n])
    own.start()
    yield
    own.wait()
    swap.wait_recv()

    @pl.loop(0, 4)
    def _(x):
        summed[0, x] = (summed[0, x].astype(F32) + at.se_got[x].astype(F32)).astype(BF16)

    yield from direct_scatter(
        summed,
        n,
        at.se_held,
        at.se_line,
        at.se_last,
        at.se_send,
        at.se_recv,
        at.se_out,
        slot=0,
    )
    swap.wait_send()
    piece = at.se_piece.at[n]
    piece[...] = at.se_out[n, :, 768:896]
    partners = tp_peers()
    sent = [
        remote(piece, at.sp_held.at[n, k], at.sp_send.at[n, k], at.sp_recv.at[n, k], partner)
        for k, partner in enumerate(partners)
    ]
    for copy in sent:
        copy.start()
    yield
    for copy in sent:
        copy.wait()
    at.se_total[n] = piece[...] + ((at.sp_held[n, 0] + at.sp_held[n, 1]) + at.sp_held[n, 2])
    expert = lax.axis_index("exp")
    whole_small = at.se_small.at[n]
    sent = [
        remote(
            at.se_total.at[n],
            whole_small.at[expert],
            at.sg_send.at[n, k],
            at.sg_recv.at[n, k],
            {"exp": lax.rem(expert + k + 1, 16)},
        )
        for k in range(15)
    ]
    for copy in sent:
        copy.start()
    whole_small[expert] = at.se_total[n]
    yield
    for copy in sent:
        copy.wait()


def swap_chain(at, k, wait, kept, got, write):
    for _ in range(wait):
        yield
    me = lax.axis_index("section")
    (peer,) = around("section")
    for copy in at.late[k:3:2] if k < 2 else []:
        copy.wait()
    swap = remote(kept.at[1 - me], got, at.last_swap.at[0, k], at.last_swap.at[1, k], peer)
    swap.start()
    write(me, kept.at[me])
    yield
    swap.wait_recv()
    write(1 - me, got)
    swap.wait_send()


def rows_swap(at, k, wait, out):
    kept, got = (at.all_out, at.got_out) if k == 0 else (at.all_grad, at.got_grad)

    def write(core, ref):
        out[pl.ds(2 * core, 2)] = ref[...]

    return swap_chain(at, k, wait, kept, got, write)


def expert_swap(at, wait):
    def write(core, ref):
        at.grad_expert[core] = ref[...]

    return swap_chain(at, 2, wait, at.all_done, at.got_done, write)


def attention_swap(at, wait):
    def write(core, ref):
        at.grad_wide[pl.ds(pl.multiple_of(32 * core, 32), 32)] = ref[...]

    return swap_chain(at, 3, wait, at.se_out, at.got_wide, write)


def small_swap(at, wait):
    def write(core, ref):
        at.grad_small[:, pl.ds(pl.multiple_of(32 * core, 32), 32)] = ref[...]

    return swap_chain(at, 4, wait, at.se_small, at.got_small, write)


def expert_ring(at, n, own, out):
    place = lax.axis_index("tp")
    left, right = around("tp")

    def view(k, part):
        columns = pl.multiple_of(lax.rem(place + k, 4) * 256, 256)
        return own.at[pl.ds(256 * part, 256), pl.ds(columns, 256)]

    return RingScatter(
        view,
        lambda side: at.ex_temp.at[n, side],
        lambda side, part: at.ex_block.at[n, side, part],
        lambda side: at.ex_stage.at[n, side],
        left,
        right,
        [at.ex_send.at[n, i] for i in range(6)],
        [at.ex_recv.at[n, i] for i in range(6)],
    )


def add_into(own, got):
    @pl.loop(0, 8)
    def _(i):
        r = pl.ds(pl.multiple_of(i * 64, 64), 64)
        own[r] = (own[r].astype(F32) + got[r].astype(F32)).astype(BF16)


def end_ring(ring, out):
    ring.finish()
    out[:256] = ring.total(0).astype(BF16)
    out[256:] = ring.total(1).astype(BF16)
    ring.drain()


def early_expert_chain(at, n):
    me = lax.axis_index("section")
    (peer,) = around("section")
    source = (at.late_gu, at.late_gu, at.late_d)[n]
    rows = pl.ds((0, 512, 0)[n], 512)
    own = (at.dd.at[0], at.dd.at[1], at.dgu.at[0, pl.ds(512, 512)])[n]
    got = at.gj.at[n // 2, pl.ds(512 * (n % 2), 512)]
    out = at.all_done.at[1, pl.ds(512 * n, 512)]
    sems = at.swap_sems
    swap = remote(source.at[1 - me, rows], got, sems.at[0, n], sems.at[1, n], peer)
    swap.start()
    kept = pltpu.make_async_copy(source.at[me, rows], own, sems.at[2, n])
    kept.start()
    yield
    kept.wait()
    swap.wait()
    add_into(own, got)
    ring = expert_ring(at, n, own, out)
    ring.start()
    yield
    ring.middle()
    yield
    end_ring(ring, out)


def expert_chain(at, n):
    for _ in range(2 + n):
        yield
    me = lax.axis_index("section")
    (peer,) = around("section")
    source = (at.dgu, at.dgu, at.dd)[n]
    rows = pl.ds((0, 512, 0)[n], 512)
    own, got = source.at[me, rows], at.got.at[n]
    out = at.all_done.at[0, pl.ds(512 * n, 512)]
    sems = at.swap_sems
    swap = remote(source.at[1 - me, rows], got, sems.at[3, n], sems.at[4, n], peer)
    swap.start()
    for _ in range(3 - n):
        yield
    swap.wait()
    add_into(own, got)
    yield
    ring = expert_ring(at, n, own, out)
    ring.start()
    yield
    yield
    yield
    ring.middle()
    yield
    yield
    end_ring(ring, out)


def backward_pass(grad, kept, xin, layer, tables, sel, weights, routed_own, routed, late=None):
    cosine, sine, mask = tables
    wqkv, wo, gains, router, wgu, wd = weights
    v, a = in_vmem(), in_any()
    ins = dict(
        grad=(grad, v),
        xin=(xin, v),
        gains=(gains, v),
        cosine=(cosine, v),
        sine=(sine, v),
        mask=(mask, v),
        sel=(sel, v),
        rows=(kept.rows, v),
        qkv=(kept.qkv, v),
        att=(kept.att, v),
        after=(kept.after, v),
        y=(kept.y, v),
        routed=(routed, v),
        routed_own=(routed_own, v),
        x=(kept.x_all, a),
        gu=(kept.gu, a),
        wqkv=(wqkv, a),
        wo=(wo, a),
        router=(router, a),
        wgu=(wgu, a),
        wd=(wd, a),
    )
    last = late is not None
    if last:
        outs = dict(
            section_output=((4, 32, D), BF16, v),
            section_grad=((4, 32, D), F32, v),
            grad_wide=((64, D), F32, v),
            grad_small=((16, 64, LANES), F32, v),
            grad_expert=((2, 1536, 256), BF16, v),
        )
        ins.update(
            late_wide=(late.wide, a),
            late_gu=(late.dgu, a),
            late_d=(late.dd, a),
            late_grad=(late.grad_in, a),
            late_first=(late.first, a),
            late_second=(late.second, a),
        )
    else:
        outs = dict(
            grad_in=((2, 32, D), F32, v),
            grad_low=((2, 32, D), BF16, v),
            wide=((2, 4, 4, 32, D), BF16, v),
            dgu_out=((2, D, 2 * F), BF16, a),
            dd_out=((2, F, D), BF16, a),
        )
    scratch = dict(
        v_x=pltpu.VMEM((2, 4, 4, 32, D), BF16),
        v_g=pltpu.VMEM((2, 4, 4, 32, D), BF16),
        v_gu=pltpu.VMEM((2, 2, 512, 2 * F), BF16),
        v_wqkv=pltpu.VMEM((D, 512), BF16),
        v_wo=pltpu.VMEM((256, D), BF16),
        v_router=pltpu.VMEM((D, LANES), BF16),
        v_wgu=pltpu.VMEM((2, D, 2 * F), BF16),
        v_wd=pltpu.VMEM((2, F, D), BF16),
        load_sems=pltpu.SemaphoreType.DMA((7,)),
        small_left=pltpu.VMEM((2, 96, D), BF16),
        small_right=pltpu.VMEM((2, 96, LANES), BF16),
        small=pltpu.VMEM((D, LANES), F32),
        hs=pltpu.VMEM((2, 1024, F), BF16),
        gj=pltpu.VMEM((2, 1024, 2 * F), BF16),
        gl=pltpu.VMEM((1024, LANES), BF16),
        dgu=pltpu.VMEM((2, D, 2 * F), BF16),
        dd=pltpu.VMEM((2, F, D), BF16),
        es_sum=pltpu.VMEM((2, 32, D), F32),
        grad_after=pltpu.VMEM((2, 32, D), F32),
        ga_own=pltpu.VMEM((2, 32, D), BF16),
        ga=pltpu.VMEM((2, 128, D), BF16),
        gqkv=pltpu.VMEM((2, 128, 512), BF16),
        part=pltpu.VMEM((2, 128, D), BF16),
        **TP_SCRATCH,
        **EXP_SCRATCH,
    )
    if not last:
        scratch.update(move_sems=pltpu.SemaphoreType.DMA((3,)))
    else:
        scratch.update(
            got=pltpu.VMEM((3, 512, D), BF16),
            ex_temp=pltpu.VMEM((3, 2, 256, 256), BF16),
            ex_block=pltpu.VMEM((3, 2, 2, 256, 256), BF16),
            ex_stage=pltpu.VMEM((3, 2, 256, 256), BF16),
            ex_send=pltpu.SemaphoreType.DMA((3, 6)),
            ex_recv=pltpu.SemaphoreType.DMA((3, 6)),
            swap_sems=pltpu.SemaphoreType.DMA((5, 3)),
            all_out=pltpu.VMEM((2, 2, 32, D), BF16),
            got_out=pltpu.VMEM((2, 32, D), BF16),
            all_grad=pltpu.VMEM((2, 2, 32, D), F32),
            got_grad=pltpu.VMEM((2, 32, D), F32),
            all_done=pltpu.VMEM((2, 1536, 256), BF16),
            got_done=pltpu.VMEM((1536, 256), BF16),
            got_wide=pltpu.VMEM((32, D), F32),
            got_small=pltpu.VMEM((16, 32, LANES), F32),
            last_swap=pltpu.SemaphoreType.DMA((2, 5)),
            se_got=pltpu.VMEM((4, 4, 32, D), BF16),
            se_sum=pltpu.VMEM((1, 4, 4, 32, D), BF16),
            se_held=pltpu.VMEM((2, 2, 3, 4, 32, 512), BF16),
            se_line=pltpu.VMEM((2, 2, 4, 32, 512), BF16),
            se_last=pltpu.VMEM((2, 2, 3, 32, 512), BF16),
            se_out=pltpu.VMEM((2, 32, D), F32),
            se_piece=pltpu.VMEM((2, 32, LANES), F32),
            sp_held=pltpu.VMEM((2, 3, 32, LANES), F32),
            se_total=pltpu.VMEM((2, 32, LANES), F32),
            se_small=pltpu.VMEM((2, 16, 32, LANES), F32),
            se_swap=pltpu.SemaphoreType.DMA((3, 2)),
            late_sems=pltpu.SemaphoreType.DMA((3,)),
            se_send=pltpu.SemaphoreType.DMA((2, 2, 2, 3)),
            se_recv=pltpu.SemaphoreType.DMA((2, 2, 2, 3)),
            sp_send=pltpu.SemaphoreType.DMA((2, 3)),
            sp_recv=pltpu.SemaphoreType.DMA((2, 3)),
            sg_send=pltpu.SemaphoreType.DMA((2, 15)),
            sg_recv=pltpu.SemaphoreType.DMA((2, 15)),
        )

    def chains(at):
        loads = {}
        for n, key in enumerate(("router", "x", "gu", "wd", "wgu", "wqkv", "wo")):
            ref = getattr(at, key)
            loads[key] = pltpu.make_async_copy(
                ref if key in ("x", "gu") else ref.at[layer],
                getattr(at, "v_" + key),
                at.load_sems.at[n],
            )
            loads[key].start()
        running = []
        if last:
            at.late = [
                pltpu.make_async_copy(src, dst, at.late_sems.at[n])
                for n, (src, dst) in enumerate(
                    (
                        (at.late_first, at.all_out.at[0]),
                        (at.late_grad, at.all_grad.at[1]),
                        (at.late_second, at.all_out.at[1]),
                    )
                )
            ]
            for copy in at.late:
                copy.start()
            at.grad_in = at.all_grad.at[0]
            at.wide = at.v_g
        else:
            at.moves = [
                pltpu.make_async_copy(src.at[:, rows], dst.at[:, rows], at.move_sems.at[n])
                for n, (src, dst, rows) in enumerate(
                    (
                        (at.dgu, at.dgu_out, pl.ds(0, 512)),
                        (at.dgu, at.dgu_out, pl.ds(512, 512)),
                        (at.dd, at.dd_out, pl.ds(0, 512)),
                    )
                )
            ]
        running += [backward_chain(at, c, layer, loads) for c in range(2)]
        if last:
            running += [early_expert_chain(at, n) for n in range(3)]
        running.append(weight_chain(at))
        if last:
            running += [
                settle_chain(at, 1, at.late_wide, at.se_sum, 2),
                settle_chain(at, 0, at.wide, at.es_made.at[pl.ds(0, 1)], 6),
            ]
            running += [expert_chain(at, n) for n in range(3)]
            running += [
                rows_swap(at, 0, 1, at.section_output),
                rows_swap(at, 1, 6, at.section_grad),
                attention_swap(at, 9),
                small_swap(at, 11),
                expert_swap(at, 11),
            ]
        return running

    axes = ["tp_all", "section", "exp_all" if last else "exp_lines"]
    return one_kernel("backward%d" % layer, 12 + layer, axes, ins, outs, scratch, chains)


def rope_tables(seg_rows):
    length = seg_rows.shape[0]
    before = jnp.sum((seg_rows[None, :] < seg_rows[:, None]).astype(jnp.int32), axis=1)
    places = (jnp.arange(length, dtype=jnp.int32) - before).astype(F32)
    powers = jnp.arange(0, HD, 2, dtype=jnp.int32).astype(F32) / HD
    angles = places[:, None] * (ROPE_BASE ** (-powers))[None, :]
    cosine, sine = jnp.cos(angles), jnp.sin(angles)
    indices = jnp.arange(length, dtype=jnp.int32)
    allowed = (seg_rows[:, None] == seg_rows[None, :]) & (indices[None, :] <= indices[:, None])
    return (
        jnp.concatenate([cosine] * 4, axis=1),
        jnp.concatenate([-sine, sine, -sine, sine], axis=1),
        allowed.astype(F32),
    )


def routed(routes):
    labels = jnp.arange(LANES, dtype=jnp.int32)
    return jnp.sum((routes[:, :, None] == labels[None, None, :]).astype(F32), axis=1)


def per_device(
    activations,
    cotangent,
    segments,
    routes,
    attention_gain,
    query_weight,
    key_weight,
    value_weight,
    output_weight,
    mixture_gain,
    router_weight,
    expert_gate_up,
    expert_down,
):
    section = lax.axis_index("section")
    expert = lax.axis_index("exp")

    def own_batches(array):
        return lax.dynamic_slice_in_dim(array, 2 * section, 2, 0)

    gains_own = jnp.concatenate(
        [attention_gain, mixture_gain, jnp.zeros((6, D), BF16)], axis=0
    ).astype(F32)[None]
    router_own = jnp.pad(router_weight, ((0, 0), (0, 0), (0, LANES - E)))
    part = pair_part(
        [query_weight, key_weight, value_weight, output_weight, gains_own, router_own],
        [(0, 0), (0, 256), (0, 384), (1, 0), (2, 0), (3, 0)],
        [((D, 512), BF16), ((256, D), BF16), ((8, D), F32), ((D, LANES), BF16)],
    )
    (paired,) = fuse([part], 0, "pair")
    weights = tuple(paired) + (expert_gate_up, expert_down)

    cosine, sine, mask = jax.vmap(rope_tables)(own_batches(segments))
    tables = (cosine.reshape(256, LANES), sine.reshape(256, LANES), mask)
    routes_own = own_batches(routes).reshape(64, 8)
    lanes = lax.broadcasted_iota(jnp.int32, (8, LANES), 1)
    sel = (lanes == 2 * expert + lax.broadcasted_iota(jnp.int32, (8, LANES), 0)).astype(F32)
    routed_own = routed(routes_own)
    routed_own = routed_own.astype(BF16).reshape(2, 32, LANES)

    start = own_batches(activations)
    made = forward_pass(start, 0, tables, sel, weights, routed_own, None)
    out_first = made.out
    weights = tuple(paired) + (made.wgu, made.wd)
    routed_all = made.routed[..., :LANES]
    kept = forward_pass(out_first, 1, tables, sel, weights, None, made.routed)
    out_second = kept.out

    shared = (tables, sel, weights, routed_own, made.routed)
    grad = own_batches(cotangent)
    second = backward_pass(grad, kept, out_first, 1, *shared)
    second.first, second.second = out_first, out_second
    second.dgu, second.dd = second.dgu_out, second.dd_out
    last = backward_pass(second.grad_low, made, start, 0, *shared, late=second)
    wide, small = last.grad_wide, last.grad_small.reshape(D, LANES)
    return (
        last.section_output[None],
        last.section_grad[None],
        small[:, E][None],
        wide[None, :, :256],
        wide[None, :, 256:384],
        wide[None, :, 384:512],
        wide[:, 512:768].T[None],
        small[:, E + 1][None],
        small[None, :, :E],
        last.grad_expert[None, :, :D].astype(F32),
        last.grad_expert[None, :, D:].astype(F32),
    )


def solution(mesh):
    placed = (
        P(None, ("exp", "tp"), None),
        P(None, ("exp", "tp"), None),
        P(None, "exp"),
        P(None, ("exp", "tp"), None),
        P("section", None),
        P("section", None, "tp"),
        P("section", None, "tp"),
        P("section", None, "tp"),
        P("section", "tp", None),
        P("section", None),
        P("section", None, None),
        P("section", "exp", None, None),
        P("section", "exp", None, None),
    )
    return jax.shard_map(
        per_device,
        mesh=mesh,
        in_specs=placed,
        out_specs=(
            P("section", None, ("exp", "tp"), None),
            P("section", None, ("exp", "tp"), None),
            P("section", None),
            P("section", "exp", "tp"),
            P("section", "exp", "tp"),
            P("section", "exp", "tp"),
            P("section", "tp", "exp"),
            P("section", None),
            P("section", None, None),
            P("section", "exp", None, "tp"),
            P("section", "exp", None, "tp"),
        ),
        check_vma=False,
    )
```
